32 devices in a mesh: sub: 4 (over z), blk: 2 (over y), rep: 4 (over x, core).
Axes of the slice: x: 2, y: 2, z: 4, core: 2. Of those that a mesh axis runs over, the one named last changes fastest.
Arguments:
- start_vector: float32 [4, 4, 2048], P('rep', 'sub', 'blk'), may hold values from -120 to 120
- blocks: bfloat16 [4, 4, 8, 32, 4096], P('rep', 'sub', 'blk'), may hold values from -0.4 to 2.4
- pattern: int32 [4, 4, 8, 32], P('rep', 'sub'), may hold values from 0 to 31, as said below
- trace_map: int32 [4, 4, 256], P('rep', 'sub', 'blk'), may hold values from 0 to 2047, as said below
- neighbours: int32 [4, 4, 2], P('rep', 'sub'), may hold values from 0 to 3, as said below
- coupling: float32 [4, 4, 2, 256], P('rep', 'sub', None, 'blk'), may hold values from -1 to 1
Outputs:
- basis_second: float32 [4, 4, 2048], P('rep', 'sub', 'blk')
- basis_third: float32 [4, 4, 2048], P('rep', 'sub', 'blk')
- hessenberg: float32 [5], replicated
The draws below stay inside these ranges and needn't reach their ends.
Inputs may be any that keep to these rules, and one draw needn't show every extreme that they name: `pattern`: slot 0 of block row r names r itself; the other slots name any block row of the subdomain. `trace_map`: place t names a cell from (t // 128) * 16 * 64 to (t // 128 + 1) * 16 * 64 - 1; cells may repeat. The 2 neighbours of subdomain s are distinct and each lies one or two subdomains away from s in the same group.
All inputs are finite; a program needn't handle non-finite values.
Results may differ from the reference program's by a relative error of at most 0.0075.
Values may be sent and summed in bfloat16 or wider, within the bound.
No kernel may reach another device: no remote copies, remote signals or barrier semaphores. Data moves between devices by JAX's collectives and lax.ppermute only.
A program may use at most 64 MiB of HBM per device.

```python
import math
import jax
import jax.numpy as jnp
from jax import lax

BS = 64
K = 8
NNB = 2
NB_DEV = 16
TR_DEV = 128
NB = 32
CELLS = 2048
TR = 256
SUBS = 4
GROUPS = 4


def draw_start_vector(key, part):
    key = jax.random.fold_in(key, 11)
    key_base, key_scale = jax.random.split(key, 2)
    shape = (GROUPS, SUBS, CELLS)
    rising = 1.0 + 2.0 * jnp.arange(SUBS, dtype=jnp.float32) / max(SUBS - 1, 1)
    base = jnp.clip(jax.random.normal(key_base, shape, jnp.float32), -4.0, 4.0)
    scales = jnp.exp(jax.random.uniform(key_scale, shape, jnp.float32, 0.0, math.log(10.0)))
    return base * scales * rising[None, :, None]


def diagonal_values(key, level_lo, level_hi, factor_lo, factor_hi):
    key_level, key_factor = jax.random.split(key, 2)
    levels = jax.random.uniform(key_level, (GROUPS, 1, 1, 1, 1, 1), jnp.float32, level_lo, level_hi)
    factors = jax.random.uniform(key_factor, (GROUPS, SUBS, 1, NB, BS, 1), jnp.float32, factor_lo, factor_hi)
    place_rows = jnp.arange(BS, dtype=jnp.int32)[:, None]
    place_cols = jnp.arange(BS, dtype=jnp.int32)[None, :]
    identity = (place_rows == place_cols).astype(jnp.float32)
    slot_first = (jnp.arange(K, dtype=jnp.int32) == 0).astype(jnp.float32)[None, None, :, None, None, None]
    values = levels * factors * identity[None, None, None, None] * slot_first
    return values.reshape((GROUPS, SUBS, K, NB, BS * BS))


def draw_blocks(key, part):
    key = jax.random.fold_in(key, 9)
    key_noise, key_diag = jax.random.split(key, 2)
    shape = (GROUPS, SUBS, K, NB, BS * BS)
    noise = jnp.clip(jax.random.normal(key_noise, shape, jnp.float32), -4.0, 4.0)
    diagonal = diagonal_values(key_diag, 0.8, 1.6, 0.5, 1.35)
    return (noise / math.sqrt(K * BS) + diagonal).astype(jnp.bfloat16)


def draw_pattern(key, part):
    key = jax.random.fold_in(key, 3)
    spread = jax.random.randint(key, (GROUPS, SUBS, K, NB), 0, NB, dtype=jnp.int32)
    own_rows = jnp.arange(NB, dtype=jnp.int32)[None, None, None, :]
    slot_ids = jnp.arange(K, dtype=jnp.int32)[None, None, :, None]
    return jnp.where(slot_ids == 0, own_rows, spread).astype(jnp.int32)


def draw_trace_map(key, part):
    key = jax.random.fold_in(key, 5)
    local_cells = jax.random.randint(key, (GROUPS, SUBS, TR), 0, NB_DEV * BS, dtype=jnp.int32)
    owner = jnp.arange(TR, dtype=jnp.int32) // TR_DEV
    return (owner[None, None, :] * (NB_DEV * BS) + local_cells).astype(jnp.int32)


def draw_neighbours(key, part):
    key = jax.random.fold_in(key, 7)
    offsets = jnp.array([-2, -1, 1, 2], dtype=jnp.int32)
    sub_ids = jnp.arange(SUBS, dtype=jnp.int32)
    targets = jnp.broadcast_to(sub_ids[None, :, None] + offsets[None, None, :], (GROUPS, SUBS, 4))
    valid = (targets >= 0) & (targets < SUBS)
    places = jnp.arange(4, dtype=jnp.int32)
    scores = jax.random.randint(key, (GROUPS, SUBS, 4), 0, 1 << 20, dtype=jnp.int32) * 4 + places
    scores = jnp.where(valid, scores, -1 - places)
    top_scores, top_places = lax.top_k(scores, NNB)
    return jnp.take_along_axis(targets, top_places, axis=2).astype(jnp.int32)


def level_of(key, dims, pieces, smallest, largest):
    level = 1.0
    for position, shards_of in pieces:
        steps = jax.random.uniform(jax.random.fold_in(jax.random.fold_in(key, 6), position), (shards_of,), jnp.float32, smallest / len(pieces), largest / len(pieces))
        level = level * jnp.repeat(jnp.exp(steps), dims[position] // shards_of).reshape((-1,) + (1,) * (len(dims) - 1 - position))
    return level


def setup_inputs(seed: int = 0) -> dict:
    seeds = jax.random.split(jax.random.key(seed), 7)
    return {
        "start_vector": draw_start_vector(jax.random.fold_in(seeds[6], 71), 0),
        "blocks": draw_blocks(jax.random.fold_in(seeds[6], 71), 0),
        "pattern": draw_pattern(jax.random.fold_in(seeds[6], 71), 0),
        "trace_map": draw_trace_map(jax.random.fold_in(seeds[6], 71), 0),
        "neighbours": draw_neighbours(jax.random.fold_in(seeds[6], 71), 0),
        "coupling": jnp.clip(jax.random.uniform(seeds[5], (GROUPS, SUBS, NNB, TR), jnp.float32, -1.0, 1.0) * level_of(seeds[5], (GROUPS, SUBS, NNB, TR), ((0, 4), (1, 4), (3, 2)), -0.4, 0.0), -1.0, 1.0),
    }


epsilon = 1e-06

def block_product(rounded, blocks, pattern):
    flat_blocks = blocks.reshape((GROUPS * SUBS, K, NB, BS * BS))
    flat_pattern = pattern.reshape((GROUPS * SUBS, K, NB))
    flat_rows = rounded.reshape((GROUPS * SUBS, NB, BS))

    def per_subdomain(operand):
        sub_blocks, sub_pattern, sub_rows = operand
        picked = sub_rows[sub_pattern]
        square_blocks = sub_blocks.reshape((K, NB, BS, BS))
        result = jnp.einsum('kbij,kbj->bi', square_blocks.astype(jnp.float32), picked.astype(jnp.float32), precision=lax.Precision.HIGHEST)
        return result.reshape(-1)
    return lax.map(per_subdomain, (flat_blocks, flat_pattern, flat_rows)).reshape((GROUPS, SUBS, CELLS))

def jacobian(vector_in, blocks, pattern, trace_map, neighbours, coupling):
    rounded = vector_in.astype(jnp.bfloat16)
    product = block_product(rounded, blocks, pattern)
    traces = jnp.take_along_axis(rounded, trace_map, axis=2).astype(jnp.float32)
    group_ids = jnp.arange(GROUPS, dtype=jnp.int32)[:, None, None]
    sub_ids = jnp.arange(SUBS, dtype=jnp.int32)[None, :, None]
    from_near = traces[group_ids, neighbours]
    inflow = lax.optimization_barrier(jnp.sum(coupling * from_near, axis=2))
    return product.at[group_ids, sub_ids, trace_map].add(inflow)

def reference(start_vector, blocks, pattern, trace_map, neighbours, coupling):
    cell_total = GROUPS * SUBS * CELLS

    def inner(left, right):
        return jnp.sum(left * right) / cell_total

    def apply_op(vector_in):
        return jacobian(vector_in, blocks, pattern, trace_map, neighbours, coupling)
    square = inner(start_vector, start_vector)
    basis_one = start_vector / jnp.sqrt(square + epsilon)
    image_one = apply_op(basis_one)
    diag_first = inner(basis_one, image_one)
    residue_one = image_one - diag_first * basis_one
    below_first = jnp.sqrt(inner(residue_one, residue_one) + epsilon)
    basis_second = residue_one / below_first
    image_two = apply_op(basis_second)
    upper_second = inner(basis_one, image_two)
    diag_second = inner(basis_second, image_two)
    residue_two = image_two - upper_second * basis_one - diag_second * basis_second
    below_second = jnp.sqrt(inner(residue_two, residue_two) + epsilon)
    basis_third = residue_two / below_second
    hessenberg = jnp.stack([diag_first, below_first, upper_second, diag_second, below_second])
    return (basis_second, basis_third, hessenberg)
```

```python
import functools

import jax
import jax.numpy as jnp
from jax import lax
from jax.experimental import pallas as pl
from jax.experimental.pallas import tpu as pltpu
from jax.sharding import PartitionSpec as P

BS = 64
LANES = 128
SUBL = 8
epsilon = 1e-06


def pieces(value):
    high = value.astype(jnp.bfloat16)
    rest = value - high.astype(jnp.float32)
    middle = rest.astype(jnp.bfloat16)
    low = (rest - middle.astype(jnp.float32)).astype(jnp.bfloat16)
    return high, middle, low


def lane_iota(shape):
    return lax.broadcasted_iota(jnp.int32, shape, len(shape) - 1)


def row_iota(shape):
    return lax.broadcasted_iota(jnp.int32, shape, 0)


def block_product(vector, blocks_ref, pattern_ref, first_slot, fold_ref):
    slots, block_rows, width = blocks_ref.shape
    half = block_rows // 2
    lower = lane_iota(vector.shape) < BS
    turned = pltpu.roll(vector, BS, 1)
    table = jnp.concatenate([jnp.where(lower, vector, turned), jnp.where(lower, turned, vector)], 0)
    table = jnp.concatenate(pieces(table), 0)
    place = row_iota((block_rows, block_rows))
    place = jnp.where(place < half, 2 * place, 2 * (place - half) + 1)
    picked = []
    for k in range(slots):
        names = pattern_ref[pl.ds(first_slot + k, 1), :]
        chosen = (place == names).astype(jnp.float32).astype(jnp.bfloat16)
        chosen = jnp.concatenate([chosen] * 3, 0)
        picked.append(
            lax.dot_general(chosen, table, (((0,), (0,)), ((), ())), preferred_element_type=jnp.float32)
        )
    ones = (row_iota((2 * LANES, LANES)) % LANES) // BS == lane_iota((2 * LANES, LANES)) % 2
    ones = ones.astype(jnp.float32).astype(jnp.bfloat16)
    pair = (lane_iota((block_rows, LANES)) % BS) // 2
    result = jnp.zeros((block_rows, LANES), jnp.float32)
    for c in range(width // LANES):
        total = None
        for k in range(slots):
            term = blocks_ref[k, :, pl.ds(c * LANES, LANES)].astype(jnp.float32) * picked[k]
            total = term if total is None else total + term
        high = total.astype(jnp.bfloat16)
        low = (total - high.astype(jnp.float32)).astype(jnp.bfloat16)
        sums = lax.dot_general(
            jnp.concatenate([high, low], 1), ones, (((1,), (0,)), ((), ())), preferred_element_type=jnp.float32
        )
        result = jnp.where(pair == c, sums, result)
    fold_ref[...] = result
    even = fold_ref[pl.ds(0, half, stride=2), :]
    odd = fold_ref[pl.ds(1, half, stride=2), :]
    return jnp.where(lane_iota((half, LANES)) < BS, even, odd)


def take_trace(rows, places):
    count = rows.shape[0]
    low = jnp.broadcast_to(places % LANES, (count, LANES))
    picked = jnp.take_along_axis(rows, low, axis=1)
    return jnp.sum(jnp.where(row_iota((count, LANES)) == places // LANES, picked, 0.0), axis=0, keepdims=True)


def spread(values, places, count):
    aimed = jnp.where(row_iota((count, LANES)) == places // LANES, values, 0.0)
    high = aimed.astype(jnp.bfloat16).astype(jnp.float32)
    rest = aimed - high
    middle = rest.astype(jnp.bfloat16).astype(jnp.float32)
    stack = jnp.concatenate([high, middle, rest - middle], 0).astype(jnp.bfloat16)
    target = (row_iota((LANES, LANES)) == places % LANES).astype(jnp.float32).astype(jnp.bfloat16)
    landed = lax.dot_general(stack, target, (((1,), (1,)), ((), ())), preferred_element_type=jnp.float32)
    return landed[0:count] + landed[count : 2 * count] + landed[2 * count : 3 * count]


def first_kernel(near_ref, blocks_ref, pattern_ref, map_ref, neighbours_ref, coupling_ref, out_ref, fold_ref):
    rows = out_ref.shape[0]
    parts = lax.axis_size("blk")
    own_rows = rows // parts
    sub, blk = lax.axis_index("sub"), lax.axis_index("blk")
    first_cell = blk * own_rows * LANES
    vector = jnp.concatenate([near_ref[sub * parts + b, 0:own_rows, :] for b in range(parts)], 0)
    out_ref[...] = block_product(vector, blocks_ref, pattern_ref, blk * blocks_ref.shape[0], fold_ref)
    inflow = jnp.zeros((1, LANES), jnp.float32)
    for n in range(coupling_ref.shape[0]):
        source = neighbours_ref[n] * parts + blk
        places = near_ref[source, own_rows : own_rows + 1, :].astype(jnp.int32) - first_cell
        trace = take_trace(near_ref[source, 0:own_rows, :], places)
        inflow = inflow + coupling_ref[n : n + 1, :] * trace
    own = pl.ds(pl.multiple_of(blk * own_rows, SUBL), own_rows)
    out_ref[own, :] = out_ref[own, :] + spread(inflow, map_ref[...] - first_cell, own_rows)


def second_kernel(
    near_ref, image_ref, blocks_ref, pattern_ref, map_ref, neighbours_ref, coupling_ref, out_ref, own_ref, fold_ref
):
    rows = image_ref.shape[1]
    parts = lax.axis_size("blk")
    own_rows = rows // parts
    sub, blk = lax.axis_index("sub"), lax.axis_index("blk")
    first_cell = blk * own_rows * LANES
    own = pl.ds(pl.multiple_of(blk * own_rows, SUBL), own_rows)

    def summed(index, where):
        total = image_ref[index * parts, where, :]
        for b in range(1, parts):
            total = total + image_ref[index * parts + b, where, :]
        return total

    vector = jnp.concatenate([near_ref[sub * parts + b, 0:own_rows, :] for b in range(parts)], 0)
    image = summed(sub, pl.ds(0, rows))
    out_ref[0:rows, :] = block_product(image, blocks_ref, pattern_ref, blk * blocks_ref.shape[0], fold_ref)
    inflow = jnp.zeros((1, LANES), jnp.float32)
    for n in range(coupling_ref.shape[0]):
        source = neighbours_ref[n]
        places = near_ref[source * parts + blk, own_rows : own_rows + 1, :].astype(jnp.int32) - first_cell
        trace = take_trace(summed(source, own), places)
        inflow = inflow + coupling_ref[n : n + 1, :] * trace
    out_ref[own, :] = out_ref[own, :] + spread(inflow, map_ref[...] - first_cell, own_rows)
    second = out_ref[0:rows, :]
    vector_own = near_ref[sub * parts + blk, 0:own_rows, :]
    image_own = summed(sub, own)
    own_ref[...] = image_own

    def down(left, right):
        return jnp.sum(left * right, axis=0, keepdims=True)

    sums = [
        down(vector_own, vector_own),
        down(vector_own, image_own),
        down(image_own, image_own),
        down(vector, second),
        down(image, second),
        jnp.zeros((SUBL - 5, LANES), jnp.float32),
    ]
    out_ref[rows : rows + SUBL, :] = jnp.concatenate(sums, 0)


def last_kernel(cells, start_ref, own_ref, all_ref, second_ref, third_ref, entries_ref):
    devices, height, _ = all_ref.shape
    rows = height - SUBL
    parts = lax.axis_size("blk")
    subs = lax.axis_size("sub")
    own_rows = rows // parts
    rep, sub, blk = lax.axis_index("rep"), lax.axis_index("sub"), lax.axis_index("blk")
    own = pl.ds(pl.multiple_of(blk * own_rows, SUBL), own_rows)

    sums = jnp.zeros((SUBL, LANES), jnp.float32)
    square = jnp.zeros((rows, LANES), jnp.float32)
    for pair in range(devices // parts):
        total = None
        for b in range(parts):
            sums = sums + all_ref[pair * parts + b, rows:height, :]
            term = all_ref[pair * parts + b, 0:rows, :]
            total = term if total is None else total + term
        square = square + total * total
    square = jnp.sum(square, axis=0, keepdims=True)

    def whole(line):
        return jnp.broadcast_to(jnp.sum(line, axis=1, keepdims=True), (1, LANES)) / cells

    vv, vw, ww, vy, wy = (whole(sums[i : i + 1, :]) for i in range(5))
    yy = whole(square)
    norm_square = vv + epsilon
    h11 = vw / norm_square
    first_square = jnp.maximum(ww - 2.0 * h11 * vw + h11 * h11 * vv, 0.0) / norm_square
    h21 = jnp.sqrt(first_square + epsilon)
    scale = 1.0 / (jnp.sqrt(norm_square) * h21)
    h12 = (vy - h11 * vw) / (norm_square * h21)
    h22 = (wy - h11 * (ww + vy - h11 * vw)) * scale * scale
    near = h11 + h22
    far = h12 * h21 - h11 * h22
    second_square = yy + near * near * ww + far * far * vv + 2.0 * (near * far * vw - near * wy - far * vy)
    h32 = jnp.sqrt(jnp.maximum(second_square, 0.0) * scale * scale + epsilon)

    vector = start_ref[...]
    image = own_ref[...]
    base = (rep * subs + sub) * parts
    again = all_ref[base, own, :]
    for b in range(1, parts):
        again = again + all_ref[base + b, own, :]
    second_ref[...] = (image - h11 * vector) * scale
    third_ref[...] = (again - near * image - far * vector) * (scale / h32)
    lane = lane_iota((1, LANES))
    entries = h32
    for i, value in enumerate((h11, h21, h12, h22)):
        entries = jnp.where(lane == i, value, entries)
    entries_ref[...] = entries[:, 0:5]


def per_device(start_vector, blocks, pattern, trace_map, neighbours, coupling):
    own_cells = start_vector.shape[2]
    own_rows = own_cells // LANES
    parts = lax.axis_size("blk")
    rows = own_rows * parts
    cells = own_cells * parts * lax.axis_size("sub") * lax.axis_size("rep")
    start = start_vector.reshape(own_rows, LANES)
    local_map = trace_map[0]
    blocks, pattern, neighbours, coupling = blocks[0, 0], pattern[0, 0], neighbours[0, 0], coupling[0, 0]
    vmem = pl.BlockSpec(memory_space=pltpu.VMEM)
    smem = pl.BlockSpec(memory_space=pltpu.SMEM)
    fold = pltpu.VMEM((blocks.shape[1], LANES), jnp.float32)
    params = pltpu.CompilerParams(vmem_limit_bytes=40 * 1024 * 1024)

    near = lax.all_gather(jnp.concatenate([start, local_map.astype(jnp.float32)], 0), ("sub", "blk"))
    partial = pl.pallas_call(
        first_kernel,
        out_shape=jax.ShapeDtypeStruct((rows, LANES), jnp.float32),
        in_specs=[vmem, vmem, vmem, vmem, smem, vmem],
        out_specs=vmem,
        scratch_shapes=[fold],
        compiler_params=params,
        name="first_image",
    )(near, blocks, pattern, local_map, neighbours, coupling)
    images = lax.all_gather(partial, ("sub", "blk"))
    partial, image = pl.pallas_call(
        second_kernel,
        out_shape=(
            jax.ShapeDtypeStruct((rows + SUBL, LANES), jnp.float32),
            jax.ShapeDtypeStruct((own_rows, LANES), jnp.float32),
        ),
        in_specs=[vmem, vmem, vmem, vmem, vmem, smem, vmem],
        out_specs=(vmem, vmem),
        scratch_shapes=[fold],
        compiler_params=params,
        name="second_image",
    )(near, images, blocks, pattern, local_map, neighbours, coupling)
    everything = lax.all_gather(partial, ("rep", "sub", "blk"))
    second, third, entries = pl.pallas_call(
        functools.partial(last_kernel, float(cells)),
        out_shape=(
            jax.ShapeDtypeStruct((own_rows, LANES), jnp.float32),
            jax.ShapeDtypeStruct((own_rows, LANES), jnp.float32),
            jax.ShapeDtypeStruct((1, 5), jnp.float32),
        ),
        in_specs=[vmem, vmem, vmem],
        out_specs=(vmem, vmem, vmem),
        compiler_params=params,
        name="arnoldi_entries",
    )(start, image, everything)
    return second.reshape(start_vector.shape), third.reshape(start_vector.shape), entries.reshape(5)


def solution(mesh):
    return jax.shard_map(
        per_device,
        mesh=mesh,
        in_specs=(
            P("rep", "sub", "blk"),
            P("rep", "sub", "blk", None, None),
            P("rep", "sub", None, None),
            P("rep", "sub", "blk"),
            P("rep", "sub", None),
            P("rep", "sub", None, "blk"),
        ),
        out_specs=(P("rep", "sub", "blk"), P("rep", "sub", "blk"), P()),
        check_vma=False,
    )
```

```python
import functools

import jax
import jax.numpy as jnp
from jax import lax
from jax.experimental import pallas as pl
from jax.experimental.pallas import tpu as pltpu
from jax.sharding import PartitionSpec as P

BS = 64
LANES = 128
SUBL = 8
epsilon = 1e-06


def pieces(value):
    high = value.astype(jnp.bfloat16)
    rest = value - high.astype(jnp.float32)
    middle = rest.astype(jnp.bfloat16)
    low = (rest - middle.astype(jnp.float32)).astype(jnp.bfloat16)
    return high, middle, low


def lane_iota(shape):
    return lax.broadcasted_iota(jnp.int32, shape, len(shape) - 1)


def row_iota(shape):
    return lax.broadcasted_iota(jnp.int32, shape, 0)


def block_product(vector, blocks_ref, pattern_ref, first_slot, fold_ref):
    slots, block_rows, width = blocks_ref.shape
    half = block_rows // 2
    lower = lane_iota(vector.shape) < BS
    turned = pltpu.roll(vector, BS, 1)
    table = jnp.concatenate([jnp.where(lower, vector, turned), jnp.where(lower, turned, vector)], 0)
    table = jnp.concatenate(pieces(table), 0)
    place = row_iota((block_rows, block_rows))
    place = jnp.where(place < half, 2 * place, 2 * (place - half) + 1)
    picked = []
    for k in range(slots):
        names = pattern_ref[pl.ds(first_slot + k, 1), :]
        chosen = (place == names).astype(jnp.float32).astype(jnp.bfloat16)
        chosen = jnp.concatenate([chosen] * 3, 0)
        picked.append(
            lax.dot_general(chosen, table, (((0,), (0,)), ((), ())), preferred_element_type=jnp.float32)
        )
    ones = (row_iota((2 * LANES, LANES)) % LANES) // BS == lane_iota((2 * LANES, LANES)) % 2
    ones = ones.astype(jnp.float32).astype(jnp.bfloat16)
    pair = (lane_iota((block_rows, LANES)) % BS) // 2
    result = jnp.zeros((block_rows, LANES), jnp.float32)
    for c in range(width // LANES):
        total = None
        for k in range(slots):
            term = blocks_ref[k, :, pl.ds(c * LANES, LANES)].astype(jnp.float32) * picked[k]
            total = term if total is None else total + term
        high = total.astype(jnp.bfloat16)
        low = (total - high.astype(jnp.float32)).astype(jnp.bfloat16)
        sums = lax.dot_general(
            jnp.concatenate([high, low], 1), ones, (((1,), (0,)), ((), ())), preferred_element_type=jnp.float32
        )
        result = jnp.where(pair == c, sums, result)
    fold_ref[...] = result
    even = fold_ref[pl.ds(0, half, stride=2), :]
    odd = fold_ref[pl.ds(1, half, stride=2), :]
    return jnp.where(lane_iota((half, LANES)) < BS, even, odd)


def take_trace(rows, places):
    count = rows.shape[0]
    low = jnp.broadcast_to(places % LANES, (count, LANES))
    picked = jnp.take_along_axis(rows, low, axis=1)
    return jnp.sum(jnp.where(row_iota((count, LANES)) == places // LANES, picked, 0.0), axis=0, keepdims=True)


def spread(values, places, count):
    aimed = jnp.where(row_iota((count, LANES)) == places // LANES, values, 0.0)
    high = aimed.astype(jnp.bfloat16).astype(jnp.float32)
    rest = aimed - high
    middle = rest.astype(jnp.bfloat16).astype(jnp.float32)
    stack = jnp.concatenate([high, middle, rest - middle], 0).astype(jnp.bfloat16)
    target = (row_iota((LANES, LANES)) == places % LANES).astype(jnp.float32).astype(jnp.bfloat16)
    landed = lax.dot_general(stack, target, (((1,), (1,)), ((), ())), preferred_element_type=jnp.float32)
    return landed[0:count] + landed[count : 2 * count] + landed[2 * count : 3 * count]


def first_kernel(near_ref, blocks_ref, pattern_ref, map_ref, neighbours_ref, coupling_ref, out_ref, fold_ref, sum_ref):
    rows = sum_ref.shape[0]
    parts = lax.axis_size("blk")
    own_rows = rows // parts
    sub, blk = lax.axis_index("sub"), lax.axis_index("blk")
    first_cell = blk * own_rows * LANES
    vector = jnp.concatenate([near_ref[sub * parts + b, 0:own_rows, :] for b in range(parts)], 0)
    sum_ref[...] = block_product(vector, blocks_ref, pattern_ref, blk * blocks_ref.shape[0], fold_ref)
    inflow = jnp.zeros((1, LANES), jnp.float32)
    for n in range(coupling_ref.shape[0]):
        source = neighbours_ref[n] * parts + blk
        places = near_ref[source, own_rows : own_rows + 1, :].astype(jnp.int32) - first_cell
        trace = take_trace(near_ref[source, 0:own_rows, :], places)
        inflow = inflow + coupling_ref[n : n + 1, :] * trace
    own = pl.ds(pl.multiple_of(blk * own_rows, SUBL), own_rows)
    sum_ref[own, :] = sum_ref[own, :] + spread(inflow, map_ref[...] - first_cell, own_rows)
    partial = sum_ref[...]
    for device in range(out_ref.shape[0]):
        out_ref[device] = partial


def second_kernel(
    near_ref, image_ref, blocks_ref, pattern_ref, map_ref, neighbours_ref, coupling_ref, out_ref, own_ref, fold_ref
):
    rows = image_ref.shape[1]
    parts = lax.axis_size("blk")
    own_rows = rows // parts
    sub, blk = lax.axis_index("sub"), lax.axis_index("blk")
    first_cell = blk * own_rows * LANES
    own = pl.ds(pl.multiple_of(blk * own_rows, SUBL), own_rows)

    def summed(index, where):
        total = image_ref[index * parts, where, :]
        for b in range(1, parts):
            total = total + image_ref[index * parts + b, where, :]
        return total

    vector = jnp.concatenate([near_ref[sub * parts + b, 0:own_rows, :] for b in range(parts)], 0)
    image = summed(sub, pl.ds(0, rows))
    out_ref[0:rows, :] = block_product(image, blocks_ref, pattern_ref, blk * blocks_ref.shape[0], fold_ref)
    inflow = jnp.zeros((1, LANES), jnp.float32)
    for n in range(coupling_ref.shape[0]):
        source = neighbours_ref[n]
        places = near_ref[source * parts + blk, own_rows : own_rows + 1, :].astype(jnp.int32) - first_cell
        trace = take_trace(summed(source, own), places)
        inflow = inflow + coupling_ref[n : n + 1, :] * trace
    out_ref[own, :] = out_ref[own, :] + spread(inflow, map_ref[...] - first_cell, own_rows)
    second = out_ref[0:rows, :]
    vector_own = near_ref[sub * parts + blk, 0:own_rows, :]
    image_own = summed(sub, own)
    own_ref[...] = image_own

    def down(left, right):
        return jnp.sum(left * right, axis=0, keepdims=True)

    sums = [
        down(vector_own, vector_own),
        down(vector_own, image_own),
        down(image_own, image_own),
        down(vector, second),
        down(image, second),
        jnp.zeros((SUBL - 5, LANES), jnp.float32),
    ]
    out_ref[rows : rows + SUBL, :] = jnp.concatenate(sums, 0)


def pair_kernel(pair_ref, out_ref, own_ref):
    parts, height, _ = pair_ref.shape
    rows = height - SUBL
    own_rows = rows // parts
    total = pair_ref[0]
    for b in range(1, parts):
        total = total + pair_ref[b]
    square = jnp.sum(total[0:rows] * total[0:rows], axis=0, keepdims=True)
    sums = jnp.where(row_iota((SUBL, LANES)) == 5, square, total[rows:height])
    for device in range(out_ref.shape[0]):
        out_ref[device] = sums
    own = pl.ds(pl.multiple_of(lax.axis_index("blk") * own_rows, SUBL), own_rows)
    again = pair_ref[0, own, :]
    for b in range(1, parts):
        again = again + pair_ref[b, own, :]
    own_ref[...] = again


def last_kernel(cells, start_ref, own_ref, again_ref, sums_ref, second_ref, third_ref, entries_ref):
    sums = jnp.sum(sums_ref[...], axis=0)

    def whole(i):
        return jnp.broadcast_to(jnp.sum(sums[i : i + 1, :], axis=1, keepdims=True), (1, LANES)) / cells

    vv, vw, ww, vy, wy, yy = (whole(i) for i in range(6))
    norm_square = vv + epsilon
    h11 = vw / norm_square
    first_square = jnp.maximum(ww - 2.0 * h11 * vw + h11 * h11 * vv, 0.0) / norm_square
    h21 = jnp.sqrt(first_square + epsilon)
    scale = 1.0 / (jnp.sqrt(norm_square) * h21)
    h12 = (vy - h11 * vw) / (norm_square * h21)
    h22 = (wy - h11 * (ww + vy - h11 * vw)) * scale * scale
    near = h11 + h22
    far = h12 * h21 - h11 * h22
    second_square = yy + near * near * ww + far * far * vv + 2.0 * (near * far * vw - near * wy - far * vy)
    h32 = jnp.sqrt(jnp.maximum(second_square, 0.0) * scale * scale + epsilon)

    vector, image = start_ref[...], own_ref[...]
    second_ref[...] = (image - h11 * vector) * scale
    third_ref[...] = (again_ref[...] - near * image - far * vector) * (scale / h32)
    lane = lane_iota((1, LANES))
    entries = h32
    for i, value in enumerate((h11, h21, h12, h22)):
        entries = jnp.where(lane == i, value, entries)
    entries_ref[...] = entries[:, 0:5]


def per_device(start_vector, blocks, pattern, trace_map, neighbours, coupling):
    own_cells = start_vector.shape[2]
    own_rows = own_cells // LANES
    parts, subs, reps = lax.axis_size("blk"), lax.axis_size("sub"), lax.axis_size("rep")
    rows = own_rows * parts
    cells = own_cells * parts * subs * reps
    start = start_vector.reshape(own_rows, LANES)
    local_map = trace_map[0]
    blocks, pattern, neighbours, coupling = blocks[0, 0], pattern[0, 0], neighbours[0, 0], coupling[0, 0]
    vmem = pl.BlockSpec(memory_space=pltpu.VMEM)
    smem = pl.BlockSpec(memory_space=pltpu.SMEM)
    params = pltpu.CompilerParams(vmem_limit_bytes=40 * 1024 * 1024)

    def rowed(*shape):
        return jax.ShapeDtypeStruct((*shape, LANES), jnp.float32)

    payload = jnp.concatenate([start, local_map.astype(jnp.float32)], 0)
    payload = jnp.pad(payload, ((0, SUBL - 1), (0, 0)))
    payload = jnp.broadcast_to(payload, (subs * parts, *payload.shape))
    near = lax.all_to_all(payload, ("sub", "blk"), 0, 0, tiled=True)
    fold = pltpu.VMEM((blocks.shape[1], LANES), jnp.float32)
    partial = pl.pallas_call(
        first_kernel,
        out_shape=rowed(subs * parts, rows),
        in_specs=[vmem, vmem, vmem, vmem, smem, vmem],
        out_specs=vmem,
        scratch_shapes=[fold, pltpu.VMEM((rows, LANES), jnp.float32)],
        compiler_params=params,
        name="first_image",
    )(near, blocks, pattern, local_map, neighbours, coupling)
    images = lax.all_to_all(partial, ("sub", "blk"), 0, 0, tiled=True)
    partial, image = pl.pallas_call(
        second_kernel,
        out_shape=(rowed(rows + SUBL), rowed(own_rows)),
        in_specs=[vmem, vmem, vmem, vmem, vmem, smem, vmem],
        out_specs=(vmem, vmem),
        scratch_shapes=[fold],
        compiler_params=params,
        name="second_image",
    )(near, images, blocks, pattern, local_map, neighbours, coupling)
    pair = lax.all_gather(partial, "blk")
    sums, again = pl.pallas_call(
        pair_kernel,
        out_shape=(rowed(reps * subs, SUBL), rowed(own_rows)),
        in_specs=[vmem],
        out_specs=(vmem, vmem),
        compiler_params=params,
        name="pair_sums",
    )(pair)
    sums = lax.all_to_all(sums, ("rep", "sub"), 0, 0, tiled=True)
    second, third, entries = pl.pallas_call(
        functools.partial(last_kernel, float(cells)),
        out_shape=(rowed(own_rows), rowed(own_rows), jax.ShapeDtypeStruct((1, 5), jnp.float32)),
        in_specs=[vmem] * 4,
        out_specs=(vmem, vmem, vmem),
        compiler_params=params,
        name="arnoldi_entries",
    )(start, image, again, sums)
    return second.reshape(start_vector.shape), third.reshape(start_vector.shape), entries.reshape(5)


def solution(mesh):
    return jax.shard_map(
        per_device,
        mesh=mesh,
        in_specs=(
            P("rep", "sub", "blk"),
            P("rep", "sub", "blk", None, None),
            P("rep", "sub", None, None),
            P("rep", "sub", "blk"),
            P("rep", "sub", None),
            P("rep", "sub", None, "blk"),
        ),
        out_specs=(P("rep", "sub", "blk"), P("rep", "sub", "blk"), P()),
        check_vma=False,
    )
```

```python
import functools

import jax
import jax.numpy as jnp
from jax import lax
from jax.experimental import pallas as pl
from jax.experimental.pallas import tpu as pltpu
from jax.sharding import PartitionSpec as P

BS = 64
LANES = 128
SUBL = 8
epsilon = 1e-06


def pieces(value):
    high = value.astype(jnp.bfloat16)
    rest = value - high.astype(jnp.float32)
    middle = rest.astype(jnp.bfloat16)
    low = (rest - middle.astype(jnp.float32)).astype(jnp.bfloat16)
    return high, middle, low


def lane_iota(shape):
    return lax.broadcasted_iota(jnp.int32, shape, len(shape) - 1)


def row_iota(shape):
    return lax.broadcasted_iota(jnp.int32, shape, 0)


def start_blocks(blocks_ref, held_ref, sems):
    count = sems.shape[0]
    step = blocks_ref.shape[2] // count
    copies = []
    for i in range(count):
        part = pl.ds(i * step, step)
        copies.append(pltpu.make_async_copy(blocks_ref.at[:, :, part], held_ref.at[:, :, part], sems.at[i]))
        copies[-1].start()
    return copies


def block_product(vector, held_ref, copies, pattern_ref, first_slot, fold_ref):
    slots, block_rows, width = held_ref.shape
    half = block_rows // 2
    lower = lane_iota(vector.shape) < BS
    turned = pltpu.roll(vector, BS, 1)
    table = jnp.concatenate([jnp.where(lower, vector, turned), jnp.where(lower, turned, vector)], 0)
    table = jnp.concatenate(pieces(table), 0)
    place = row_iota((block_rows, block_rows))
    place = jnp.where(place < half, 2 * place, 2 * (place - half) + 1)
    picked = []
    for k in range(slots):
        names = pattern_ref[pl.ds(first_slot + k, 1), :]
        chosen = (place == names).astype(jnp.float32).astype(jnp.bfloat16)
        chosen = jnp.concatenate([chosen] * 3, 0)
        picked.append(
            lax.dot_general(chosen, table, (((0,), (0,)), ((), ())), preferred_element_type=jnp.float32)
        )
    ones = (row_iota((2 * LANES, LANES)) % LANES) // BS == lane_iota((2 * LANES, LANES)) % 2
    ones = ones.astype(jnp.float32).astype(jnp.bfloat16)
    pair = (lane_iota((block_rows, LANES)) % BS) // 2
    result = jnp.zeros((block_rows, LANES), jnp.float32)
    pieces_each = width // LANES // len(copies)
    for c in range(width // LANES):
        if c % pieces_each == 0:
            copies[c // pieces_each].wait()
        total = None
        for k in range(slots):
            term = held_ref[k, :, pl.ds(c * LANES, LANES)].astype(jnp.float32) * picked[k]
            total = term if total is None else total + term
        high = total.astype(jnp.bfloat16)
        low = (total - high.astype(jnp.float32)).astype(jnp.bfloat16)
        sums = lax.dot_general(
            jnp.concatenate([high, low], 1), ones, (((1,), (0,)), ((), ())), preferred_element_type=jnp.float32
        )
        result = jnp.where(pair == c, sums, result)
    fold_ref[...] = result
    even = fold_ref[pl.ds(0, half, stride=2), :]
    odd = fold_ref[pl.ds(1, half, stride=2), :]
    return jnp.where(lane_iota((half, LANES)) < BS, even, odd)


def take_trace(rows, places):
    count = rows.shape[0]
    low = jnp.broadcast_to(places % LANES, (count, LANES))
    picked = jnp.take_along_axis(rows, low, axis=1)
    return jnp.sum(jnp.where(row_iota((count, LANES)) == places // LANES, picked, 0.0), axis=0, keepdims=True)


def spread(values, places, count):
    aimed = jnp.where(row_iota((count, LANES)) == places // LANES, values, 0.0)
    high = aimed.astype(jnp.bfloat16).astype(jnp.float32)
    rest = aimed - high
    middle = rest.astype(jnp.bfloat16).astype(jnp.float32)
    stack = jnp.concatenate([high, middle, rest - middle], 0).astype(jnp.bfloat16)
    target = (row_iota((LANES, LANES)) == places % LANES).astype(jnp.float32).astype(jnp.bfloat16)
    landed = lax.dot_general(stack, target, (((1,), (1,)), ((), ())), preferred_element_type=jnp.float32)
    return landed[0:count] + landed[count : 2 * count] + landed[2 * count : 3 * count]


def first_kernel(
    pair_ref, blocks_ref, pattern_ref, map_ref, neighbours_ref, coupling_ref, out_ref, held_ref, sems, fold_ref
):
    copies = start_blocks(blocks_ref, held_ref, sems)
    parts, own_rows, _ = pair_ref.shape
    rows = parts * own_rows
    blk = lax.axis_index("blk")
    places = map_ref[...]
    count = coupling_ref.shape[0]
    lines = [take_trace(pair_ref[blk], places - blk * own_rows * LANES), places.astype(jnp.float32)]
    lines += [coupling_ref[n : n + 1, :] for n in range(count)]
    lines += [jnp.full((1, LANES), neighbours_ref[n], jnp.int32).astype(jnp.float32) for n in range(count)]
    lines += [jnp.zeros((out_ref.shape[1] - rows - len(lines), LANES), jnp.float32)]
    lines = jnp.concatenate(lines, 0)
    vector = jnp.concatenate([pair_ref[b] for b in range(parts)], 0)
    partial = block_product(vector, held_ref, copies, pattern_ref, blk * held_ref.shape[0], fold_ref)
    for device in range(out_ref.shape[0]):
        out_ref[device, 0:rows, :] = partial
        out_ref[device, rows : rows + SUBL, :] = lines


def second_kernel(
    pair_ref,
    group_ref,
    blocks_ref,
    pattern_ref,
    map_ref,
    neighbours_ref,
    coupling_ref,
    out_ref,
    own_ref,
    held_ref,
    sems,
    fold_ref,
    image_ref,
):
    copies = start_blocks(blocks_ref, held_ref, sems)
    parts, own_rows, _ = pair_ref.shape
    rows = parts * own_rows
    count = coupling_ref.shape[0]
    subs = lax.axis_size("sub")
    sub, blk = lax.axis_index("sub"), lax.axis_index("blk")
    own = pl.ds(pl.multiple_of(blk * own_rows, SUBL), own_rows)

    def line(sub_at, part, i):
        return group_ref[sub_at * parts + part, rows + i : rows + i + 1, :]

    def landed(sub_at, part):
        traces = jnp.concatenate([line(other, part, 0) for other in range(subs)], 0)
        names = row_iota(traces.shape).astype(jnp.float32)
        inflow = jnp.zeros((1, LANES), jnp.float32)
        for n in range(count):
            chosen = jnp.where(names == line(sub_at, part, 2 + count + n), traces, 0.0)
            inflow = inflow + line(sub_at, part, 2 + n) * jnp.sum(chosen, axis=0, keepdims=True)
        places = line(sub_at, part, 1).astype(jnp.int32) - part * own_rows * LANES
        return spread(inflow, places, own_rows), places

    def summed(index, where):
        total = group_ref[index * parts, where, :]
        for b in range(1, parts):
            total = total + group_ref[index * parts + b, where, :]
        return total

    added = jnp.concatenate([landed(sub, b)[0] for b in range(parts)], 0)
    image = summed(sub, pl.ds(0, rows)) + added
    image_ref[...] = image
    second = block_product(image, held_ref, copies, pattern_ref, blk * held_ref.shape[0], fold_ref)
    inflow = jnp.zeros((1, LANES), jnp.float32)
    for n in range(count):
        source = neighbours_ref[n]
        added, places = landed(source, blk)
        inflow = inflow + coupling_ref[n : n + 1, :] * take_trace(summed(source, own) + added, places)
    out_ref[0:rows, :] = second
    out_ref[own, :] = out_ref[own, :] + spread(inflow, map_ref[...] - blk * own_rows * LANES, own_rows)
    second = out_ref[0:rows, :]
    vector = jnp.concatenate([pair_ref[b] for b in range(parts)], 0)
    vector_own, image_own = pair_ref[blk], image_ref[own, :]
    own_ref[...] = image_own

    def down(left, right):
        return jnp.sum(left * right, axis=0, keepdims=True)

    sums = [
        down(vector_own, vector_own),
        down(vector_own, image_own),
        down(image_own, image_own),
        down(vector, second),
        down(image, second),
        jnp.zeros((SUBL - 5, LANES), jnp.float32),
    ]
    out_ref[rows : rows + SUBL, :] = jnp.concatenate(sums, 0)


def pair_kernel(pair_ref, out_ref, own_ref):
    parts, height, _ = pair_ref.shape
    rows = height - SUBL
    own_rows = rows // parts
    total = pair_ref[0]
    for b in range(1, parts):
        total = total + pair_ref[b]
    square = jnp.sum(total[0:rows] * total[0:rows], axis=0, keepdims=True)
    sums = jnp.where(row_iota((SUBL, LANES)) == 5, square, total[rows:height])
    sums = jnp.sum(sums, axis=1, keepdims=True)
    sums = jnp.where(row_iota((SUBL, LANES)) == lane_iota((SUBL, LANES)), sums, 0.0)
    sums = jnp.sum(sums, axis=0, keepdims=True)
    for device in range(out_ref.shape[0]):
        out_ref[device] = sums
    own = pl.ds(pl.multiple_of(lax.axis_index("blk") * own_rows, SUBL), own_rows)
    again = pair_ref[0, own, :]
    for b in range(1, parts):
        again = again + pair_ref[b, own, :]
    own_ref[...] = again


def last_kernel(cells, start_ref, own_ref, again_ref, sums_ref, second_ref, third_ref, entries_ref):
    sums = jnp.sum(sums_ref[...], axis=0) / cells

    def whole(i):
        return jnp.broadcast_to(sums[:, i : i + 1], (1, LANES))

    vv, vw, ww, vy, wy, yy = (whole(i) for i in range(6))
    norm_square = vv + epsilon
    h11 = vw / norm_square
    first_square = jnp.maximum(ww - 2.0 * h11 * vw + h11 * h11 * vv, 0.0) / norm_square
    h21 = jnp.sqrt(first_square + epsilon)
    scale = 1.0 / (jnp.sqrt(norm_square) * h21)
    h12 = (vy - h11 * vw) / (norm_square * h21)
    h22 = (wy - h11 * (ww + vy - h11 * vw)) * scale * scale
    near = h11 + h22
    far = h12 * h21 - h11 * h22
    second_square = yy + near * near * ww + far * far * vv + 2.0 * (near * far * vw - near * wy - far * vy)
    h32 = jnp.sqrt(jnp.maximum(second_square, 0.0) * scale * scale + epsilon)

    vector, image = start_ref[...], own_ref[...]
    second_ref[...] = (image - h11 * vector) * scale
    third_ref[...] = (again_ref[...] - near * image - far * vector) * (scale / h32)
    lane = lane_iota((1, LANES))
    entries = h32
    for i, value in enumerate((h11, h21, h12, h22)):
        entries = jnp.where(lane == i, value, entries)
    entries_ref[...] = entries[:, 0:5]


def per_device(start_vector, blocks, pattern, trace_map, neighbours, coupling):
    own_cells = start_vector.shape[2]
    own_rows = own_cells // LANES
    parts, subs, reps = lax.axis_size("blk"), lax.axis_size("sub"), lax.axis_size("rep")
    rows = own_rows * parts
    cells = own_cells * parts * subs * reps
    start = start_vector.reshape(own_rows, LANES)
    local_map = trace_map[0]
    blocks, pattern, neighbours, coupling = blocks[0, 0], pattern[0, 0], neighbours[0, 0], coupling[0, 0]
    vmem = pl.BlockSpec(memory_space=pltpu.VMEM)
    smem = pl.BlockSpec(memory_space=pltpu.SMEM)
    params = pltpu.CompilerParams(vmem_limit_bytes=40 * 1024 * 1024)

    def rowed(*shape):
        return jax.ShapeDtypeStruct((*shape, LANES), jnp.float32)

    pair = lax.all_gather(start, "blk")
    chunks = 8
    fold = pltpu.VMEM((blocks.shape[1], LANES), jnp.float32)
    held = [pltpu.VMEM(blocks.shape, jnp.bfloat16), pltpu.SemaphoreType.DMA((chunks,))]
    anywhere = pl.BlockSpec(memory_space=pl.ANY)
    partial = pl.pallas_call(
        first_kernel,
        out_shape=rowed(subs * parts, rows + SUBL),
        in_specs=[vmem, anywhere, vmem, vmem, smem, vmem],
        out_specs=vmem,
        scratch_shapes=[*held, fold],
        compiler_params=params,
        name="first_image",
    )(pair, blocks, pattern, local_map, neighbours, coupling)
    group = lax.all_to_all(partial, ("sub", "blk"), 0, 0, tiled=True)
    partial, image = pl.pallas_call(
        second_kernel,
        out_shape=(rowed(rows + SUBL), rowed(own_rows)),
        in_specs=[vmem, vmem, anywhere, vmem, vmem, smem, vmem],
        out_specs=(vmem, vmem),
        scratch_shapes=[*held, fold, pltpu.VMEM((rows, LANES), jnp.float32)],
        compiler_params=params,
        name="second_image",
    )(pair, group, blocks, pattern, local_map, neighbours, coupling)
    both = lax.all_gather(partial, "blk")
    sums, again = pl.pallas_call(
        pair_kernel,
        out_shape=(rowed(reps * subs, 1), rowed(own_rows)),
        in_specs=[vmem],
        out_specs=(vmem, vmem),
        compiler_params=params,
        name="pair_sums",
    )(both)
    sums = lax.all_to_all(sums, ("rep", "sub"), 0, 0, tiled=True)
    second, third, entries = pl.pallas_call(
        functools.partial(last_kernel, float(cells)),
        out_shape=(rowed(own_rows), rowed(own_rows), jax.ShapeDtypeStruct((1, 5), jnp.float32)),
        in_specs=[vmem] * 4,
        out_specs=(vmem, vmem, vmem),
        compiler_params=params,
        name="arnoldi_entries",
    )(start, image, again, sums)
    return second.reshape(start_vector.shape), third.reshape(start_vector.shape), entries.reshape(5)


def solution(mesh):
    return jax.shard_map(
        per_device,
        mesh=mesh,
        in_specs=(
            P("rep", "sub", "blk"),
            P("rep", "sub", "blk", None, None),
            P("rep", "sub", None, None),
            P("rep", "sub", "blk"),
            P("rep", "sub", None),
            P("rep", "sub", None, "blk"),
        ),
        out_specs=(P("rep", "sub", "blk"), P("rep", "sub", "blk"), P()),
        check_vma=False,
    )
```

```python
import functools

import jax
import jax.numpy as jnp
from jax import lax
from jax.experimental import pallas as pl
from jax.experimental.pallas import tpu as pltpu
from jax.sharding import PartitionSpec as P

BS = 64
LANES = 128
SUBL = 8
epsilon = 1e-06


def pieces(value):
    high = value.astype(jnp.bfloat16)
    rest = value - high.astype(jnp.float32)
    middle = rest.astype(jnp.bfloat16)
    low = (rest - middle.astype(jnp.float32)).astype(jnp.bfloat16)
    return high, middle, low


def lane_iota(shape):
    return lax.broadcasted_iota(jnp.int32, shape, len(shape) - 1)


def row_iota(shape):
    return lax.broadcasted_iota(jnp.int32, shape, 0)


def block_product(vector, blocks_ref, pattern_ref, first_slot, fold_ref):
    slots, block_rows, width = blocks_ref.shape
    half = block_rows // 2
    lower = lane_iota(vector.shape) < BS
    turned = pltpu.roll(vector, BS, 1)
    table = jnp.concatenate([jnp.where(lower, vector, turned), jnp.where(lower, turned, vector)], 0)
    table = jnp.concatenate(pieces(table), 0)
    place = row_iota((block_rows, block_rows))
    place = jnp.where(place < half, 2 * place, 2 * (place - half) + 1)
    picked = []
    for k in range(slots):
        names = pattern_ref[pl.ds(first_slot + k, 1), :]
        chosen = (place == names).astype(jnp.float32).astype(jnp.bfloat16)
        chosen = jnp.concatenate([chosen] * 3, 0)
        picked.append(
            lax.dot_general(chosen, table, (((0,), (0,)), ((), ())), preferred_element_type=jnp.float32)
        )
    ones = (row_iota((2 * LANES, LANES)) % LANES) // BS == lane_iota((2 * LANES, LANES)) % 2
    ones = ones.astype(jnp.float32).astype(jnp.bfloat16)
    pair = (lane_iota((block_rows, LANES)) % BS) // 2
    result = jnp.zeros((block_rows, LANES), jnp.float32)
    for c in range(width // LANES):
        total = None
        for k in range(slots):
            term = blocks_ref[k, :, pl.ds(c * LANES, LANES)].astype(jnp.float32) * picked[k]
            total = term if total is None else total + term
        high = total.astype(jnp.bfloat16)
        low = (total - high.astype(jnp.float32)).astype(jnp.bfloat16)
        sums = lax.dot_general(
            jnp.concatenate([high, low], 1), ones, (((1,), (0,)), ((), ())), preferred_element_type=jnp.float32
        )
        result = jnp.where(pair == c, sums, result)
    fold_ref[...] = result
    even = fold_ref[pl.ds(0, half, stride=2), :]
    odd = fold_ref[pl.ds(1, half, stride=2), :]
    return jnp.where(lane_iota((half, LANES)) < BS, even, odd)


def take_trace(rows, places):
    count = rows.shape[0]
    low = jnp.broadcast_to(places % LANES, (count, LANES))
    picked = jnp.take_along_axis(rows, low, axis=1)
    return jnp.sum(jnp.where(row_iota((count, LANES)) == places // LANES, picked, 0.0), axis=0, keepdims=True)


def spread(values, places, count):
    aimed = jnp.where(row_iota((count, LANES)) == places // LANES, values, 0.0)
    high = aimed.astype(jnp.bfloat16).astype(jnp.float32)
    rest = aimed - high
    middle = rest.astype(jnp.bfloat16).astype(jnp.float32)
    stack = jnp.concatenate([high, middle, rest - middle], 0).astype(jnp.bfloat16)
    target = (row_iota((LANES, LANES)) == places % LANES).astype(jnp.float32).astype(jnp.bfloat16)
    landed = lax.dot_general(stack, target, (((1,), (1,)), ((), ())), preferred_element_type=jnp.float32)
    return landed[0:count] + landed[count : 2 * count] + landed[2 * count : 3 * count]


def lines_kernel(start_ref, map_ref, near_ref, coupling_ref, out_ref):
    places = map_ref[...]
    count = coupling_ref.shape[0]
    first_cell = lax.axis_index("blk") * start_ref.shape[0] * LANES
    lines = [take_trace(start_ref[...], places - first_cell), places.astype(jnp.float32)]
    lines += [coupling_ref[n : n + 1, :] for n in range(count)]
    near = near_ref[...].astype(jnp.float32)
    lines += [jnp.broadcast_to(near[:, n : n + 1], (1, LANES)) for n in range(count)]
    lines += [jnp.zeros((SUBL - len(lines), LANES), jnp.float32)]
    out_ref[...] = jnp.concatenate(lines, 0)


def first_kernel(start_ref, lines_ref, other_ref, blocks_ref, pattern_ref, out_ref, vector_ref, fold_ref):
    own_rows, rows = start_ref.shape[0], vector_ref.shape[0]
    blk, parts = lax.axis_index("blk"), lax.axis_size("blk")
    for step in range(parts):
        place = lax.rem(blk + step, parts)
        place = pl.ds(pl.multiple_of(place * own_rows, SUBL), own_rows)
        vector_ref[place, :] = other_ref[step - 1] if step else start_ref[...]
    partial = block_product(vector_ref[...], blocks_ref, pattern_ref, blk * blocks_ref.shape[0], fold_ref)
    for device in range(out_ref.shape[0]):
        out_ref[device, 0:rows, :] = partial
        out_ref[device, rows : rows + SUBL, :] = lines_ref[...]


def second_kernel(
    start_ref, vector_ref, group_ref, blocks_ref, pattern_ref, near_ref, out_ref, own_ref, fold_ref, image_ref
):
    own_rows, rows = start_ref.shape[0], vector_ref.shape[0]
    sub, blk = lax.axis_index("sub"), lax.axis_index("blk")
    subs, parts = lax.axis_size("sub"), lax.axis_size("blk")
    count = near_ref.shape[1]
    own = pl.ds(pl.multiple_of(blk * own_rows, SUBL), own_rows)

    def line(sub_at, part, i):
        return group_ref[sub_at * parts + part, rows + i : rows + i + 1, :]

    def landed(sub_at, part):
        traces = jnp.concatenate([line(other, part, 0) for other in range(subs)], 0)
        names = row_iota(traces.shape).astype(jnp.float32)
        inflow = jnp.zeros((1, LANES), jnp.float32)
        for n in range(count):
            chosen = jnp.where(names == line(sub_at, part, 2 + count + n), traces, 0.0)
            inflow = inflow + line(sub_at, part, 2 + n) * jnp.sum(chosen, axis=0, keepdims=True)
        places = line(sub_at, part, 1).astype(jnp.int32) - part * own_rows * LANES
        return spread(inflow, places, own_rows), places

    def summed(index, where):
        total = group_ref[index * parts, where, :]
        for b in range(1, parts):
            total = total + group_ref[index * parts + b, where, :]
        return total

    added = jnp.concatenate([landed(sub, b)[0] for b in range(parts)], 0)
    image = summed(sub, pl.ds(0, rows)) + added
    image_ref[...] = image
    second = block_product(image, blocks_ref, pattern_ref, blk * blocks_ref.shape[0], fold_ref)
    inflow = jnp.zeros((1, LANES), jnp.float32)
    for n in range(count):
        source = near_ref[0, n]
        added, places = landed(source, blk)
        inflow = inflow + line(sub, blk, 2 + n) * take_trace(summed(source, own) + added, places)
    places = line(sub, blk, 1).astype(jnp.int32) - blk * own_rows * LANES
    out_ref[0:rows, :] = second
    out_ref[own, :] = out_ref[own, :] + spread(inflow, places, own_rows)
    second = out_ref[0:rows, :]
    vector = vector_ref[...]
    vector_own, image_own = start_ref[...], image_ref[own, :]
    own_ref[...] = image_own

    def down(left, right):
        return jnp.sum(left * right, axis=0, keepdims=True)

    sums = [
        down(vector_own, vector_own),
        down(vector_own, image_own),
        down(image_own, image_own),
        down(vector, second),
        down(image, second),
        jnp.zeros((SUBL - 5, LANES), jnp.float32),
    ]
    out_ref[rows : rows + SUBL, :] = jnp.concatenate(sums, 0)


def pair_kernel(pair_ref, out_ref, own_ref):
    parts, height, _ = pair_ref.shape
    rows = height - SUBL
    own_rows = rows // parts
    total = pair_ref[0]
    for b in range(1, parts):
        total = total + pair_ref[b]
    square = jnp.sum(total[0:rows] * total[0:rows], axis=0, keepdims=True)
    sums = jnp.where(row_iota((SUBL, LANES)) == 5, square, total[rows:height])
    sums = jnp.sum(sums, axis=1, keepdims=True)
    sums = jnp.where(row_iota((SUBL, LANES)) == lane_iota((SUBL, LANES)), sums, 0.0)
    sums = jnp.sum(sums, axis=0, keepdims=True)
    for device in range(out_ref.shape[0]):
        out_ref[device] = sums
    own = pl.ds(pl.multiple_of(lax.axis_index("blk") * own_rows, SUBL), own_rows)
    again = pair_ref[0, own, :]
    for b in range(1, parts):
        again = again + pair_ref[b, own, :]
    own_ref[...] = again


def last_kernel(cells, start_ref, own_ref, again_ref, sums_ref, second_ref, third_ref, entries_ref):
    sums = jnp.sum(sums_ref[...], axis=0) / cells

    def whole(i):
        return jnp.broadcast_to(sums[:, i : i + 1], (1, LANES))

    vv, vw, ww, vy, wy, yy = (whole(i) for i in range(6))
    norm_square = vv + epsilon
    h11 = vw / norm_square
    first_square = jnp.maximum(ww - 2.0 * h11 * vw + h11 * h11 * vv, 0.0) / norm_square
    h21 = jnp.sqrt(first_square + epsilon)
    scale = 1.0 / (jnp.sqrt(norm_square) * h21)
    h12 = (vy - h11 * vw) / (norm_square * h21)
    h22 = (wy - h11 * (ww + vy - h11 * vw)) * scale * scale
    near = h11 + h22
    far = h12 * h21 - h11 * h22
    second_square = yy + near * near * ww + far * far * vv + 2.0 * (near * far * vw - near * wy - far * vy)
    h32 = jnp.sqrt(jnp.maximum(second_square, 0.0) * scale * scale + epsilon)

    vector, image = start_ref[...], own_ref[...]
    second_ref[...] = (image - h11 * vector) * scale
    third_ref[...] = (again_ref[...] - near * image - far * vector) * (scale / h32)
    lane = lane_iota((1, LANES))
    entries = h32
    for i, value in enumerate((h11, h21, h12, h22)):
        entries = jnp.where(lane == i, value, entries)
    entries_ref[...] = entries[:, 0:5]


def per_device(start_vector, blocks, pattern, trace_map, neighbours, coupling):
    own_cells = start_vector.shape[2]
    own_rows = own_cells // LANES
    parts, subs, reps = lax.axis_size("blk"), lax.axis_size("sub"), lax.axis_size("rep")
    rows = own_rows * parts
    cells = own_cells * parts * subs * reps
    start = start_vector.reshape(own_rows, LANES)
    local_map = trace_map[0]
    blocks, pattern, neighbours, coupling = blocks[0, 0], pattern[0, 0], neighbours[0], coupling[0, 0]
    vmem = pl.BlockSpec(memory_space=pltpu.VMEM)
    params = pltpu.CompilerParams(vmem_limit_bytes=32 * 1024 * 1024)

    def rowed(*shape):
        return jax.ShapeDtypeStruct((*shape, LANES), jnp.float32)

    smem = pl.BlockSpec(memory_space=pltpu.SMEM)
    others = [
        lax.ppermute(start[None], "blk", [((i + step) % parts, i) for i in range(parts)])
        for step in range(1, parts)
    ]
    others = others[0] if parts == 2 else jnp.concatenate(others, 0)
    fold = pltpu.VMEM((blocks.shape[1], LANES), jnp.float32)
    lines = pl.pallas_call(
        lines_kernel,
        out_shape=rowed(SUBL),
        in_specs=[vmem] * 4,
        out_specs=vmem,
        compiler_params=params,
        cost_estimate=pl.CostEstimate(flops=1 << 32, bytes_accessed=1 << 20, transcendentals=0),
        name="group_lines",
    )(start, local_map, neighbours, coupling)
    partial, vector = pl.pallas_call(
        first_kernel,
        out_shape=(rowed(subs * parts, rows + SUBL), rowed(rows)),
        in_specs=[vmem] * 5,
        out_specs=(vmem, vmem),
        scratch_shapes=[fold],
        compiler_params=params,
        name="first_image",
    )(start, lines, others, blocks, pattern)
    group = lax.all_to_all(partial, ("sub", "blk"), 0, 0, tiled=True)
    partial, image = pl.pallas_call(
        second_kernel,
        out_shape=(rowed(rows + SUBL), rowed(own_rows)),
        in_specs=[vmem, vmem, vmem, vmem, vmem, smem],
        out_specs=(vmem, vmem),
        scratch_shapes=[fold, pltpu.VMEM((rows, LANES), jnp.float32)],
        compiler_params=params,
        name="second_image",
    )(start, vector, group, blocks, pattern, neighbours)
    both = lax.all_gather(partial, "blk")
    sums, again = pl.pallas_call(
        pair_kernel,
        out_shape=(rowed(reps * subs, 1), rowed(own_rows)),
        in_specs=[vmem],
        out_specs=(vmem, vmem),
        compiler_params=params,
        name="pair_sums",
    )(both)
    sums = lax.all_to_all(sums, ("rep", "sub"), 0, 0, tiled=True)
    second, third, entries = pl.pallas_call(
        functools.partial(last_kernel, float(cells)),
        out_shape=(rowed(own_rows), rowed(own_rows), jax.ShapeDtypeStruct((1, 5), jnp.float32)),
        in_specs=[vmem] * 4,
        out_specs=(vmem, vmem, vmem),
        compiler_params=params,
        name="arnoldi_entries",
    )(start, image, again, sums)
    return second.reshape(start_vector.shape), third.reshape(start_vector.shape), entries.reshape(5)


def solution(mesh):
    return jax.shard_map(
        per_device,
        mesh=mesh,
        in_specs=(
            P("rep", "sub", "blk"),
            P("rep", "sub", "blk", None, None),
            P("rep", "sub", None, None),
            P("rep", "sub", "blk"),
            P("rep", "sub", None),
            P("rep", "sub", None, "blk"),
        ),
        out_specs=(P("rep", "sub", "blk"), P("rep", "sub", "blk"), P()),
        check_vma=False,
    )
```

```python
import functools

import jax
import jax.numpy as jnp
from jax import lax
from jax.experimental import pallas as pl
from jax.experimental.pallas import tpu as pltpu
from jax.sharding import PartitionSpec as P

BS = 64
LANES = 128
SUBL = 8
epsilon = 1e-06


def pieces(value):
    high = value.astype(jnp.bfloat16)
    rest = value - high.astype(jnp.float32)
    middle = rest.astype(jnp.bfloat16)
    low = (rest - middle.astype(jnp.float32)).astype(jnp.bfloat16)
    return high, middle, low


def lane_iota(shape):
    return lax.broadcasted_iota(jnp.int32, shape, len(shape) - 1)


def row_iota(shape):
    return lax.broadcasted_iota(jnp.int32, shape, 0)


def block_product(vector, blocks_ref, pattern_ref, first_slot, fold_ref):
    slots, block_rows, width = blocks_ref.shape
    half = block_rows // 2
    lower = lane_iota(vector.shape) < BS
    turned = pltpu.roll(vector, BS, 1)
    table = jnp.concatenate([jnp.where(lower, vector, turned), jnp.where(lower, turned, vector)], 0)
    table = jnp.concatenate(pieces(table), 0)
    place = row_iota((block_rows, block_rows))
    place = jnp.where(place < half, 2 * place, 2 * (place - half) + 1)
    picked = []
    for k in range(slots):
        names = pattern_ref[pl.ds(first_slot + k, 1), :]
        chosen = (place == names).astype(jnp.float32).astype(jnp.bfloat16)
        chosen = jnp.concatenate([chosen] * 3, 0)
        picked.append(
            lax.dot_general(chosen, table, (((0,), (0,)), ((), ())), preferred_element_type=jnp.float32)
        )
    ones = (row_iota((2 * LANES, LANES)) % LANES) // BS == lane_iota((2 * LANES, LANES)) % 2
    ones = ones.astype(jnp.float32).astype(jnp.bfloat16)
    pair = (lane_iota((block_rows, LANES)) % BS) // 2
    result = jnp.zeros((block_rows, LANES), jnp.float32)
    for c in range(width // LANES):
        total = None
        for k in range(slots):
            term = blocks_ref[k, :, pl.ds(c * LANES, LANES)].astype(jnp.float32) * picked[k]
            total = term if total is None else total + term
        high = total.astype(jnp.bfloat16)
        low = (total - high.astype(jnp.float32)).astype(jnp.bfloat16)
        sums = lax.dot_general(
            jnp.concatenate([high, low], 1), ones, (((1,), (0,)), ((), ())), preferred_element_type=jnp.float32
        )
        result = jnp.where(pair == c, sums, result)
    fold_ref[...] = result
    even = fold_ref[pl.ds(0, half, stride=2), :]
    odd = fold_ref[pl.ds(1, half, stride=2), :]
    return jnp.where(lane_iota((half, LANES)) < BS, even, odd)


def take_trace(rows, places):
    count = rows.shape[0]
    low = jnp.broadcast_to(places % LANES, (count, LANES))
    picked = jnp.take_along_axis(rows, low, axis=1)
    return jnp.sum(jnp.where(row_iota((count, LANES)) == places // LANES, picked, 0.0), axis=0, keepdims=True)


def spread(values, places, count):
    aimed = jnp.where(row_iota((count, LANES)) == places // LANES, values, 0.0)
    high = aimed.astype(jnp.bfloat16).astype(jnp.float32)
    rest = aimed - high
    middle = rest.astype(jnp.bfloat16).astype(jnp.float32)
    stack = jnp.concatenate([high, middle, rest - middle], 0).astype(jnp.bfloat16)
    target = (row_iota((LANES, LANES)) == places % LANES).astype(jnp.float32).astype(jnp.bfloat16)
    landed = lax.dot_general(stack, target, (((1,), (1,)), ((), ())), preferred_element_type=jnp.float32)
    return landed[0:count] + landed[count : 2 * count] + landed[2 * count : 3 * count]


def lines_kernel(start_ref, map_ref, near_ref, coupling_ref, out_ref):
    places = map_ref[...]
    count = coupling_ref.shape[0]
    first_cell = lax.axis_index("blk") * start_ref.shape[0] * LANES
    lines = [take_trace(start_ref[...], places - first_cell), places.astype(jnp.float32)]
    lines += [coupling_ref[n : n + 1, :] for n in range(count)]
    near = near_ref[...].astype(jnp.float32)
    lines += [jnp.broadcast_to(near[:, n : n + 1], (1, LANES)) for n in range(count)]
    lines += [jnp.zeros((SUBL - len(lines), LANES), jnp.float32)]
    out_ref[...] = jnp.concatenate(lines, 0)


def first_kernel(start_ref, lines_ref, other_ref, blocks_ref, pattern_ref, out_ref, vector_ref, fold_ref):
    own_rows, rows = start_ref.shape[0], vector_ref.shape[0]
    blk, parts = lax.axis_index("blk"), lax.axis_size("blk")
    for step in range(parts):
        place = lax.rem(blk + step, parts)
        place = pl.ds(pl.multiple_of(place * own_rows, SUBL), own_rows)
        vector_ref[place, :] = other_ref[step - 1] if step else start_ref[...]
    partial = block_product(vector_ref[...], blocks_ref, pattern_ref, blk * blocks_ref.shape[0], fold_ref)
    for device in range(out_ref.shape[0]):
        out_ref[device, 0:rows, :] = partial
        out_ref[device, rows : rows + SUBL, :] = lines_ref[...]


def line(group_ref, device, i):
    first = group_ref.shape[1] - SUBL + i
    return group_ref[device, first : first + 1, :]


def landed(group_ref, sub_at, part, own_rows, count):
    parts = lax.axis_size("blk")
    traces = [line(group_ref, other * parts + part, 0) for other in range(lax.axis_size("sub"))]
    traces = jnp.concatenate(traces, 0)
    names = row_iota(traces.shape).astype(jnp.float32)
    device = sub_at * parts + part
    inflow = jnp.zeros((1, LANES), jnp.float32)
    for n in range(count):
        chosen = jnp.where(names == line(group_ref, device, 2 + count + n), traces, 0.0)
        inflow = inflow + line(group_ref, device, 2 + n) * jnp.sum(chosen, axis=0, keepdims=True)
    places = line(group_ref, device, 1).astype(jnp.int32) - part * own_rows * LANES
    return spread(inflow, places, own_rows), places


def summed(group_ref, sub_at, first, count):
    parts = lax.axis_size("blk")
    total = group_ref[sub_at * parts, first : first + count, :]
    for b in range(1, parts):
        total = total + group_ref[sub_at * parts + b, first : first + count, :]
    return total


def second_kernel(count, group_ref, blocks_ref, pattern_ref, out_ref, image_ref, fold_ref):
    rows = image_ref.shape[0]
    sub, blk, parts = lax.axis_index("sub"), lax.axis_index("blk"), lax.axis_size("blk")
    added = [landed(group_ref, sub, part, rows // parts, count)[0] for part in range(parts)]
    image = summed(group_ref, sub, 0, rows) + jnp.concatenate(added, 0)
    image_ref[...] = image
    out_ref[...] = block_product(image, blocks_ref, pattern_ref, blk * blocks_ref.shape[0], fold_ref)


def down(left, right):
    return jnp.sum(left * right, axis=0, keepdims=True)


def inflow_kernel(vector_ref, image_ref, group_ref, near_ref, out_ref, sums_ref):
    rows = image_ref.shape[0]
    count = near_ref.shape[1]
    sub, parts = lax.axis_index("sub"), lax.axis_size("blk")
    own_rows = rows // parts
    for part in range(parts):
        device = sub * parts + part
        inflow = jnp.zeros((1, LANES), jnp.float32)
        for n in range(count):
            source = near_ref[0, n]
            added, places = landed(group_ref, source, part, own_rows, count)
            trace = take_trace(summed(group_ref, source, part * own_rows, own_rows) + added, places)
            inflow = inflow + line(group_ref, device, 2 + n) * trace
        places = line(group_ref, device, 1).astype(jnp.int32) - part * own_rows * LANES
        out_ref[part * own_rows : (part + 1) * own_rows, :] = spread(inflow, places, own_rows)
    vector, image = vector_ref[...], image_ref[...]
    sums = [down(vector, vector), down(vector, image), down(image, image)]
    sums_ref[...] = jnp.concatenate([*sums, jnp.zeros((SUBL - len(sums), LANES), jnp.float32)], 0)


def pair_kernel(vector_ref, image_ref, sums_ref, inflow_ref, mine_ref, other_ref, out_ref, again_ref, part_ref):
    parts = part_ref.shape[0]
    for step in range(parts):
        part_ref[lax.rem(lax.axis_index("blk") + step, parts)] = other_ref[step - 1] if step else mine_ref[...]
    again = inflow_ref[...]
    for part in range(parts):
        again = again + part_ref[part]
    again_ref[...] = again
    sums = [down(vector_ref[...], again), down(image_ref[...], again), down(again, again)]
    sums = jnp.concatenate([sums_ref[0:3, :], *sums, sums_ref[6:SUBL, :]], 0)
    sums = jnp.sum(sums, axis=1, keepdims=True)
    sums = jnp.where(row_iota((SUBL, LANES)) == lane_iota((SUBL, LANES)), sums, 0.0)
    sums = jnp.sum(sums, axis=0, keepdims=True)
    for device in range(out_ref.shape[0]):
        out_ref[device] = sums


def last_kernel(cells, start_ref, image_ref, again_ref, sums_ref, second_ref, third_ref, entries_ref):
    sums = jnp.sum(sums_ref[...], axis=0) / cells

    def whole(i):
        return jnp.broadcast_to(sums[:, i : i + 1], (1, LANES))

    vv, vw, ww, vy, wy, yy = (whole(i) for i in range(6))
    norm_square = vv + epsilon
    h11 = vw / norm_square
    first_square = jnp.maximum(ww - 2.0 * h11 * vw + h11 * h11 * vv, 0.0) / norm_square
    h21 = jnp.sqrt(first_square + epsilon)
    scale = 1.0 / (jnp.sqrt(norm_square) * h21)
    h12 = (vy - h11 * vw) / (norm_square * h21)
    h22 = (wy - h11 * (ww + vy - h11 * vw)) * scale * scale
    near = h11 + h22
    far = h12 * h21 - h11 * h22
    second_square = yy + near * near * ww + far * far * vv + 2.0 * (near * far * vw - near * wy - far * vy)
    h32 = jnp.sqrt(jnp.maximum(second_square, 0.0) * scale * scale + epsilon)

    own_rows = start_ref.shape[0]
    own = pl.ds(pl.multiple_of(lax.axis_index("blk") * own_rows, SUBL), own_rows)
    vector, image = start_ref[...], image_ref[own, :]
    second_ref[...] = (image - h11 * vector) * scale
    third_ref[...] = (again_ref[own, :] - near * image - far * vector) * (scale / h32)
    lane = lane_iota((1, LANES))
    entries = h32
    for i, value in enumerate((h11, h21, h12, h22)):
        entries = jnp.where(lane == i, value, entries)
    entries_ref[...] = entries[:, 0:5]


def per_device(start_vector, blocks, pattern, trace_map, neighbours, coupling):
    own_cells = start_vector.shape[2]
    own_rows = own_cells // LANES
    parts, subs, reps = lax.axis_size("blk"), lax.axis_size("sub"), lax.axis_size("rep")
    rows = own_rows * parts
    cells = own_cells * parts * subs * reps
    start = start_vector.reshape(own_rows, LANES)
    local_map = trace_map[0]
    blocks, pattern, neighbours, coupling = blocks[0, 0], pattern[0, 0], neighbours[0], coupling[0, 0]
    vmem = pl.BlockSpec(memory_space=pltpu.VMEM)
    params = pltpu.CompilerParams(vmem_limit_bytes=32 * 1024 * 1024)

    def rowed(*shape):
        return jax.ShapeDtypeStruct((*shape, LANES), jnp.float32)

    smem = pl.BlockSpec(memory_space=pltpu.SMEM)

    def from_others(value):
        got = [
            lax.ppermute(value[None], "blk", [((i + step) % parts, i) for i in range(parts)])
            for step in range(1, parts)
        ]
        return got[0] if parts == 2 else jnp.concatenate(got, 0)

    others = from_others(start)
    fold = pltpu.VMEM((blocks.shape[1], LANES), jnp.float32)
    lines = pl.pallas_call(
        lines_kernel,
        out_shape=rowed(SUBL),
        in_specs=[vmem] * 4,
        out_specs=vmem,
        compiler_params=params,
        cost_estimate=pl.CostEstimate(flops=1 << 32, bytes_accessed=1 << 20, transcendentals=0),
        name="group_lines",
    )(start, local_map, neighbours, coupling)
    partial, vector = pl.pallas_call(
        first_kernel,
        out_shape=(rowed(subs * parts, rows + SUBL), rowed(rows)),
        in_specs=[vmem] * 5,
        out_specs=(vmem, vmem),
        scratch_shapes=[fold],
        compiler_params=params,
        name="first_image",
    )(start, lines, others, blocks, pattern)
    group = lax.all_to_all(partial, ("sub", "blk"), 0, 0, tiled=True)
    second, image = pl.pallas_call(
        functools.partial(second_kernel, coupling.shape[0]),
        out_shape=(rowed(rows), rowed(rows)),
        in_specs=[vmem] * 3,
        out_specs=(vmem, vmem),
        scratch_shapes=[fold],
        compiler_params=params,
        name="second_image",
    )(group, blocks, pattern)
    others = from_others(second)
    inflow, sums = pl.pallas_call(
        inflow_kernel,
        out_shape=(rowed(rows), rowed(SUBL)),
        in_specs=[vmem, vmem, vmem, smem],
        out_specs=(vmem, vmem),
        compiler_params=params,
        cost_estimate=pl.CostEstimate(flops=1 << 32, bytes_accessed=1 << 20, transcendentals=0),
        name="second_inflow",
    )(vector, image, group, neighbours)
    sums, again = pl.pallas_call(
        pair_kernel,
        out_shape=(rowed(reps * subs, 1), rowed(rows)),
        in_specs=[vmem] * 6,
        out_specs=(vmem, vmem),
        scratch_shapes=[pltpu.VMEM((parts, rows, LANES), jnp.float32)],
        compiler_params=params,
        name="pair_sums",
    )(vector, image, sums, inflow, second, others)
    sums = lax.all_to_all(sums, ("rep", "sub"), 0, 0, tiled=True)
    second, third, entries = pl.pallas_call(
        functools.partial(last_kernel, float(cells)),
        out_shape=(rowed(own_rows), rowed(own_rows), jax.ShapeDtypeStruct((1, 5), jnp.float32)),
        in_specs=[vmem] * 4,
        out_specs=(vmem, vmem, vmem),
        compiler_params=params,
        name="arnoldi_entries",
    )(start, image, again, sums)
    return second.reshape(start_vector.shape), third.reshape(start_vector.shape), entries.reshape(5)


def solution(mesh):
    return jax.shard_map(
        per_device,
        mesh=mesh,
        in_specs=(
            P("rep", "sub", "blk"),
            P("rep", "sub", "blk", None, None),
            P("rep", "sub", None, None),
            P("rep", "sub", "blk"),
            P("rep", "sub", None),
            P("rep", "sub", None, "blk"),
        ),
        out_specs=(P("rep", "sub", "blk"), P("rep", "sub", "blk"), P()),
        check_vma=False,
    )
```

```python
import functools

import jax
import jax.numpy as jnp
from jax import lax
from jax.experimental import pallas as pl
from jax.experimental.pallas import tpu as pltpu
from jax.sharding import PartitionSpec as P

BS = 64
LANES = 128
SUBL = 8
epsilon = 1e-06


def pieces(value):
    high = value.astype(jnp.bfloat16)
    rest = value - high.astype(jnp.float32)
    middle = rest.astype(jnp.bfloat16)
    low = (rest - middle.astype(jnp.float32)).astype(jnp.bfloat16)
    return high, middle, low


def lane_iota(shape):
    return lax.broadcasted_iota(jnp.int32, shape, len(shape) - 1)


def row_iota(shape):
    return lax.broadcasted_iota(jnp.int32, shape, 0)


def block_product(vector, blocks_ref, pattern_ref, first_slot, fold_ref):
    slots, block_rows, width = blocks_ref.shape
    half = block_rows // 2
    lower = lane_iota(vector.shape) < BS
    turned = pltpu.roll(vector, BS, 1)
    table = jnp.concatenate([jnp.where(lower, vector, turned), jnp.where(lower, turned, vector)], 0)
    table = jnp.concatenate(pieces(table), 0)
    place = row_iota((block_rows, block_rows))
    place = jnp.where(place < half, 2 * place, 2 * (place - half) + 1)
    picked = []
    for k in range(slots):
        names = pattern_ref[pl.ds(first_slot + k, 1), :]
        chosen = (place == names).astype(jnp.float32).astype(jnp.bfloat16)
        chosen = jnp.concatenate([chosen] * 3, 0)
        picked.append(
            lax.dot_general(chosen, table, (((0,), (0,)), ((), ())), preferred_element_type=jnp.float32)
        )
    ones = (row_iota((2 * LANES, LANES)) % LANES) // BS == lane_iota((2 * LANES, LANES)) % 2
    ones = ones.astype(jnp.float32).astype(jnp.bfloat16)
    pair = (lane_iota((block_rows, LANES)) % BS) // 2
    result = jnp.zeros((block_rows, LANES), jnp.float32)
    for c in range(width // LANES):
        total = None
        for k in range(slots):
            term = blocks_ref[k, :, pl.ds(c * LANES, LANES)] * picked[k]
            total = term if total is None else total + term
        high = total.astype(jnp.bfloat16)
        low = (total - high.astype(jnp.float32)).astype(jnp.bfloat16)
        sums = lax.dot_general(
            jnp.concatenate([high, low], 1), ones, (((1,), (0,)), ((), ())), preferred_element_type=jnp.float32
        )
        result = jnp.where(pair == c, sums, result)
    fold_ref[...] = result
    even = fold_ref[pl.ds(0, half, stride=2), :]
    odd = fold_ref[pl.ds(1, half, stride=2), :]
    return jnp.where(lane_iota((half, LANES)) < BS, even, odd)


def take_trace(rows, places):
    count = rows.shape[0]
    low = jnp.broadcast_to(places % LANES, (count, LANES))
    picked = jnp.take_along_axis(rows, low, axis=1)
    return jnp.sum(jnp.where(row_iota((count, LANES)) == places // LANES, picked, 0.0), axis=0, keepdims=True)


def spread(values, places, count):
    aimed = jnp.where(row_iota((count, LANES)) == places // LANES, values, 0.0)
    high = aimed.astype(jnp.bfloat16).astype(jnp.float32)
    rest = aimed - high
    middle = rest.astype(jnp.bfloat16).astype(jnp.float32)
    stack = jnp.concatenate([high, middle, rest - middle], 0).astype(jnp.bfloat16)
    target = (row_iota((LANES, LANES)) == places % LANES).astype(jnp.float32).astype(jnp.bfloat16)
    landed = lax.dot_general(stack, target, (((1,), (1,)), ((), ())), preferred_element_type=jnp.float32)
    return landed[0:count] + landed[count : 2 * count] + landed[2 * count : 3 * count]


def lines_kernel(start_ref, map_ref, near_ref, coupling_ref, out_ref):
    places = map_ref[...]
    count = coupling_ref.shape[0]
    first_cell = lax.axis_index("blk") * start_ref.shape[0] * LANES
    lines = [take_trace(start_ref[...], places - first_cell), places.astype(jnp.float32)]
    lines += [coupling_ref[n : n + 1, :] for n in range(count)]
    near = near_ref[...].astype(jnp.float32)
    lines += [jnp.broadcast_to(near[:, n : n + 1], (1, LANES)) for n in range(count)]
    lines += [jnp.zeros((SUBL - len(lines), LANES), jnp.float32)]
    out_ref[...] = jnp.concatenate(lines, 0)


def widen_kernel(blocks_ref, out_ref):
    out_ref[...] = blocks_ref[...].astype(jnp.float32)


def first_kernel(start_ref, lines_ref, other_ref, blocks_ref, pattern_ref, out_ref, vector_ref, fold_ref):
    own_rows, rows = start_ref.shape[0], vector_ref.shape[0]
    blk, parts = lax.axis_index("blk"), lax.axis_size("blk")
    for step in range(parts):
        place = lax.rem(blk + step, parts)
        place = pl.ds(pl.multiple_of(place * own_rows, SUBL), own_rows)
        vector_ref[place, :] = other_ref[step - 1] if step else start_ref[...]
    partial = block_product(vector_ref[...], blocks_ref, pattern_ref, blk * blocks_ref.shape[0], fold_ref)
    for device in range(out_ref.shape[0]):
        out_ref[device, 0:rows, :] = partial
        out_ref[device, rows : rows + SUBL, :] = lines_ref[...]


def line(group_ref, device, i):
    first = group_ref.shape[1] - SUBL + i
    return group_ref[device, first : first + 1, :]


def landed(group_ref, sub_at, part, own_rows, count):
    parts = lax.axis_size("blk")
    traces = [line(group_ref, other * parts + part, 0) for other in range(lax.axis_size("sub"))]
    traces = jnp.concatenate(traces, 0)
    names = row_iota(traces.shape).astype(jnp.float32)
    device = sub_at * parts + part
    inflow = jnp.zeros((1, LANES), jnp.float32)
    for n in range(count):
        chosen = jnp.where(names == line(group_ref, device, 2 + count + n), traces, 0.0)
        inflow = inflow + line(group_ref, device, 2 + n) * jnp.sum(chosen, axis=0, keepdims=True)
    places = line(group_ref, device, 1).astype(jnp.int32) - part * own_rows * LANES
    return spread(inflow, places, own_rows), places


def summed(group_ref, sub_at, first, count):
    parts = lax.axis_size("blk")
    total = group_ref[sub_at * parts, first : first + count, :]
    for b in range(1, parts):
        total = total + group_ref[sub_at * parts + b, first : first + count, :]
    return total


def second_kernel(count, group_ref, blocks_ref, pattern_ref, out_ref, image_ref, fold_ref):
    rows = image_ref.shape[0]
    sub, blk, parts = lax.axis_index("sub"), lax.axis_index("blk"), lax.axis_size("blk")
    added = [landed(group_ref, sub, part, rows // parts, count)[0] for part in range(parts)]
    image = summed(group_ref, sub, 0, rows) + jnp.concatenate(added, 0)
    image_ref[...] = image
    out_ref[...] = block_product(image, blocks_ref, pattern_ref, blk * blocks_ref.shape[0], fold_ref)


def down(left, right):
    return jnp.sum(left * right, axis=0, keepdims=True)


def inflow_kernel(vector_ref, image_ref, group_ref, near_ref, out_ref, sums_ref):
    rows = image_ref.shape[0]
    count = near_ref.shape[1]
    sub, parts = lax.axis_index("sub"), lax.axis_size("blk")
    own_rows = rows // parts
    for part in range(parts):
        device = sub * parts + part
        inflow = jnp.zeros((1, LANES), jnp.float32)
        for n in range(count):
            source = near_ref[0, n]
            added, places = landed(group_ref, source, part, own_rows, count)
            trace = take_trace(summed(group_ref, source, part * own_rows, own_rows) + added, places)
            inflow = inflow + line(group_ref, device, 2 + n) * trace
        places = line(group_ref, device, 1).astype(jnp.int32) - part * own_rows * LANES
        out_ref[part * own_rows : (part + 1) * own_rows, :] = spread(inflow, places, own_rows)
    vector, image = vector_ref[...], image_ref[...]
    sums = [down(vector, vector), down(vector, image), down(image, image)]
    sums_ref[...] = jnp.concatenate([*sums, jnp.zeros((SUBL - len(sums), LANES), jnp.float32)], 0)


def pair_kernel(vector_ref, image_ref, sums_ref, inflow_ref, mine_ref, other_ref, out_ref, again_ref, part_ref):
    parts = part_ref.shape[0]
    for step in range(parts):
        part_ref[lax.rem(lax.axis_index("blk") + step, parts)] = other_ref[step - 1] if step else mine_ref[...]
    again = inflow_ref[...]
    for part in range(parts):
        again = again + part_ref[part]
    again_ref[...] = again
    sums = [down(vector_ref[...], again), down(image_ref[...], again), down(again, again)]
    sums = jnp.concatenate([sums_ref[0:3, :], *sums, sums_ref[6:SUBL, :]], 0)
    sums = jnp.sum(sums, axis=1, keepdims=True)
    sums = jnp.where(row_iota((SUBL, LANES)) == lane_iota((SUBL, LANES)), sums, 0.0)
    sums = jnp.sum(sums, axis=0, keepdims=True)
    for device in range(out_ref.shape[0]):
        out_ref[device] = sums


def last_kernel(cells, start_ref, image_ref, again_ref, sums_ref, second_ref, third_ref, entries_ref):
    sums = jnp.sum(sums_ref[...], axis=0) / cells

    def whole(i):
        return jnp.broadcast_to(sums[:, i : i + 1], (1, LANES))

    vv, vw, ww, vy, wy, yy = (whole(i) for i in range(6))
    norm_square = vv + epsilon
    inverse = 1.0 / norm_square
    h11 = vw * inverse
    skew = vy - h11 * vw
    first_square = jnp.maximum(ww - 2.0 * h11 * vw + h11 * h11 * vv, 0.0) * inverse + epsilon
    over_first = lax.rsqrt(first_square)
    h21 = first_square * over_first
    scale = lax.rsqrt(norm_square) * over_first
    h12 = skew * inverse * over_first
    h22 = (wy - h11 * (ww + skew)) * scale * scale
    near = h11 + h22
    far = skew * inverse - h11 * h22
    second_square = yy + near * near * ww + far * far * vv + 2.0 * (near * far * vw - near * wy - far * vy)
    second_square = jnp.maximum(second_square, 0.0) * scale * scale + epsilon
    over_second = lax.rsqrt(second_square)
    h32 = second_square * over_second

    own_rows = start_ref.shape[0]
    own = pl.ds(pl.multiple_of(lax.axis_index("blk") * own_rows, SUBL), own_rows)
    vector, image = start_ref[...], image_ref[own, :]
    second_ref[...] = (image - h11 * vector) * scale
    third_ref[...] = (again_ref[own, :] - near * image - far * vector) * (scale * over_second)
    lane = lane_iota((1, LANES))
    entries = h32
    for i, value in enumerate((h11, h21, h12, h22)):
        entries = jnp.where(lane == i, value, entries)
    entries_ref[...] = entries[:, 0:5]


def per_device(start_vector, blocks, pattern, trace_map, neighbours, coupling):
    own_cells = start_vector.shape[2]
    own_rows = own_cells // LANES
    parts, subs, reps = lax.axis_size("blk"), lax.axis_size("sub"), lax.axis_size("rep")
    rows = own_rows * parts
    cells = own_cells * parts * subs * reps
    start = start_vector.reshape(own_rows, LANES)
    local_map = trace_map[0]
    blocks, pattern, neighbours, coupling = blocks[0, 0], pattern[0, 0], neighbours[0], coupling[0, 0]
    vmem = pl.BlockSpec(memory_space=pltpu.VMEM)
    params = pltpu.CompilerParams(vmem_limit_bytes=32 * 1024 * 1024)

    def rowed(*shape):
        return jax.ShapeDtypeStruct((*shape, LANES), jnp.float32)

    smem = pl.BlockSpec(memory_space=pltpu.SMEM)

    def from_others(value):
        got = [
            lax.ppermute(value[None], "blk", [((i + step) % parts, i) for i in range(parts)])
            for step in range(1, parts)
        ]
        return got[0] if parts == 2 else jnp.concatenate(got, 0)

    others = from_others(start)
    fold = pltpu.VMEM((blocks.shape[1], LANES), jnp.float32)
    lines = pl.pallas_call(
        lines_kernel,
        out_shape=rowed(SUBL),
        in_specs=[vmem] * 4,
        out_specs=vmem,
        compiler_params=params,
        cost_estimate=pl.CostEstimate(flops=1 << 32, bytes_accessed=1 << 20, transcendentals=0),
        name="group_lines",
    )(start, local_map, neighbours, coupling)
    wide = pl.pallas_call(
        widen_kernel,
        out_shape=jax.ShapeDtypeStruct(blocks.shape, jnp.float32),
        in_specs=[vmem],
        out_specs=vmem,
        compiler_params=params,
        cost_estimate=pl.CostEstimate(flops=1 << 32, bytes_accessed=3 << 20, transcendentals=0),
        name="wide_blocks",
    )(blocks)
    partial, vector = pl.pallas_call(
        first_kernel,
        out_shape=(rowed(subs * parts, rows + SUBL), rowed(rows)),
        in_specs=[vmem] * 5,
        out_specs=(vmem, vmem),
        scratch_shapes=[fold],
        compiler_params=params,
        name="first_image",
    )(start, lines, others, wide, pattern)
    group = lax.all_to_all(partial, ("sub", "blk"), 0, 0, tiled=True)
    second, image = pl.pallas_call(
        functools.partial(second_kernel, coupling.shape[0]),
        out_shape=(rowed(rows), rowed(rows)),
        in_specs=[vmem] * 3,
        out_specs=(vmem, vmem),
        scratch_shapes=[fold],
        compiler_params=params,
        name="second_image",
    )(group, wide, pattern)
    others = from_others(second)
    inflow, sums = pl.pallas_call(
        inflow_kernel,
        out_shape=(rowed(rows), rowed(SUBL)),
        in_specs=[vmem, vmem, vmem, smem],
        out_specs=(vmem, vmem),
        compiler_params=params,
        cost_estimate=pl.CostEstimate(flops=1 << 32, bytes_accessed=1 << 20, transcendentals=0),
        name="second_inflow",
    )(vector, image, group, neighbours)
    sums, again = pl.pallas_call(
        pair_kernel,
        out_shape=(rowed(reps * subs, 1), rowed(rows)),
        in_specs=[vmem] * 6,
        out_specs=(vmem, vmem),
        scratch_shapes=[pltpu.VMEM((parts, rows, LANES), jnp.float32)],
        compiler_params=params,
        name="pair_sums",
    )(vector, image, sums, inflow, second, others)
    sums = lax.all_to_all(sums, ("rep", "sub"), 0, 0, tiled=True)
    second, third, entries = pl.pallas_call(
        functools.partial(last_kernel, float(cells)),
        out_shape=(rowed(own_rows), rowed(own_rows), jax.ShapeDtypeStruct((1, 5), jnp.float32)),
        in_specs=[vmem] * 4,
        out_specs=(vmem, vmem, vmem),
        compiler_params=params,
        name="arnoldi_entries",
    )(start, image, again, sums)
    return second.reshape(start_vector.shape), third.reshape(start_vector.shape), entries.reshape(5)


def solution(mesh):
    return jax.shard_map(
        per_device,
        mesh=mesh,
        in_specs=(
            P("rep", "sub", "blk"),
            P("rep", "sub", "blk", None, None),
            P("rep", "sub", None, None),
            P("rep", "sub", "blk"),
            P("rep", "sub", None),
            P("rep", "sub", None, "blk"),
        ),
        out_specs=(P("rep", "sub", "blk"), P("rep", "sub", "blk"), P()),
        check_vma=False,
    )
```

```python
import functools

import jax
import jax.numpy as jnp
from jax import lax
from jax.experimental import pallas as pl
from jax.experimental.pallas import tpu as pltpu
from jax.sharding import PartitionSpec as P

BS = 64
LANES = 128
SUBL = 8
epsilon = 1e-06


def pieces(value):
    high = value.astype(jnp.bfloat16)
    rest = value - high.astype(jnp.float32)
    middle = rest.astype(jnp.bfloat16)
    low = (rest - middle.astype(jnp.float32)).astype(jnp.bfloat16)
    return high, middle, low


def lane_iota(shape):
    return lax.broadcasted_iota(jnp.int32, shape, len(shape) - 1)


def row_iota(shape):
    return lax.broadcasted_iota(jnp.int32, shape, 0)


def block_product(vector, blocks_ref, pattern_ref, first_slot, fold_ref, halves_ref):
    slots, block_rows, width = blocks_ref.shape
    half = block_rows // 2
    lower = lane_iota(vector.shape) < BS
    turned = pltpu.roll(vector, BS, 1)
    table = jnp.concatenate([jnp.where(lower, vector, turned), jnp.where(lower, turned, vector)], 0)
    table = jnp.concatenate(pieces(table), 0)
    place = row_iota((block_rows, block_rows))
    place = jnp.where(place < half, 2 * place, 2 * (place - half) + 1)
    picked = []
    for k in range(slots):
        names = pattern_ref[pl.ds(first_slot + k, 1), :]
        chosen = (place == names).astype(jnp.float32).astype(jnp.bfloat16)
        chosen = jnp.concatenate([chosen] * 3, 0)
        picked.append(
            lax.dot_general(chosen, table, (((0,), (0,)), ((), ())), preferred_element_type=jnp.float32)
        )
    ones = (row_iota((2 * LANES, LANES)) % LANES) // BS == lane_iota((2 * LANES, LANES)) % 2
    ones = ones.astype(jnp.float32).astype(jnp.bfloat16)
    pair = (lane_iota((block_rows, LANES)) % BS) // 2
    chunks = width // LANES
    for c in range(chunks):
        total = None
        for k in range(slots):
            term = blocks_ref[k, :, pl.ds(c * LANES, LANES)] * picked[k]
            total = term if total is None else total + term
        high = total.astype(jnp.bfloat16)
        here = pl.ds(c * block_rows, block_rows)
        halves_ref[here, 0:LANES] = high
        halves_ref[here, LANES : 2 * LANES] = (total - high.astype(jnp.float32)).astype(jnp.bfloat16)
    sums = lax.dot_general(halves_ref[...], ones, (((1,), (0,)), ((), ())), preferred_element_type=jnp.float32)
    result = sums[0:block_rows]
    for c in range(1, chunks):
        result = jnp.where(pair == c, sums[c * block_rows : (c + 1) * block_rows], result)
    fold_ref[...] = result
    even = fold_ref[pl.ds(0, half, stride=2), :]
    odd = fold_ref[pl.ds(1, half, stride=2), :]
    return jnp.where(lane_iota((half, LANES)) < BS, even, odd)


def take_trace(rows, places):
    count = rows.shape[0]
    low = jnp.broadcast_to(places % LANES, (count, LANES))
    picked = jnp.take_along_axis(rows, low, axis=1)
    return jnp.sum(jnp.where(row_iota((count, LANES)) == places // LANES, picked, 0.0), axis=0, keepdims=True)


def spread(values, places, count):
    aimed = jnp.where(row_iota((count, LANES)) == places // LANES, values, 0.0)
    high = aimed.astype(jnp.bfloat16).astype(jnp.float32)
    rest = aimed - high
    middle = rest.astype(jnp.bfloat16).astype(jnp.float32)
    stack = jnp.concatenate([high, middle, rest - middle], 0).astype(jnp.bfloat16)
    target = (row_iota((LANES, LANES)) == places % LANES).astype(jnp.float32).astype(jnp.bfloat16)
    landed = lax.dot_general(stack, target, (((1,), (1,)), ((), ())), preferred_element_type=jnp.float32)
    return landed[0:count] + landed[count : 2 * count] + landed[2 * count : 3 * count]


def lines_kernel(start_ref, map_ref, near_ref, coupling_ref, out_ref):
    places = map_ref[...]
    count = coupling_ref.shape[0]
    first_cell = lax.axis_index("blk") * start_ref.shape[0] * LANES
    lines = [take_trace(start_ref[...], places - first_cell), places.astype(jnp.float32)]
    lines += [coupling_ref[n : n + 1, :] for n in range(count)]
    near = near_ref[...].astype(jnp.float32)
    lines += [jnp.broadcast_to(near[:, n : n + 1], (1, LANES)) for n in range(count)]
    lines += [jnp.zeros((SUBL - len(lines), LANES), jnp.float32)]
    out_ref[...] = jnp.concatenate(lines, 0)


def widen_kernel(blocks_ref, out_ref):
    out_ref[...] = blocks_ref[...].astype(jnp.float32)


def first_kernel(start_ref, lines_ref, other_ref, blocks_ref, pattern_ref, out_ref, vector_ref, fold_ref, halves_ref):
    own_rows, rows = start_ref.shape[0], vector_ref.shape[0]
    blk, parts = lax.axis_index("blk"), lax.axis_size("blk")
    for step in range(parts):
        place = lax.rem(blk + step, parts)
        place = pl.ds(pl.multiple_of(place * own_rows, SUBL), own_rows)
        vector_ref[place, :] = other_ref[step - 1] if step else start_ref[...]
    partial = block_product(vector_ref[...], blocks_ref, pattern_ref, blk * blocks_ref.shape[0], fold_ref, halves_ref)
    for device in range(out_ref.shape[0]):
        out_ref[device, 0:rows, :] = partial
        out_ref[device, rows : rows + SUBL, :] = lines_ref[...]


def line(group_ref, device, i):
    first = group_ref.shape[1] - SUBL + i
    return group_ref[device, first : first + 1, :]


def landed(group_ref, sub_at, part, own_rows, count):
    parts = lax.axis_size("blk")
    traces = [line(group_ref, other * parts + part, 0) for other in range(lax.axis_size("sub"))]
    traces = jnp.concatenate(traces, 0)
    names = row_iota(traces.shape).astype(jnp.float32)
    device = sub_at * parts + part
    inflow = jnp.zeros((1, LANES), jnp.float32)
    for n in range(count):
        chosen = jnp.where(names == line(group_ref, device, 2 + count + n), traces, 0.0)
        inflow = inflow + line(group_ref, device, 2 + n) * jnp.sum(chosen, axis=0, keepdims=True)
    places = line(group_ref, device, 1).astype(jnp.int32) - part * own_rows * LANES
    return spread(inflow, places, own_rows), places


def summed(group_ref, sub_at, first, count):
    parts = lax.axis_size("blk")
    total = group_ref[sub_at * parts, first : first + count, :]
    for b in range(1, parts):
        total = total + group_ref[sub_at * parts + b, first : first + count, :]
    return total


def second_kernel(count, group_ref, blocks_ref, pattern_ref, out_ref, image_ref, fold_ref, halves_ref):
    rows = image_ref.shape[0]
    sub, blk, parts = lax.axis_index("sub"), lax.axis_index("blk"), lax.axis_size("blk")
    added = [landed(group_ref, sub, part, rows // parts, count)[0] for part in range(parts)]
    image = summed(group_ref, sub, 0, rows) + jnp.concatenate(added, 0)
    image_ref[...] = image
    out_ref[...] = block_product(image, blocks_ref, pattern_ref, blk * blocks_ref.shape[0], fold_ref, halves_ref)


def down(left, right):
    return jnp.sum(left * right, axis=0, keepdims=True)


def inflow_kernel(vector_ref, image_ref, group_ref, near_ref, out_ref, sums_ref):
    rows = image_ref.shape[0]
    count = near_ref.shape[1]
    sub, parts = lax.axis_index("sub"), lax.axis_size("blk")
    own_rows = rows // parts
    for part in range(parts):
        device = sub * parts + part
        inflow = jnp.zeros((1, LANES), jnp.float32)
        for n in range(count):
            source = near_ref[0, n]
            added, places = landed(group_ref, source, part, own_rows, count)
            trace = take_trace(summed(group_ref, source, part * own_rows, own_rows) + added, places)
            inflow = inflow + line(group_ref, device, 2 + n) * trace
        places = line(group_ref, device, 1).astype(jnp.int32) - part * own_rows * LANES
        out_ref[part * own_rows : (part + 1) * own_rows, :] = spread(inflow, places, own_rows)
    vector, image = vector_ref[...], image_ref[...]
    sums = [down(vector, vector), down(vector, image), down(image, image)]
    sums_ref[...] = jnp.concatenate([*sums, jnp.zeros((SUBL - len(sums), LANES), jnp.float32)], 0)


def pair_kernel(vector_ref, image_ref, sums_ref, inflow_ref, mine_ref, other_ref, out_ref, again_ref, part_ref):
    parts = part_ref.shape[0]
    for step in range(parts):
        part_ref[lax.rem(lax.axis_index("blk") + step, parts)] = other_ref[step - 1] if step else mine_ref[...]
    again = inflow_ref[...]
    for part in range(parts):
        again = again + part_ref[part]
    again_ref[...] = again
    sums = [down(vector_ref[...], again), down(image_ref[...], again), down(again, again)]
    sums = jnp.concatenate([sums_ref[0:3, :], *sums, sums_ref[6:SUBL, :]], 0)
    sums = jnp.sum(sums, axis=1, keepdims=True)
    sums = jnp.where(row_iota((SUBL, LANES)) == lane_iota((SUBL, LANES)), sums, 0.0)
    sums = jnp.sum(sums, axis=0, keepdims=True)
    for device in range(out_ref.shape[0]):
        out_ref[device] = sums


def last_kernel(cells, start_ref, image_ref, again_ref, sums_ref, second_ref, third_ref, entries_ref):
    sums = jnp.sum(sums_ref[...], axis=0) / cells

    def whole(i):
        return jnp.broadcast_to(sums[:, i : i + 1], (1, LANES))

    vv, vw, ww, vy, wy, yy = (whole(i) for i in range(6))
    norm_square = vv + epsilon
    inverse = 1.0 / norm_square
    h11 = vw * inverse
    skew = vy - h11 * vw
    first_square = jnp.maximum(ww - 2.0 * h11 * vw + h11 * h11 * vv, 0.0) * inverse + epsilon
    over_first = lax.rsqrt(first_square)
    h21 = first_square * over_first
    scale = lax.rsqrt(norm_square) * over_first
    h12 = skew * inverse * over_first
    h22 = (wy - h11 * (ww + skew)) * scale * scale
    near = h11 + h22
    far = skew * inverse - h11 * h22
    second_square = yy + near * near * ww + far * far * vv + 2.0 * (near * far * vw - near * wy - far * vy)
    second_square = jnp.maximum(second_square, 0.0) * scale * scale + epsilon
    over_second = lax.rsqrt(second_square)
    h32 = second_square * over_second

    own_rows = start_ref.shape[0]
    own = pl.ds(pl.multiple_of(lax.axis_index("blk") * own_rows, SUBL), own_rows)
    vector, image = start_ref[...], image_ref[own, :]
    second_ref[...] = (image - h11 * vector) * scale
    third_ref[...] = (again_ref[own, :] - near * image - far * vector) * (scale * over_second)
    lane = lane_iota((1, LANES))
    entries = h32
    for i, value in enumerate((h11, h21, h12, h22)):
        entries = jnp.where(lane == i, value, entries)
    entries_ref[...] = entries[:, 0:5]


def per_device(start_vector, blocks, pattern, trace_map, neighbours, coupling):
    own_cells = start_vector.shape[2]
    own_rows = own_cells // LANES
    parts, subs, reps = lax.axis_size("blk"), lax.axis_size("sub"), lax.axis_size("rep")
    rows = own_rows * parts
    cells = own_cells * parts * subs * reps
    start = start_vector.reshape(own_rows, LANES)
    local_map = trace_map[0]
    blocks, pattern, neighbours, coupling = blocks[0, 0], pattern[0, 0], neighbours[0], coupling[0, 0]
    vmem = pl.BlockSpec(memory_space=pltpu.VMEM)
    params = pltpu.CompilerParams(vmem_limit_bytes=32 * 1024 * 1024)

    def rowed(*shape):
        return jax.ShapeDtypeStruct((*shape, LANES), jnp.float32)

    smem = pl.BlockSpec(memory_space=pltpu.SMEM)

    def from_others(value):
        got = [
            lax.ppermute(value[None], "blk", [((i + step) % parts, i) for i in range(parts)])
            for step in range(1, parts)
        ]
        return got[0] if parts == 2 else jnp.concatenate(got, 0)

    others = from_others(start)
    block_rows, width = blocks.shape[1:]
    scratch = [
        pltpu.VMEM((block_rows, LANES), jnp.float32),
        pltpu.VMEM((block_rows * width // LANES, 2 * LANES), jnp.bfloat16),
    ]
    lines = pl.pallas_call(
        lines_kernel,
        out_shape=rowed(SUBL),
        in_specs=[vmem] * 4,
        out_specs=vmem,
        compiler_params=params,
        cost_estimate=pl.CostEstimate(flops=1 << 32, bytes_accessed=1 << 20, transcendentals=0),
        name="group_lines",
    )(start, local_map, neighbours, coupling)
    wide = pl.pallas_call(
        widen_kernel,
        out_shape=jax.ShapeDtypeStruct(blocks.shape, jnp.float32),
        in_specs=[vmem],
        out_specs=vmem,
        compiler_params=params,
        cost_estimate=pl.CostEstimate(flops=1 << 32, bytes_accessed=3 << 20, transcendentals=0),
        name="wide_blocks",
    )(blocks)
    partial, vector = pl.pallas_call(
        first_kernel,
        out_shape=(rowed(subs * parts, rows + SUBL), rowed(rows)),
        in_specs=[vmem] * 5,
        out_specs=(vmem, vmem),
        scratch_shapes=scratch,
        compiler_params=params,
        name="first_image",
    )(start, lines, others, wide, pattern)
    group = lax.all_to_all(partial, ("sub", "blk"), 0, 0, tiled=True)
    second, image = pl.pallas_call(
        functools.partial(second_kernel, coupling.shape[0]),
        out_shape=(rowed(rows), rowed(rows)),
        in_specs=[vmem] * 3,
        out_specs=(vmem, vmem),
        scratch_shapes=scratch,
        compiler_params=params,
        name="second_image",
    )(group, wide, pattern)
    others = from_others(second)
    inflow, sums = pl.pallas_call(
        inflow_kernel,
        out_shape=(rowed(rows), rowed(SUBL)),
        in_specs=[vmem, vmem, vmem, smem],
        out_specs=(vmem, vmem),
        compiler_params=params,
        cost_estimate=pl.CostEstimate(flops=1 << 32, bytes_accessed=1 << 20, transcendentals=0),
        name="second_inflow",
    )(vector, image, group, neighbours)
    sums, again = pl.pallas_call(
        pair_kernel,
        out_shape=(rowed(reps * subs, 1), rowed(rows)),
        in_specs=[vmem] * 6,
        out_specs=(vmem, vmem),
        scratch_shapes=[pltpu.VMEM((parts, rows, LANES), jnp.float32)],
        compiler_params=params,
        name="pair_sums",
    )(vector, image, sums, inflow, second, others)
    sums = lax.all_to_all(sums, ("rep", "sub"), 0, 0, tiled=True)
    second, third, entries = pl.pallas_call(
        functools.partial(last_kernel, float(cells)),
        out_shape=(rowed(own_rows), rowed(own_rows), jax.ShapeDtypeStruct((1, 5), jnp.float32)),
        in_specs=[vmem] * 4,
        out_specs=(vmem, vmem, vmem),
        compiler_params=params,
        name="arnoldi_entries",
    )(start, image, again, sums)
    return second.reshape(start_vector.shape), third.reshape(start_vector.shape), entries.reshape(5)


def solution(mesh):
    return jax.shard_map(
        per_device,
        mesh=mesh,
        in_specs=(
            P("rep", "sub", "blk"),
            P("rep", "sub", "blk", None, None),
            P("rep", "sub", None, None),
            P("rep", "sub", "blk"),
            P("rep", "sub", None),
            P("rep", "sub", None, "blk"),
        ),
        out_specs=(P("rep", "sub", "blk"), P("rep", "sub", "blk"), P()),
        check_vma=False,
    )
```

```python
import functools

import jax
import jax.numpy as jnp
from jax import lax
from jax.experimental import pallas as pl
from jax.experimental.pallas import tpu as pltpu
from jax.sharding import PartitionSpec as P

BS = 64
LANES = 128
SUBL = 8
epsilon = 1e-06


def pieces(value):
    high = value.astype(jnp.bfloat16)
    rest = value - high.astype(jnp.float32)
    middle = rest.astype(jnp.bfloat16)
    low = (rest - middle.astype(jnp.float32)).astype(jnp.bfloat16)
    return high, middle, low


def lane_iota(shape):
    return lax.broadcasted_iota(jnp.int32, shape, len(shape) - 1)


def row_iota(shape):
    return lax.broadcasted_iota(jnp.int32, shape, 0)


def block_product(vector, blocks_ref, pattern_ref, first_slot, fold_ref, halves_ref):
    slots, block_rows, width = blocks_ref.shape
    half = block_rows // 2
    lower = lane_iota(vector.shape) < BS
    turned = pltpu.roll(vector, BS, 1)
    table = jnp.concatenate([jnp.where(lower, vector, turned), jnp.where(lower, turned, vector)], 0)
    table = jnp.concatenate(pieces(table), 0)
    place = row_iota((block_rows, block_rows))
    place = jnp.where(place < half, 2 * place, 2 * (place - half) + 1)
    picked = []
    for k in range(slots):
        names = pattern_ref[pl.ds(first_slot + k, 1), :]
        chosen = (place == names).astype(jnp.float32).astype(jnp.bfloat16)
        chosen = jnp.concatenate([chosen] * 3, 0)
        picked.append(
            lax.dot_general(chosen, table, (((0,), (0,)), ((), ())), preferred_element_type=jnp.float32)
        )
    ones = (row_iota((2 * LANES, LANES)) % LANES) // BS == lane_iota((2 * LANES, LANES)) % 2
    ones = ones.astype(jnp.float32).astype(jnp.bfloat16)
    pair = (lane_iota((block_rows, LANES)) % BS) // 2
    chunks = width // LANES
    for c in range(chunks):
        total = None
        for k in range(slots):
            term = blocks_ref[k, :, pl.ds(c * LANES, LANES)] * picked[k]
            total = term if total is None else total + term
        high = total.astype(jnp.bfloat16)
        here = pl.ds(c * block_rows, block_rows)
        halves_ref[here, 0:LANES] = high
        halves_ref[here, LANES : 2 * LANES] = (total - high.astype(jnp.float32)).astype(jnp.bfloat16)
    sums = lax.dot_general(halves_ref[...], ones, (((1,), (0,)), ((), ())), preferred_element_type=jnp.float32)
    result = sums[0:block_rows]
    for c in range(1, chunks):
        result = jnp.where(pair == c, sums[c * block_rows : (c + 1) * block_rows], result)
    fold_ref[...] = result
    even = fold_ref[pl.ds(0, half, stride=2), :]
    odd = fold_ref[pl.ds(1, half, stride=2), :]
    return jnp.where(lane_iota((half, LANES)) < BS, even, odd)


def take_trace(rows, places):
    count = rows.shape[0]
    low = jnp.broadcast_to(places % LANES, (count, LANES))
    picked = jnp.take_along_axis(rows, low, axis=1)
    return jnp.sum(jnp.where(row_iota((count, LANES)) == places // LANES, picked, 0.0), axis=0, keepdims=True)


def spread(values, places, count):
    aimed = jnp.where(row_iota((count, LANES)) == places // LANES, values, 0.0)
    high = aimed.astype(jnp.bfloat16).astype(jnp.float32)
    rest = aimed - high
    middle = rest.astype(jnp.bfloat16).astype(jnp.float32)
    stack = jnp.concatenate([high, middle, rest - middle], 0).astype(jnp.bfloat16)
    target = (row_iota((LANES, LANES)) == places % LANES).astype(jnp.float32).astype(jnp.bfloat16)
    landed = lax.dot_general(stack, target, (((1,), (1,)), ((), ())), preferred_element_type=jnp.float32)
    return landed[0:count] + landed[count : 2 * count] + landed[2 * count : 3 * count]


def lines_kernel(start_ref, map_ref, near_ref, coupling_ref, out_ref):
    places = map_ref[...]
    count = coupling_ref.shape[0]
    first_cell = lax.axis_index("blk") * start_ref.shape[0] * LANES
    lines = [take_trace(start_ref[...], places - first_cell), places.astype(jnp.float32)]
    lines += [coupling_ref[n : n + 1, :] for n in range(count)]
    near = near_ref[...].astype(jnp.float32)
    lines += [jnp.broadcast_to(near[:, n : n + 1], (1, LANES)) for n in range(count)]
    lines += [jnp.zeros((SUBL - len(lines), LANES), jnp.float32)]
    lines = jnp.concatenate(lines, 0)
    for device in range(out_ref.shape[0]):
        out_ref[device] = lines


def widen_kernel(blocks_ref, out_ref):
    out_ref[...] = blocks_ref[...].astype(jnp.float32)


def in_order(parts_ref, mine, other_ref):
    parts = parts_ref.shape[0]
    for step in range(parts):
        parts_ref[lax.rem(lax.axis_index("blk") + step, parts)] = other_ref[step - 1] if step else mine
    total = parts_ref[0]
    for part in range(1, parts):
        total = total + parts_ref[part]
    return total


def first_kernel(
    start_ref, other_ref, blocks_ref, pattern_ref, out_ref, partial_ref, vector_ref, parts_ref, fold_ref, halves_ref
):
    in_order(parts_ref, start_ref[...], other_ref)
    vector = jnp.concatenate([parts_ref[part] for part in range(parts_ref.shape[0])], 0)
    vector_ref[...] = vector
    blk = lax.axis_index("blk")
    partial = block_product(vector, blocks_ref, pattern_ref, blk * blocks_ref.shape[0], fold_ref, halves_ref)
    partial_ref[...] = partial
    for device in range(out_ref.shape[0]):
        out_ref[device] = partial


def line(group_ref, device, i):
    return group_ref[device, i : i + 1, :]


def landed(group_ref, sub_at, part, own_rows, count):
    parts = lax.axis_size("blk")
    traces = [line(group_ref, other * parts + part, 0) for other in range(lax.axis_size("sub"))]
    traces = jnp.concatenate(traces, 0)
    names = row_iota(traces.shape).astype(jnp.float32)
    device = sub_at * parts + part
    inflow = jnp.zeros((1, LANES), jnp.float32)
    for n in range(count):
        chosen = jnp.where(names == line(group_ref, device, 2 + count + n), traces, 0.0)
        inflow = inflow + line(group_ref, device, 2 + n) * jnp.sum(chosen, axis=0, keepdims=True)
    places = line(group_ref, device, 1).astype(jnp.int32) - part * own_rows * LANES
    return spread(inflow, places, own_rows), places


def second_kernel(
    count, lines_ref, mine_ref, other_ref, blocks_ref, pattern_ref, out_ref, image_ref, parts_ref, fold_ref, halves_ref
):
    parts, rows, _ = parts_ref.shape
    sub, blk = lax.axis_index("sub"), lax.axis_index("blk")
    added = [landed(lines_ref, sub, part, rows // parts, count)[0] for part in range(parts)]
    image = in_order(parts_ref, mine_ref[...], other_ref) + jnp.concatenate(added, 0)
    image_ref[...] = image
    out_ref[...] = block_product(image, blocks_ref, pattern_ref, blk * blocks_ref.shape[0], fold_ref, halves_ref)


def down(left, right):
    return jnp.sum(left * right, axis=0, keepdims=True)


def early_kernel(vector_ref, image_ref, lines_ref, near_ref, out_ref):
    vector, image = vector_ref[...], image_ref[...]
    own_rows = image.shape[0] // lax.axis_size("blk")
    sub, parts = lax.axis_index("sub"), lax.axis_size("blk")
    known = [down(vector, vector), down(vector, image), down(image, image)]
    count = near_ref.shape[1]
    for part in range(parts):
        share = jnp.zeros((1, LANES), jnp.float32)
        for n in range(count):
            added, places = landed(lines_ref, near_ref[0, n], part, own_rows, count)
            share = share + line(lines_ref, sub * parts + part, 2 + n) * take_trace(added, places)
        known.append(share)
    known.append(jnp.zeros((out_ref.shape[0] - len(known), LANES), jnp.float32))
    out_ref[...] = jnp.concatenate(known, 0)


def pair_kernel(
    vector_ref, image_ref, known_ref, lines_ref, group_ref, near_ref, mine_ref, other_ref, out_ref, again_ref, parts_ref
):
    parts, rows, _ = parts_ref.shape
    own_rows = rows // parts
    sub = lax.axis_index("sub")
    inflows = []
    for part in range(parts):
        inflow = known_ref[3 + part : 4 + part, :]
        first_cell = part * own_rows * LANES
        here = slice(part * own_rows, (part + 1) * own_rows)
        for n in range(near_ref.shape[1]):
            source = near_ref[0, n] * parts
            image = group_ref[source, here, :]
            for b in range(1, parts):
                image = image + group_ref[source + b, here, :]
            trace = take_trace(image, line(lines_ref, source + part, 1).astype(jnp.int32) - first_cell)
            inflow = inflow + line(lines_ref, sub * parts + part, 2 + n) * trace
        places = line(lines_ref, sub * parts + part, 1).astype(jnp.int32) - first_cell
        inflows.append(spread(inflow, places, own_rows))
    again = in_order(parts_ref, mine_ref[...], other_ref) + jnp.concatenate(inflows, 0)
    again_ref[...] = again
    sums = [down(vector_ref[...], again), down(image_ref[...], again), down(again, again)]
    sums = jnp.concatenate([known_ref[0:3, :], *sums, jnp.zeros((SUBL - 6, LANES), jnp.float32)], 0)
    sums = jnp.sum(sums, axis=1, keepdims=True)
    sums = jnp.where(row_iota((SUBL, LANES)) == lane_iota((SUBL, LANES)), sums, 0.0)
    sums = jnp.sum(sums, axis=0, keepdims=True)
    for device in range(out_ref.shape[0]):
        out_ref[device] = sums


def last_kernel(cells, start_ref, image_ref, again_ref, sums_ref, second_ref, third_ref, entries_ref):
    sums = jnp.sum(sums_ref[...], axis=0) / cells

    def whole(i):
        return jnp.broadcast_to(sums[:, i : i + 1], (1, LANES))

    vv, vw, ww, vy, wy, yy = (whole(i) for i in range(6))
    norm_square = vv + epsilon
    inverse = 1.0 / norm_square
    h11 = vw * inverse
    skew = vy - h11 * vw
    first_square = jnp.maximum(ww - 2.0 * h11 * vw + h11 * h11 * vv, 0.0) * inverse + epsilon
    over_first = lax.rsqrt(first_square)
    h21 = first_square * over_first
    scale = lax.rsqrt(norm_square) * over_first
    h12 = skew * inverse * over_first
    h22 = (wy - h11 * (ww + skew)) * scale * scale
    near = h11 + h22
    far = skew * inverse - h11 * h22
    second_square = yy + near * near * ww + far * far * vv + 2.0 * (near * far * vw - near * wy - far * vy)
    second_square = jnp.maximum(second_square, 0.0) * scale * scale + epsilon
    over_second = lax.rsqrt(second_square)
    h32 = second_square * over_second

    own_rows = start_ref.shape[0]
    own = pl.ds(pl.multiple_of(lax.axis_index("blk") * own_rows, SUBL), own_rows)
    vector, image = start_ref[...], image_ref[own, :]
    second_ref[...] = (image - h11 * vector) * scale
    third_ref[...] = (again_ref[own, :] - near * image - far * vector) * (scale * over_second)
    lane = lane_iota((1, LANES))
    entries = h32
    for i, value in enumerate((h11, h21, h12, h22)):
        entries = jnp.where(lane == i, value, entries)
    entries_ref[...] = entries[:, 0:5]


def per_device(start_vector, blocks, pattern, trace_map, neighbours, coupling):
    own_cells = start_vector.shape[2]
    own_rows = own_cells // LANES
    parts, subs, reps = lax.axis_size("blk"), lax.axis_size("sub"), lax.axis_size("rep")
    rows = own_rows * parts
    cells = own_cells * parts * subs * reps
    start = start_vector.reshape(own_rows, LANES)
    local_map = trace_map[0]
    blocks, pattern, neighbours, coupling = blocks[0, 0], pattern[0, 0], neighbours[0], coupling[0, 0]
    vmem = pl.BlockSpec(memory_space=pltpu.VMEM)
    params = pltpu.CompilerParams(vmem_limit_bytes=32 * 1024 * 1024)

    def rowed(*shape):
        return jax.ShapeDtypeStruct((*shape, LANES), jnp.float32)

    smem = pl.BlockSpec(memory_space=pltpu.SMEM)

    def from_others(value):
        got = [
            lax.ppermute(value[None], "blk", [((i + step) % parts, i) for i in range(parts)])
            for step in range(1, parts)
        ]
        return got[0] if parts == 2 else jnp.concatenate(got, 0)

    block_rows, width = blocks.shape[1:]
    scratch = [
        pltpu.VMEM((block_rows, LANES), jnp.float32),
        pltpu.VMEM((block_rows * width // LANES, 2 * LANES), jnp.bfloat16),
    ]
    in_parts = pltpu.VMEM((parts, rows, LANES), jnp.float32)
    long = pl.CostEstimate(flops=1 << 32, bytes_accessed=1 << 20, transcendentals=0)

    others = from_others(start)
    lines = pl.pallas_call(
        lines_kernel,
        out_shape=rowed(subs * parts, SUBL),
        in_specs=[vmem] * 4,
        out_specs=vmem,
        compiler_params=params,
        cost_estimate=long,
        name="group_lines",
    )(start, local_map, neighbours, coupling)
    lines = lax.all_to_all(lines, ("sub", "blk"), 0, 0, tiled=True)
    wide = pl.pallas_call(
        widen_kernel,
        out_shape=jax.ShapeDtypeStruct(blocks.shape, jnp.float32),
        in_specs=[vmem],
        out_specs=vmem,
        compiler_params=params,
        cost_estimate=long,
        name="wide_blocks",
    )(blocks)
    slots, partial, vector = pl.pallas_call(
        first_kernel,
        out_shape=(rowed(subs * parts, rows), rowed(rows), rowed(rows)),
        in_specs=[vmem] * 4,
        out_specs=(vmem, vmem, vmem),
        scratch_shapes=[pltpu.VMEM((parts, own_rows, LANES), jnp.float32), *scratch],
        compiler_params=params,
        name="first_image",
    )(start, others, wide, pattern)
    others = from_others(partial)
    group = lax.all_to_all(slots, ("sub", "blk"), 0, 0, tiled=True)
    second, image = pl.pallas_call(
        functools.partial(second_kernel, coupling.shape[0]),
        out_shape=(rowed(rows), rowed(rows)),
        in_specs=[vmem] * 5,
        out_specs=(vmem, vmem),
        scratch_shapes=[in_parts, *scratch],
        compiler_params=params,
        name="second_image",
    )(lines, partial, others, wide, pattern)
    others = from_others(second)
    known = pl.pallas_call(
        early_kernel,
        out_shape=rowed(SUBL * pl.cdiv(3 + parts, SUBL)),
        in_specs=[vmem, vmem, vmem, smem],
        out_specs=vmem,
        compiler_params=params,
        cost_estimate=long,
        name="known_sums",
    )(vector, image, lines, neighbours)
    sums, again = pl.pallas_call(
        pair_kernel,
        out_shape=(rowed(reps * subs, 1), rowed(rows)),
        in_specs=[vmem] * 5 + [smem] + [vmem] * 2,
        out_specs=(vmem, vmem),
        scratch_shapes=[in_parts],
        compiler_params=params,
        name="pair_sums",
    )(vector, image, known, lines, group, neighbours, second, others)
    sums = lax.all_to_all(sums, ("rep", "sub"), 0, 0, tiled=True)
    second, third, entries = pl.pallas_call(
        functools.partial(last_kernel, float(cells)),
        out_shape=(rowed(own_rows), rowed(own_rows), jax.ShapeDtypeStruct((1, 5), jnp.float32)),
        in_specs=[vmem] * 4,
        out_specs=(vmem, vmem, vmem),
        compiler_params=params,
        name="arnoldi_entries",
    )(start, image, again, sums)
    return second.reshape(start_vector.shape), third.reshape(start_vector.shape), entries.reshape(5)


def solution(mesh):
    return jax.shard_map(
        per_device,
        mesh=mesh,
        in_specs=(
            P("rep", "sub", "blk"),
            P("rep", "sub", "blk", None, None),
            P("rep", "sub", None, None),
            P("rep", "sub", "blk"),
            P("rep", "sub", None),
            P("rep", "sub", None, "blk"),
        ),
        out_specs=(P("rep", "sub", "blk"), P("rep", "sub", "blk"), P()),
        check_vma=False,
    )
```

```python
import functools

import jax
import jax.numpy as jnp
from jax import lax
from jax.experimental import pallas as pl
from jax.experimental.pallas import tpu as pltpu
from jax.sharding import PartitionSpec as P

BS = 64
LANES = 128
SUBL = 8
epsilon = 1e-06


def pieces(value):
    high = value.astype(jnp.bfloat16)
    rest = value - high.astype(jnp.float32)
    middle = rest.astype(jnp.bfloat16)
    low = (rest - middle.astype(jnp.float32)).astype(jnp.bfloat16)
    return high, middle, low


def lane_iota(shape):
    return lax.broadcasted_iota(jnp.int32, shape, len(shape) - 1)


def row_iota(shape):
    return lax.broadcasted_iota(jnp.int32, shape, 0)


def block_product(vector, blocks_ref, pattern_ref, first_slot, fold_ref, halves_ref):
    slots, block_rows, width = blocks_ref.shape
    half = block_rows // 2
    lower = lane_iota(vector.shape) < BS
    turned = pltpu.roll(vector, BS, 1)
    table = jnp.concatenate([jnp.where(lower, vector, turned), jnp.where(lower, turned, vector)], 0)
    table = jnp.concatenate(pieces(table), 0)
    place = row_iota((block_rows, block_rows))
    place = jnp.where(place < half, 2 * place, 2 * (place - half) + 1)
    picked = []
    for k in range(slots):
        names = pattern_ref[pl.ds(first_slot + k, 1), :]
        chosen = (place == names).astype(jnp.float32).astype(jnp.bfloat16)
        chosen = jnp.concatenate([chosen] * 3, 0)
        picked.append(
            lax.dot_general(chosen, table, (((0,), (0,)), ((), ())), preferred_element_type=jnp.float32)
        )
    ones = (row_iota((2 * LANES, LANES)) % LANES) // BS == lane_iota((2 * LANES, LANES)) % 2
    ones = ones.astype(jnp.float32).astype(jnp.bfloat16)
    pair = (lane_iota((block_rows, LANES)) % BS) // 2
    chunks = width // LANES
    for c in range(chunks):
        total = None
        for k in range(slots):
            term = blocks_ref[k, :, pl.ds(c * LANES, LANES)] * picked[k]
            total = term if total is None else total + term
        high = total.astype(jnp.bfloat16)
        here = pl.ds(c * block_rows, block_rows)
        halves_ref[here, 0:LANES] = high
        halves_ref[here, LANES : 2 * LANES] = (total - high.astype(jnp.float32)).astype(jnp.bfloat16)
    sums = lax.dot_general(halves_ref[...], ones, (((1,), (0,)), ((), ())), preferred_element_type=jnp.float32)
    result = sums[0:block_rows]
    for c in range(1, chunks):
        result = jnp.where(pair == c, sums[c * block_rows : (c + 1) * block_rows], result)
    fold_ref[...] = result
    even = fold_ref[pl.ds(0, half, stride=2), :]
    odd = fold_ref[pl.ds(1, half, stride=2), :]
    return jnp.where(lane_iota((half, LANES)) < BS, even, odd)


def take_trace(rows, places):
    count = rows.shape[0]
    low = jnp.broadcast_to(places % LANES, (count, LANES))
    picked = jnp.take_along_axis(rows, low, axis=1)
    return jnp.sum(jnp.where(row_iota((count, LANES)) == places // LANES, picked, 0.0), axis=0, keepdims=True)


def spread(values, places, count):
    aimed = jnp.where(row_iota((count, LANES)) == places // LANES, values, 0.0)
    high = aimed.astype(jnp.bfloat16).astype(jnp.float32)
    rest = aimed - high
    middle = rest.astype(jnp.bfloat16).astype(jnp.float32)
    stack = jnp.concatenate([high, middle, rest - middle], 0).astype(jnp.bfloat16)
    target = (row_iota((LANES, LANES)) == places % LANES).astype(jnp.float32).astype(jnp.bfloat16)
    landed = lax.dot_general(stack, target, (((1,), (1,)), ((), ())), preferred_element_type=jnp.float32)
    return landed[0:count] + landed[count : 2 * count] + landed[2 * count : 3 * count]


def lines_kernel(start_ref, map_ref, near_ref, coupling_ref, out_ref):
    places = map_ref[...]
    count = coupling_ref.shape[0]
    first_cell = lax.axis_index("blk") * start_ref.shape[0] * LANES
    lines = [take_trace(start_ref[...], places - first_cell), places.astype(jnp.float32)]
    lines += [coupling_ref[n : n + 1, :] for n in range(count)]
    near = near_ref[...].astype(jnp.float32)
    lines += [jnp.broadcast_to(near[:, n : n + 1], (1, LANES)) for n in range(count)]
    lines += [jnp.zeros((SUBL - len(lines), LANES), jnp.float32)]
    out_ref[...] = jnp.concatenate(lines, 0)


def widen_kernel(blocks_ref, out_ref):
    out_ref[...] = blocks_ref[...].astype(jnp.float32)


def first_kernel(start_ref, lines_ref, other_ref, blocks_ref, pattern_ref, out_ref, vector_ref, fold_ref, halves_ref):
    own_rows, rows = start_ref.shape[0], vector_ref.shape[0]
    blk, parts = lax.axis_index("blk"), lax.axis_size("blk")
    for step in range(parts):
        place = lax.rem(blk + step, parts)
        place = pl.ds(pl.multiple_of(place * own_rows, SUBL), own_rows)
        vector_ref[place, :] = other_ref[step - 1] if step else start_ref[...]
    partial = block_product(vector_ref[...], blocks_ref, pattern_ref, blk * blocks_ref.shape[0], fold_ref, halves_ref)
    for device in range(out_ref.shape[0]):
        out_ref[device, 0:rows, :] = partial
        out_ref[device, rows : rows + SUBL, :] = lines_ref[...]


def line(group_ref, device, i):
    first = group_ref.shape[1] - SUBL + i
    return group_ref[device, first : first + 1, :]


def landed(group_ref, sub_at, part, own_rows, count):
    parts = lax.axis_size("blk")
    traces = [line(group_ref, other * parts + part, 0) for other in range(lax.axis_size("sub"))]
    traces = jnp.concatenate(traces, 0)
    names = row_iota(traces.shape).astype(jnp.float32)
    device = sub_at * parts + part
    inflow = jnp.zeros((1, LANES), jnp.float32)
    for n in range(count):
        chosen = jnp.where(names == line(group_ref, device, 2 + count + n), traces, 0.0)
        inflow = inflow + line(group_ref, device, 2 + n) * jnp.sum(chosen, axis=0, keepdims=True)
    places = line(group_ref, device, 1).astype(jnp.int32) - part * own_rows * LANES
    return spread(inflow, places, own_rows), places


def summed(group_ref, sub_at, first, count):
    parts = lax.axis_size("blk")
    total = group_ref[sub_at * parts, first : first + count, :]
    for b in range(1, parts):
        total = total + group_ref[sub_at * parts + b, first : first + count, :]
    return total


def second_kernel(count, group_ref, blocks_ref, pattern_ref, out_ref, image_ref, fold_ref, halves_ref):
    rows = image_ref.shape[0]
    sub, blk, parts = lax.axis_index("sub"), lax.axis_index("blk"), lax.axis_size("blk")
    added = [landed(group_ref, sub, part, rows // parts, count)[0] for part in range(parts)]
    image = summed(group_ref, sub, 0, rows) + jnp.concatenate(added, 0)
    image_ref[...] = image
    out_ref[...] = block_product(image, blocks_ref, pattern_ref, blk * blocks_ref.shape[0], fold_ref, halves_ref)


def down(left, right):
    return jnp.sum(left * right, axis=0, keepdims=True)


def inflow_kernel(vector_ref, image_ref, group_ref, near_ref, out_ref, sums_ref):
    rows = image_ref.shape[0]
    count = near_ref.shape[1]
    sub, parts = lax.axis_index("sub"), lax.axis_size("blk")
    own_rows = rows // parts
    for part in range(parts):
        device = sub * parts + part
        inflow = jnp.zeros((1, LANES), jnp.float32)
        for n in range(count):
            source = near_ref[0, n]
            added, places = landed(group_ref, source, part, own_rows, count)
            trace = take_trace(summed(group_ref, source, part * own_rows, own_rows) + added, places)
            inflow = inflow + line(group_ref, device, 2 + n) * trace
        places = line(group_ref, device, 1).astype(jnp.int32) - part * own_rows * LANES
        out_ref[part * own_rows : (part + 1) * own_rows, :] = spread(inflow, places, own_rows)
    vector, image = vector_ref[...], image_ref[...]
    sums = [down(vector, vector), down(vector, image), down(image, image)]
    sums_ref[...] = jnp.concatenate([*sums, jnp.zeros((SUBL - len(sums), LANES), jnp.float32)], 0)


def pair_kernel(vector_ref, image_ref, sums_ref, inflow_ref, mine_ref, other_ref, out_ref, again_ref, part_ref):
    parts = part_ref.shape[0]
    for step in range(parts):
        part_ref[lax.rem(lax.axis_index("blk") + step, parts)] = other_ref[step - 1] if step else mine_ref[...]
    again = inflow_ref[...]
    for part in range(parts):
        again = again + part_ref[part]
    again_ref[...] = again
    sums = [down(vector_ref[...], again), down(image_ref[...], again), down(again, again)]
    sums = jnp.concatenate([sums_ref[0:3, :], *sums, sums_ref[6:SUBL, :]], 0)
    sums = jnp.sum(sums, axis=1, keepdims=True)
    sums = jnp.where(row_iota((SUBL, LANES)) == lane_iota((SUBL, LANES)), sums, 0.0)
    sums = jnp.sum(sums, axis=0, keepdims=True)
    for device in range(out_ref.shape[0]):
        out_ref[device] = sums


def last_kernel(
    cells, start_ref, image_ref, again_ref, sums_ref, second_ref, third_ref, entries_ref, hold_ref, line_ref, sems
):
    own_rows = start_ref.shape[0]
    own = pl.ds(pl.multiple_of(lax.axis_index("blk") * own_rows, SUBL), own_rows)
    vector, image = start_ref[...], image_ref[own, :]
    copies = [
        pltpu.make_async_copy(hold_ref.at[0], second_ref, sems.at[0]),
        pltpu.make_async_copy(hold_ref.at[1], third_ref, sems.at[1]),
        pltpu.make_async_copy(line_ref, entries_ref, sems.at[2]),
    ]
    sums = jnp.sum(sums_ref[...], axis=0) / cells

    def whole(i):
        return jnp.broadcast_to(sums[:, i : i + 1], (1, LANES))

    vv, vw, ww, vy, wy, yy = (whole(i) for i in range(6))
    norm_square = vv + epsilon
    inverse = 1.0 / norm_square
    h11 = vw * inverse
    skew = vy - h11 * vw
    first_square = jnp.maximum(ww - 2.0 * h11 * vw + h11 * h11 * vv, 0.0) * inverse + epsilon
    over_first = lax.rsqrt(first_square)
    h21 = first_square * over_first
    scale = lax.rsqrt(norm_square) * over_first
    hold_ref[0] = (image - h11 * vector) * scale
    copies[0].start()
    h12 = skew * inverse * over_first
    h22 = (wy - h11 * (ww + skew)) * scale * scale
    near = h11 + h22
    far = skew * inverse - h11 * h22
    second_square = yy + near * near * ww + far * far * vv + 2.0 * (near * far * vw - near * wy - far * vy)
    second_square = jnp.maximum(second_square, 0.0) * scale * scale + epsilon
    over_second = lax.rsqrt(second_square)
    h32 = second_square * over_second

    hold_ref[1] = (again_ref[own, :] - near * image - far * vector) * (scale * over_second)
    copies[1].start()
    lane = lane_iota((1, LANES))
    entries = h32
    for i, value in enumerate((h11, h21, h12, h22)):
        entries = jnp.where(lane == i, value, entries)
    line_ref[...] = entries[:, 0:5]
    copies[2].start()
    for copy in copies:
        copy.wait()


def per_device(start_vector, blocks, pattern, trace_map, neighbours, coupling):
    own_cells = start_vector.shape[2]
    own_rows = own_cells // LANES
    parts, subs, reps = lax.axis_size("blk"), lax.axis_size("sub"), lax.axis_size("rep")
    rows = own_rows * parts
    cells = own_cells * parts * subs * reps
    start = start_vector.reshape(own_rows, LANES)
    local_map = trace_map[0]
    blocks, pattern, neighbours, coupling = blocks[0, 0], pattern[0, 0], neighbours[0], coupling[0, 0]
    vmem = pl.BlockSpec(memory_space=pltpu.VMEM)
    params = pltpu.CompilerParams(vmem_limit_bytes=32 * 1024 * 1024)

    def rowed(*shape):
        return jax.ShapeDtypeStruct((*shape, LANES), jnp.float32)

    smem = pl.BlockSpec(memory_space=pltpu.SMEM)
    hbm = pl.BlockSpec(memory_space=pltpu.HBM)

    def from_others(value):
        got = [
            lax.ppermute(value[None], "blk", [((i + step) % parts, i) for i in range(parts)])
            for step in range(1, parts)
        ]
        return got[0] if parts == 2 else jnp.concatenate(got, 0)

    others = from_others(start)
    block_rows, width = blocks.shape[1:]
    scratch = [
        pltpu.VMEM((block_rows, LANES), jnp.float32),
        pltpu.VMEM((block_rows * width // LANES, 2 * LANES), jnp.bfloat16),
    ]
    lines = pl.pallas_call(
        lines_kernel,
        out_shape=rowed(SUBL),
        in_specs=[vmem] * 4,
        out_specs=vmem,
        compiler_params=params,
        cost_estimate=pl.CostEstimate(flops=1 << 32, bytes_accessed=1 << 20, transcendentals=0),
        name="group_lines",
    )(start, local_map, neighbours, coupling)
    wide = pl.pallas_call(
        widen_kernel,
        out_shape=jax.ShapeDtypeStruct(blocks.shape, jnp.float32),
        in_specs=[vmem],
        out_specs=vmem,
        compiler_params=params,
        cost_estimate=pl.CostEstimate(flops=1 << 32, bytes_accessed=3 << 20, transcendentals=0),
        name="wide_blocks",
    )(blocks)
    partial, vector = pl.pallas_call(
        first_kernel,
        out_shape=(rowed(subs * parts, rows + SUBL), rowed(rows)),
        in_specs=[vmem] * 5,
        out_specs=(vmem, vmem),
        scratch_shapes=scratch,
        compiler_params=params,
        name="first_image",
    )(start, lines, others, wide, pattern)
    group = lax.all_to_all(partial, ("sub", "blk"), 0, 0, tiled=True)
    second, image = pl.pallas_call(
        functools.partial(second_kernel, coupling.shape[0]),
        out_shape=(rowed(rows), rowed(rows)),
        in_specs=[vmem] * 3,
        out_specs=(vmem, vmem),
        scratch_shapes=scratch,
        compiler_params=params,
        name="second_image",
    )(group, wide, pattern)
    others = from_others(second)
    inflow, sums = pl.pallas_call(
        inflow_kernel,
        out_shape=(rowed(rows), rowed(SUBL)),
        in_specs=[vmem, vmem, vmem, smem],
        out_specs=(vmem, vmem),
        compiler_params=params,
        cost_estimate=pl.CostEstimate(flops=1 << 32, bytes_accessed=1 << 20, transcendentals=0),
        name="second_inflow",
    )(vector, image, group, neighbours)
    sums, again = pl.pallas_call(
        pair_kernel,
        out_shape=(rowed(reps * subs, 1), rowed(rows)),
        in_specs=[vmem] * 6,
        out_specs=(vmem, vmem),
        scratch_shapes=[pltpu.VMEM((parts, rows, LANES), jnp.float32)],
        compiler_params=params,
        name="pair_sums",
    )(vector, image, sums, inflow, second, others)
    sums = lax.all_to_all(sums, ("rep", "sub"), 0, 0, tiled=True)
    second, third, entries = pl.pallas_call(
        functools.partial(last_kernel, float(cells)),
        out_shape=(rowed(own_rows), rowed(own_rows), jax.ShapeDtypeStruct((1, 5), jnp.float32)),
        in_specs=[vmem] * 4,
        out_specs=(hbm, hbm, hbm),
        scratch_shapes=[
            pltpu.VMEM((2, own_rows, LANES), jnp.float32),
            pltpu.VMEM((1, 5), jnp.float32),
            pltpu.SemaphoreType.DMA((3,)),
        ],
        compiler_params=params,
        name="arnoldi_entries",
    )(start, image, again, sums)
    return second.reshape(start_vector.shape), third.reshape(start_vector.shape), entries.reshape(5)


def solution(mesh):
    return jax.shard_map(
        per_device,
        mesh=mesh,
        in_specs=(
            P("rep", "sub", "blk"),
            P("rep", "sub", "blk", None, None),
            P("rep", "sub", None, None),
            P("rep", "sub", "blk"),
            P("rep", "sub", None),
            P("rep", "sub", None, "blk"),
        ),
        out_specs=(P("rep", "sub", "blk"), P("rep", "sub", "blk"), P()),
        check_vma=False,
    )
```

```python
import functools

import jax
import jax.numpy as jnp
from jax import lax
from jax.experimental import pallas as pl
from jax.experimental.pallas import tpu as pltpu
from jax.sharding import PartitionSpec as P

BS = 64
LANES = 128
SUBL = 8
epsilon = 1e-06


def pieces(value):
    high = value.astype(jnp.bfloat16)
    rest = value - high.astype(jnp.float32)
    middle = rest.astype(jnp.bfloat16)
    low = (rest - middle.astype(jnp.float32)).astype(jnp.bfloat16)
    return high, middle, low


def lane_iota(shape):
    return lax.broadcasted_iota(jnp.int32, shape, len(shape) - 1)


def row_iota(shape):
    return lax.broadcasted_iota(jnp.int32, shape, 0)


def choices(pattern_ref, first_slot, slots):
    block_rows = pattern_ref.shape[1]
    half = block_rows // 2
    place = row_iota((block_rows, block_rows))
    place = jnp.where(place < half, 2 * place, 2 * (place - half) + 1)
    thrice = (block_rows, 3 * block_rows)
    copies = (lane_iota(thrice) % block_rows == row_iota(thrice)).astype(jnp.float32).astype(jnp.bfloat16)
    rows = []
    for k in range(slots):
        chosen = place == pattern_ref[pl.ds(first_slot + k, 1), :]
        chosen = chosen.astype(jnp.float32).astype(jnp.bfloat16)
        rows.append(
            lax.dot_general(chosen, copies, (((0,), (0,)), ((), ())), preferred_element_type=jnp.float32)
        )
    return jnp.concatenate(rows, 0).astype(jnp.bfloat16)


def block_product(vector, blocks_ref, choices_ref, fold_ref, halves_ref):
    slots, block_rows, width = blocks_ref.shape
    half = block_rows // 2
    lower = lane_iota(vector.shape) < BS
    turned = pltpu.roll(vector, BS, 1)
    table = jnp.concatenate([jnp.where(lower, vector, turned), jnp.where(lower, turned, vector)], 0)
    table = jnp.concatenate(pieces(table), 0)
    picked = lax.dot_general(
        choices_ref[...], table, (((1,), (0,)), ((), ())), preferred_element_type=jnp.float32
    )
    ones = (row_iota((2 * LANES, LANES)) % LANES) // BS == lane_iota((2 * LANES, LANES)) % 2
    ones = ones.astype(jnp.float32).astype(jnp.bfloat16)
    pair = (lane_iota((block_rows, LANES)) % BS) // 2
    chunks = width // LANES
    together = chunks // 4
    result = jnp.zeros((block_rows, LANES), jnp.float32)
    for first in range(0, chunks, together):
        for c in range(first, first + together):
            total = None
            for k in range(slots):
                term = blocks_ref[k, :, pl.ds(c * LANES, LANES)] * picked[k * block_rows : (k + 1) * block_rows]
                total = term if total is None else total + term
            high = total.astype(jnp.bfloat16)
            here = pl.ds(c * block_rows, block_rows)
            halves_ref[here, 0:LANES] = high
            halves_ref[here, LANES : 2 * LANES] = (total - high.astype(jnp.float32)).astype(jnp.bfloat16)
        sums = lax.dot_general(
            halves_ref[pl.ds(first * block_rows, together * block_rows), :],
            ones,
            (((1,), (0,)), ((), ())),
            preferred_element_type=jnp.float32,
        )
        for i in range(together):
            result = jnp.where(pair == first + i, sums[i * block_rows : (i + 1) * block_rows], result)
    fold_ref[...] = result
    even = fold_ref[pl.ds(0, half, stride=2), :]
    odd = fold_ref[pl.ds(1, half, stride=2), :]
    return jnp.where(lane_iota((half, LANES)) < BS, even, odd)


def take_trace(rows, places):
    count = rows.shape[0]
    low = jnp.broadcast_to(places % LANES, (count, LANES))
    picked = jnp.take_along_axis(rows, low, axis=1)
    return jnp.sum(jnp.where(row_iota((count, LANES)) == places // LANES, picked, 0.0), axis=0, keepdims=True)


def spread(values, places, count):
    aimed = jnp.where(row_iota((count, LANES)) == places // LANES, values, 0.0)
    high = aimed.astype(jnp.bfloat16).astype(jnp.float32)
    rest = aimed - high
    middle = rest.astype(jnp.bfloat16).astype(jnp.float32)
    stack = jnp.concatenate([high, middle, rest - middle], 0).astype(jnp.bfloat16)
    target = (row_iota((LANES, LANES)) == places % LANES).astype(jnp.float32).astype(jnp.bfloat16)
    landed = lax.dot_general(stack, target, (((1,), (1,)), ((), ())), preferred_element_type=jnp.float32)
    return landed[0:count] + landed[count : 2 * count] + landed[2 * count : 3 * count]


def lines_kernel(start_ref, map_ref, near_ref, coupling_ref, pattern_ref, out_ref, choices_ref):
    places = map_ref[...]
    count = coupling_ref.shape[0]
    first_cell = lax.axis_index("blk") * start_ref.shape[0] * LANES
    lines = [take_trace(start_ref[...], places - first_cell), places.astype(jnp.float32)]
    lines += [coupling_ref[n : n + 1, :] for n in range(count)]
    near = near_ref[...].astype(jnp.float32)
    lines += [jnp.broadcast_to(near[:, n : n + 1], (1, LANES)) for n in range(count)]
    lines += [jnp.zeros((SUBL - len(lines), LANES), jnp.float32)]
    out_ref[...] = jnp.concatenate(lines, 0)
    slots = choices_ref.shape[0] // pattern_ref.shape[1]
    choices_ref[...] = choices(pattern_ref, lax.axis_index("blk") * slots, slots)


def widen_kernel(blocks_ref, out_ref):
    out_ref[...] = blocks_ref[...].astype(jnp.float32)


def first_kernel(start_ref, lines_ref, other_ref, blocks_ref, choices_ref, out_ref, vector_ref, fold_ref, halves_ref):
    own_rows, rows = start_ref.shape[0], vector_ref.shape[0]
    blk, parts = lax.axis_index("blk"), lax.axis_size("blk")
    for step in range(parts):
        place = lax.rem(blk + step, parts)
        place = pl.ds(pl.multiple_of(place * own_rows, SUBL), own_rows)
        vector_ref[place, :] = other_ref[step - 1] if step else start_ref[...]
    partial = block_product(vector_ref[...], blocks_ref, choices_ref, fold_ref, halves_ref)
    for device in range(out_ref.shape[0]):
        out_ref[device, 0:rows, :] = partial
        out_ref[device, rows : rows + SUBL, :] = lines_ref[...]


def line(group_ref, device, i):
    first = group_ref.shape[1] - SUBL + i
    return group_ref[device, first : first + 1, :]


def landed(group_ref, sub_at, part, own_rows, count):
    parts = lax.axis_size("blk")
    traces = [line(group_ref, other * parts + part, 0) for other in range(lax.axis_size("sub"))]
    traces = jnp.concatenate(traces, 0)
    names = row_iota(traces.shape).astype(jnp.float32)
    device = sub_at * parts + part
    inflow = jnp.zeros((1, LANES), jnp.float32)
    for n in range(count):
        chosen = jnp.where(names == line(group_ref, device, 2 + count + n), traces, 0.0)
        inflow = inflow + line(group_ref, device, 2 + n) * jnp.sum(chosen, axis=0, keepdims=True)
    places = line(group_ref, device, 1).astype(jnp.int32) - part * own_rows * LANES
    return spread(inflow, places, own_rows), places


def summed(group_ref, sub_at, first, count):
    parts = lax.axis_size("blk")
    total = group_ref[sub_at * parts, first : first + count, :]
    for b in range(1, parts):
        total = total + group_ref[sub_at * parts + b, first : first + count, :]
    return total


def second_kernel(count, group_ref, blocks_ref, choices_ref, out_ref, image_ref, fold_ref, halves_ref):
    rows = image_ref.shape[0]
    sub, parts = lax.axis_index("sub"), lax.axis_size("blk")
    added = [landed(group_ref, sub, part, rows // parts, count)[0] for part in range(parts)]
    image = summed(group_ref, sub, 0, rows) + jnp.concatenate(added, 0)
    image_ref[...] = image
    out_ref[...] = block_product(image, blocks_ref, choices_ref, fold_ref, halves_ref)


def down(left, right):
    return jnp.sum(left * right, axis=0, keepdims=True)


def inflow_kernel(vector_ref, image_ref, group_ref, near_ref, out_ref, sums_ref):
    rows = image_ref.shape[0]
    count = near_ref.shape[1]
    sub, parts = lax.axis_index("sub"), lax.axis_size("blk")
    own_rows = rows // parts
    for part in range(parts):
        device = sub * parts + part
        inflow = jnp.zeros((1, LANES), jnp.float32)
        for n in range(count):
            source = near_ref[0, n]
            added, places = landed(group_ref, source, part, own_rows, count)
            trace = take_trace(summed(group_ref, source, part * own_rows, own_rows) + added, places)
            inflow = inflow + line(group_ref, device, 2 + n) * trace
        places = line(group_ref, device, 1).astype(jnp.int32) - part * own_rows * LANES
        out_ref[part * own_rows : (part + 1) * own_rows, :] = spread(inflow, places, own_rows)
    vector, image = vector_ref[...], image_ref[...]
    sums = [down(vector, vector), down(vector, image), down(image, image)]
    sums_ref[...] = jnp.concatenate([*sums, jnp.zeros((SUBL - len(sums), LANES), jnp.float32)], 0)


def pair_kernel(vector_ref, image_ref, sums_ref, inflow_ref, mine_ref, other_ref, out_ref, again_ref, part_ref):
    parts = part_ref.shape[0]
    for step in range(parts):
        part_ref[lax.rem(lax.axis_index("blk") + step, parts)] = other_ref[step - 1] if step else mine_ref[...]
    again = inflow_ref[...]
    for part in range(parts):
        again = again + part_ref[part]
    again_ref[...] = again
    sums = [down(vector_ref[...], again), down(image_ref[...], again), down(again, again)]
    sums = jnp.concatenate([sums_ref[0:3, :], *sums, sums_ref[6:SUBL, :]], 0)
    sums = jnp.sum(sums, axis=1, keepdims=True)
    sums = jnp.where(row_iota((SUBL, LANES)) == lane_iota((SUBL, LANES)), sums, 0.0)
    sums = jnp.sum(sums, axis=0, keepdims=True)
    for device in range(out_ref.shape[0]):
        out_ref[device] = sums


def last_kernel(cells, start_ref, image_ref, again_ref, sums_ref, second_ref, third_ref, entries_ref):
    sums = jnp.sum(sums_ref[...], axis=0) / cells

    def whole(i):
        return jnp.broadcast_to(sums[:, i : i + 1], (1, LANES))

    vv, vw, ww, vy, wy, yy = (whole(i) for i in range(6))
    norm_square = vv + epsilon
    inverse = 1.0 / norm_square
    h11 = vw * inverse
    skew = vy - h11 * vw
    first_square = jnp.maximum(ww - 2.0 * h11 * vw + h11 * h11 * vv, 0.0) * inverse + epsilon
    over_first = lax.rsqrt(first_square)
    h21 = first_square * over_first
    scale = lax.rsqrt(norm_square) * over_first
    h12 = skew * inverse * over_first
    h22 = (wy - h11 * (ww + skew)) * scale * scale
    near = h11 + h22
    far = skew * inverse - h11 * h22
    second_square = yy + near * near * ww + far * far * vv + 2.0 * (near * far * vw - near * wy - far * vy)
    second_square = jnp.maximum(second_square, 0.0) * scale * scale + epsilon
    over_second = lax.rsqrt(second_square)
    h32 = second_square * over_second

    own_rows = start_ref.shape[0]
    own = pl.ds(pl.multiple_of(lax.axis_index("blk") * own_rows, SUBL), own_rows)
    vector, image = start_ref[...], image_ref[own, :]
    second_ref[...] = (image - h11 * vector) * scale
    third_ref[...] = (again_ref[own, :] - near * image - far * vector) * (scale * over_second)
    lane = lane_iota((1, LANES))
    entries = h32
    for i, value in enumerate((h11, h21, h12, h22)):
        entries = jnp.where(lane == i, value, entries)
    entries_ref[...] = entries[:, 0:5]


def per_device(start_vector, blocks, pattern, trace_map, neighbours, coupling):
    own_cells = start_vector.shape[2]
    own_rows = own_cells // LANES
    parts, subs, reps = lax.axis_size("blk"), lax.axis_size("sub"), lax.axis_size("rep")
    rows = own_rows * parts
    cells = own_cells * parts * subs * reps
    start = start_vector.reshape(own_rows, LANES)
    local_map = trace_map[0]
    blocks, pattern, neighbours, coupling = blocks[0, 0], pattern[0, 0], neighbours[0], coupling[0, 0]
    vmem = pl.BlockSpec(memory_space=pltpu.VMEM)
    params = pltpu.CompilerParams(vmem_limit_bytes=32 * 1024 * 1024)

    def rowed(*shape):
        return jax.ShapeDtypeStruct((*shape, LANES), jnp.float32)

    smem = pl.BlockSpec(memory_space=pltpu.SMEM)

    def from_others(value):
        got = [
            lax.ppermute(value[None], "blk", [((i + step) % parts, i) for i in range(parts)])
            for step in range(1, parts)
        ]
        return got[0] if parts == 2 else jnp.concatenate(got, 0)

    others = from_others(start)
    slots, block_rows, width = blocks.shape
    scratch = [
        pltpu.VMEM((block_rows, LANES), jnp.float32),
        pltpu.VMEM((block_rows * width // LANES, 2 * LANES), jnp.bfloat16),
    ]
    lines, chosen = pl.pallas_call(
        lines_kernel,
        out_shape=(rowed(SUBL), jax.ShapeDtypeStruct((slots * block_rows, 3 * block_rows), jnp.bfloat16)),
        in_specs=[vmem] * 5,
        out_specs=(vmem, vmem),
        compiler_params=params,
        cost_estimate=pl.CostEstimate(flops=1 << 32, bytes_accessed=1 << 20, transcendentals=0),
        name="group_lines",
    )(start, local_map, neighbours, coupling, pattern)
    wide = pl.pallas_call(
        widen_kernel,
        out_shape=jax.ShapeDtypeStruct(blocks.shape, jnp.float32),
        in_specs=[vmem],
        out_specs=vmem,
        compiler_params=params,
        cost_estimate=pl.CostEstimate(flops=1 << 32, bytes_accessed=3 << 20, transcendentals=0),
        name="wide_blocks",
    )(blocks)
    partial, vector = pl.pallas_call(
        first_kernel,
        out_shape=(rowed(subs * parts, rows + SUBL), rowed(rows)),
        in_specs=[vmem] * 5,
        out_specs=(vmem, vmem),
        scratch_shapes=scratch,
        compiler_params=params,
        name="first_image",
    )(start, lines, others, wide, chosen)
    group = lax.all_to_all(partial, ("sub", "blk"), 0, 0, tiled=True)
    second, image = pl.pallas_call(
        functools.partial(second_kernel, coupling.shape[0]),
        out_shape=(rowed(rows), rowed(rows)),
        in_specs=[vmem] * 3,
        out_specs=(vmem, vmem),
        scratch_shapes=scratch,
        compiler_params=params,
        name="second_image",
    )(group, wide, chosen)
    others = from_others(second)
    inflow, sums = pl.pallas_call(
        inflow_kernel,
        out_shape=(rowed(rows), rowed(SUBL)),
        in_specs=[vmem, vmem, vmem, smem],
        out_specs=(vmem, vmem),
        compiler_params=params,
        cost_estimate=pl.CostEstimate(flops=1 << 32, bytes_accessed=1 << 20, transcendentals=0),
        name="second_inflow",
    )(vector, image, group, neighbours)
    sums, again = pl.pallas_call(
        pair_kernel,
        out_shape=(rowed(reps * subs, 1), rowed(rows)),
        in_specs=[vmem] * 6,
        out_specs=(vmem, vmem),
        scratch_shapes=[pltpu.VMEM((parts, rows, LANES), jnp.float32)],
        compiler_params=params,
        name="pair_sums",
    )(vector, image, sums, inflow, second, others)
    sums = lax.all_to_all(sums, ("rep", "sub"), 0, 0, tiled=True)
    second, third, entries = pl.pallas_call(
        functools.partial(last_kernel, float(cells)),
        out_shape=(rowed(own_rows), rowed(own_rows), jax.ShapeDtypeStruct((1, 5), jnp.float32)),
        in_specs=[vmem] * 4,
        out_specs=(vmem, vmem, vmem),
        compiler_params=params,
        name="arnoldi_entries",
    )(start, image, again, sums)
    return second.reshape(start_vector.shape), third.reshape(start_vector.shape), entries.reshape(5)


def solution(mesh):
    return jax.shard_map(
        per_device,
        mesh=mesh,
        in_specs=(
            P("rep", "sub", "blk"),
            P("rep", "sub", "blk", None, None),
            P("rep", "sub", None, None),
            P("rep", "sub", "blk"),
            P("rep", "sub", None),
            P("rep", "sub", None, "blk"),
        ),
        out_specs=(P("rep", "sub", "blk"), P("rep", "sub", "blk"), P()),
        check_vma=False,
    )
```

```python
import functools

import jax
import jax.numpy as jnp
from jax import lax
from jax.experimental import pallas as pl
from jax.experimental.pallas import tpu as pltpu
from jax.sharding import PartitionSpec as P

BS = 64
LANES = 128
SUBL = 8
epsilon = 1e-06


def pieces(value):
    high = value.astype(jnp.bfloat16)
    rest = value - high.astype(jnp.float32)
    middle = rest.astype(jnp.bfloat16)
    low = (rest - middle.astype(jnp.float32)).astype(jnp.bfloat16)
    return high, middle, low


def lane_iota(shape):
    return lax.broadcasted_iota(jnp.int32, shape, len(shape) - 1)


def row_iota(shape):
    return lax.broadcasted_iota(jnp.int32, shape, 0)


def choices(pattern_ref, first_slot, slots):
    block_rows = pattern_ref.shape[1]
    half = block_rows // 2
    place = row_iota((block_rows, block_rows))
    place = jnp.where(place < half, 2 * place, 2 * (place - half) + 1)
    thrice = (block_rows, 3 * block_rows)
    copies = (lane_iota(thrice) % block_rows == row_iota(thrice)).astype(jnp.float32).astype(jnp.bfloat16)
    rows = []
    for k in range(slots):
        chosen = place == pattern_ref[pl.ds(first_slot + k, 1), :]
        chosen = chosen.astype(jnp.float32).astype(jnp.bfloat16)
        rows.append(
            lax.dot_general(chosen, copies, (((0,), (0,)), ((), ())), preferred_element_type=jnp.float32)
        )
    return jnp.concatenate(rows, 0).astype(jnp.bfloat16)


def block_product(vector, blocks_ref, choices_ref, fold_ref, halves_ref):
    slots, block_rows, width = blocks_ref.shape
    half = block_rows // 2
    lower = lane_iota(vector.shape) < BS
    turned = pltpu.roll(vector, BS, 1)
    table = jnp.concatenate([jnp.where(lower, vector, turned), jnp.where(lower, turned, vector)], 0)
    table = jnp.concatenate(pieces(table), 0)
    picked = lax.dot_general(
        choices_ref[...], table, (((1,), (0,)), ((), ())), preferred_element_type=jnp.float32
    )
    ones = (row_iota((2 * LANES, LANES)) % LANES) // BS == lane_iota((2 * LANES, LANES)) % 2
    ones = ones.astype(jnp.float32).astype(jnp.bfloat16)
    pair = (lane_iota((block_rows, LANES)) % BS) // 2
    chunks = width // LANES
    together = chunks // 4
    result = jnp.zeros((block_rows, LANES), jnp.float32)
    for first in range(0, chunks, together):
        for c in range(first, first + together):
            total = None
            for k in range(slots):
                term = blocks_ref[k, :, pl.ds(c * LANES, LANES)] * picked[k * block_rows : (k + 1) * block_rows]
                total = term if total is None else total + term
            high = total.astype(jnp.bfloat16)
            here = pl.ds(c * block_rows, block_rows)
            halves_ref[here, 0:LANES] = high
            halves_ref[here, LANES : 2 * LANES] = (total - high.astype(jnp.float32)).astype(jnp.bfloat16)
        sums = lax.dot_general(
            halves_ref[pl.ds(first * block_rows, together * block_rows), :],
            ones,
            (((1,), (0,)), ((), ())),
            preferred_element_type=jnp.float32,
        )
        for i in range(together):
            result = jnp.where(pair == first + i, sums[i * block_rows : (i + 1) * block_rows], result)
    fold_ref[...] = result
    even = fold_ref[pl.ds(0, half, stride=2), :]
    odd = fold_ref[pl.ds(1, half, stride=2), :]
    return jnp.where(lane_iota((half, LANES)) < BS, even, odd)


def take_trace(rows, places):
    count = rows.shape[0]
    low = jnp.broadcast_to(places % LANES, (count, LANES))
    picked = jnp.take_along_axis(rows, low, axis=1)
    return jnp.sum(jnp.where(row_iota((count, LANES)) == places // LANES, picked, 0.0), axis=0, keepdims=True)


def spread(values, places, count):
    aimed = jnp.where(row_iota((count, LANES)) == places // LANES, values, 0.0)
    high = aimed.astype(jnp.bfloat16).astype(jnp.float32)
    rest = aimed - high
    middle = rest.astype(jnp.bfloat16).astype(jnp.float32)
    stack = jnp.concatenate([high, middle, rest - middle], 0).astype(jnp.bfloat16)
    target = (row_iota((LANES, LANES)) == places % LANES).astype(jnp.float32).astype(jnp.bfloat16)
    landed = lax.dot_general(stack, target, (((1,), (1,)), ((), ())), preferred_element_type=jnp.float32)
    return landed[0:count] + landed[count : 2 * count] + landed[2 * count : 3 * count]


def lines_kernel(start_ref, map_ref, near_ref, coupling_ref, pattern_ref, out_ref, choices_ref):
    places = map_ref[...]
    count = coupling_ref.shape[0]
    first_cell = lax.axis_index("blk") * start_ref.shape[0] * LANES
    lines = [take_trace(start_ref[...], places - first_cell), places.astype(jnp.float32)]
    lines += [coupling_ref[n : n + 1, :] for n in range(count)]
    near = near_ref[...].astype(jnp.float32)
    lines += [jnp.broadcast_to(near[:, n : n + 1], (1, LANES)) for n in range(count)]
    lines += [jnp.zeros((SUBL - len(lines), LANES), jnp.float32)]
    out_ref[...] = jnp.concatenate(lines, 0)
    slots = choices_ref.shape[0] // pattern_ref.shape[1]
    choices_ref[...] = choices(pattern_ref, lax.axis_index("blk") * slots, slots)


def widen_kernel(blocks_ref, out_ref):
    out_ref[...] = blocks_ref[...].astype(jnp.float32)


def first_kernel(start_ref, lines_ref, other_ref, blocks_ref, choices_ref, out_ref, vector_ref, fold_ref, halves_ref):
    own_rows, rows = start_ref.shape[0], vector_ref.shape[0]
    blk, parts = lax.axis_index("blk"), lax.axis_size("blk")
    for step in range(parts):
        place = lax.rem(blk + step, parts)
        place = pl.ds(pl.multiple_of(place * own_rows, SUBL), own_rows)
        vector_ref[place, :] = other_ref[step - 1] if step else start_ref[...]
    partial = block_product(vector_ref[...], blocks_ref, choices_ref, fold_ref, halves_ref)
    for device in range(out_ref.shape[0]):
        out_ref[device, 0:rows, :] = partial
        out_ref[device, rows : rows + SUBL, :] = lines_ref[...]


def member(sub_at, part):
    return part * lax.axis_size("sub") + sub_at


def line(group_ref, device, i):
    first = group_ref.shape[1] - SUBL + i
    return group_ref[device, first : first + 1, :]


def landed(group_ref, sub_at, part, own_rows, count):
    traces = [line(group_ref, member(other, part), 0) for other in range(lax.axis_size("sub"))]
    traces = jnp.concatenate(traces, 0)
    names = row_iota(traces.shape).astype(jnp.float32)
    device = member(sub_at, part)
    inflow = jnp.zeros((1, LANES), jnp.float32)
    for n in range(count):
        chosen = jnp.where(names == line(group_ref, device, 2 + count + n), traces, 0.0)
        inflow = inflow + line(group_ref, device, 2 + n) * jnp.sum(chosen, axis=0, keepdims=True)
    places = line(group_ref, device, 1).astype(jnp.int32) - part * own_rows * LANES
    return spread(inflow, places, own_rows), places


def summed(group_ref, sub_at, first, count):
    parts = lax.axis_size("blk")
    total = group_ref[member(sub_at, 0), first : first + count, :]
    for b in range(1, parts):
        total = total + group_ref[member(sub_at, b), first : first + count, :]
    return total


def second_kernel(count, group_ref, blocks_ref, choices_ref, out_ref, image_ref, fold_ref, halves_ref):
    rows = image_ref.shape[0]
    sub, parts = lax.axis_index("sub"), lax.axis_size("blk")
    added = [landed(group_ref, sub, part, rows // parts, count)[0] for part in range(parts)]
    image = summed(group_ref, sub, 0, rows) + jnp.concatenate(added, 0)
    image_ref[...] = image
    out_ref[...] = block_product(image, blocks_ref, choices_ref, fold_ref, halves_ref)


def down(left, right):
    return jnp.sum(left * right, axis=0, keepdims=True)


def inflow_kernel(vector_ref, image_ref, group_ref, near_ref, out_ref, sums_ref):
    rows = image_ref.shape[0]
    count = near_ref.shape[1]
    sub, parts = lax.axis_index("sub"), lax.axis_size("blk")
    own_rows = rows // parts
    for part in range(parts):
        device = member(sub, part)
        inflow = jnp.zeros((1, LANES), jnp.float32)
        for n in range(count):
            source = near_ref[0, n]
            added, places = landed(group_ref, source, part, own_rows, count)
            trace = take_trace(summed(group_ref, source, part * own_rows, own_rows) + added, places)
            inflow = inflow + line(group_ref, device, 2 + n) * trace
        places = line(group_ref, device, 1).astype(jnp.int32) - part * own_rows * LANES
        out_ref[part * own_rows : (part + 1) * own_rows, :] = spread(inflow, places, own_rows)
    vector, image = vector_ref[...], image_ref[...]
    sums = [down(vector, vector), down(vector, image), down(image, image)]
    sums_ref[...] = jnp.concatenate([*sums, jnp.zeros((SUBL - len(sums), LANES), jnp.float32)], 0)


def pair_kernel(vector_ref, image_ref, sums_ref, inflow_ref, mine_ref, other_ref, out_ref, again_ref, part_ref):
    parts = part_ref.shape[0]
    for step in range(parts):
        part_ref[lax.rem(lax.axis_index("blk") + step, parts)] = other_ref[step - 1] if step else mine_ref[...]
    again = inflow_ref[...]
    for part in range(parts):
        again = again + part_ref[part]
    again_ref[...] = again
    sums = [down(vector_ref[...], again), down(image_ref[...], again), down(again, again)]
    sums = jnp.concatenate([sums_ref[0:3, :], *sums, sums_ref[6:SUBL, :]], 0)
    sums = jnp.sum(sums, axis=1, keepdims=True)
    sums = jnp.where(row_iota((SUBL, LANES)) == lane_iota((SUBL, LANES)), sums, 0.0)
    sums = jnp.sum(sums, axis=0, keepdims=True)
    for device in range(out_ref.shape[0]):
        out_ref[device] = sums


def last_kernel(cells, start_ref, image_ref, again_ref, sums_ref, second_ref, third_ref, entries_ref):
    sums = jnp.sum(sums_ref[...], axis=0) / cells

    def whole(i):
        return jnp.broadcast_to(sums[:, i : i + 1], (1, LANES))

    vv, vw, ww, vy, wy, yy = (whole(i) for i in range(6))
    norm_square = vv + epsilon
    inverse = 1.0 / norm_square
    h11 = vw * inverse
    skew = vy - h11 * vw
    first_square = jnp.maximum(ww - 2.0 * h11 * vw + h11 * h11 * vv, 0.0) * inverse + epsilon
    over_first = lax.rsqrt(first_square)
    h21 = first_square * over_first
    scale = lax.rsqrt(norm_square) * over_first
    h12 = skew * inverse * over_first
    h22 = (wy - h11 * (ww + skew)) * scale * scale
    near = h11 + h22
    far = skew * inverse - h11 * h22
    second_square = yy + near * near * ww + far * far * vv + 2.0 * (near * far * vw - near * wy - far * vy)
    second_square = jnp.maximum(second_square, 0.0) * scale * scale + epsilon
    over_second = lax.rsqrt(second_square)
    h32 = second_square * over_second

    own_rows = start_ref.shape[0]
    own = pl.ds(pl.multiple_of(lax.axis_index("blk") * own_rows, SUBL), own_rows)
    vector, image = start_ref[...], image_ref[own, :]
    second_ref[...] = (image - h11 * vector) * scale
    third_ref[...] = (again_ref[own, :] - near * image - far * vector) * (scale * over_second)
    lane = lane_iota((1, LANES))
    entries = h32
    for i, value in enumerate((h11, h21, h12, h22)):
        entries = jnp.where(lane == i, value, entries)
    entries_ref[...] = entries[:, 0:5]


def per_device(start_vector, blocks, pattern, trace_map, neighbours, coupling):
    own_cells = start_vector.shape[2]
    own_rows = own_cells // LANES
    parts, subs, reps = lax.axis_size("blk"), lax.axis_size("sub"), lax.axis_size("rep")
    rows = own_rows * parts
    cells = own_cells * parts * subs * reps
    start = start_vector.reshape(own_rows, LANES)
    local_map = trace_map[0]
    blocks, pattern, neighbours, coupling = blocks[0, 0], pattern[0, 0], neighbours[0], coupling[0, 0]
    vmem = pl.BlockSpec(memory_space=pltpu.VMEM)
    params = pltpu.CompilerParams(vmem_limit_bytes=32 * 1024 * 1024)

    def rowed(*shape):
        return jax.ShapeDtypeStruct((*shape, LANES), jnp.float32)

    smem = pl.BlockSpec(memory_space=pltpu.SMEM)

    def from_others(value):
        got = [
            lax.ppermute(value[None], "blk", [((i + step) % parts, i) for i in range(parts)])
            for step in range(1, parts)
        ]
        return got[0] if parts == 2 else jnp.concatenate(got, 0)

    others = from_others(start)
    slots, block_rows, width = blocks.shape
    scratch = [
        pltpu.VMEM((block_rows, LANES), jnp.float32),
        pltpu.VMEM((block_rows * width // LANES, 2 * LANES), jnp.bfloat16),
    ]
    lines, chosen = pl.pallas_call(
        lines_kernel,
        out_shape=(rowed(SUBL), jax.ShapeDtypeStruct((slots * block_rows, 3 * block_rows), jnp.bfloat16)),
        in_specs=[vmem] * 5,
        out_specs=(vmem, vmem),
        compiler_params=params,
        cost_estimate=pl.CostEstimate(flops=1 << 32, bytes_accessed=1 << 20, transcendentals=0),
        name="group_lines",
    )(start, local_map, neighbours, coupling, pattern)
    wide = pl.pallas_call(
        widen_kernel,
        out_shape=jax.ShapeDtypeStruct(blocks.shape, jnp.float32),
        in_specs=[vmem],
        out_specs=vmem,
        compiler_params=params,
        cost_estimate=pl.CostEstimate(flops=1 << 32, bytes_accessed=3 << 20, transcendentals=0),
        name="wide_blocks",
    )(blocks)
    partial, vector = pl.pallas_call(
        first_kernel,
        out_shape=(rowed(subs * parts, rows + SUBL), rowed(rows)),
        in_specs=[vmem] * 5,
        out_specs=(vmem, vmem),
        scratch_shapes=scratch,
        compiler_params=params,
        name="first_image",
    )(start, lines, others, wide, chosen)
    group = lax.all_to_all(partial, ("blk", "sub"), 0, 0, tiled=True)
    second, image = pl.pallas_call(
        functools.partial(second_kernel, coupling.shape[0]),
        out_shape=(rowed(rows), rowed(rows)),
        in_specs=[vmem] * 3,
        out_specs=(vmem, vmem),
        scratch_shapes=scratch,
        compiler_params=params,
        name="second_image",
    )(group, wide, chosen)
    others = from_others(second)
    inflow, sums = pl.pallas_call(
        inflow_kernel,
        out_shape=(rowed(rows), rowed(SUBL)),
        in_specs=[vmem, vmem, vmem, smem],
        out_specs=(vmem, vmem),
        compiler_params=params,
        cost_estimate=pl.CostEstimate(flops=1 << 32, bytes_accessed=1 << 20, transcendentals=0),
        name="second_inflow",
    )(vector, image, group, neighbours)
    sums, again = pl.pallas_call(
        pair_kernel,
        out_shape=(rowed(reps * subs, 1), rowed(rows)),
        in_specs=[vmem] * 6,
        out_specs=(vmem, vmem),
        scratch_shapes=[pltpu.VMEM((parts, rows, LANES), jnp.float32)],
        compiler_params=params,
        name="pair_sums",
    )(vector, image, sums, inflow, second, others)
    sums = lax.all_to_all(sums, ("sub", "rep"), 0, 0, tiled=True)
    second, third, entries = pl.pallas_call(
        functools.partial(last_kernel, float(cells)),
        out_shape=(rowed(own_rows), rowed(own_rows), jax.ShapeDtypeStruct((1, 5), jnp.float32)),
        in_specs=[vmem] * 4,
        out_specs=(vmem, vmem, vmem),
        compiler_params=params,
        name="arnoldi_entries",
    )(start, image, again, sums)
    return second.reshape(start_vector.shape), third.reshape(start_vector.shape), entries.reshape(5)


def solution(mesh):
    return jax.shard_map(
        per_device,
        mesh=mesh,
        in_specs=(
            P("rep", "sub", "blk"),
            P("rep", "sub", "blk", None, None),
            P("rep", "sub", None, None),
            P("rep", "sub", "blk"),
            P("rep", "sub", None),
            P("rep", "sub", None, "blk"),
        ),
        out_specs=(P("rep", "sub", "blk"), P("rep", "sub", "blk"), P()),
        check_vma=False,
    )
```

```python
import functools

import jax
import jax.numpy as jnp
from jax import lax
from jax.experimental import pallas as pl
from jax.experimental.pallas import tpu as pltpu
from jax.sharding import PartitionSpec as P

BS = 64
LANES = 128
SUBL = 8
epsilon = 1e-06


def pieces(value):
    high = value.astype(jnp.bfloat16)
    rest = value - high.astype(jnp.float32)
    middle = rest.astype(jnp.bfloat16)
    low = (rest - middle.astype(jnp.float32)).astype(jnp.bfloat16)
    return high, middle, low


def lane_iota(shape):
    return lax.broadcasted_iota(jnp.int32, shape, len(shape) - 1)


def row_iota(shape):
    return lax.broadcasted_iota(jnp.int32, shape, 0)


def choices(pattern_ref, first_slot, slots):
    block_rows = pattern_ref.shape[1]
    half = block_rows // 2
    place = row_iota((block_rows, block_rows))
    place = jnp.where(place < half, 2 * place, 2 * (place - half) + 1)
    thrice = (block_rows, 3 * block_rows)
    copies = (lane_iota(thrice) % block_rows == row_iota(thrice)).astype(jnp.float32).astype(jnp.bfloat16)
    rows = []
    for k in range(slots):
        chosen = place == pattern_ref[pl.ds(first_slot + k, 1), :]
        chosen = chosen.astype(jnp.float32).astype(jnp.bfloat16)
        rows.append(
            lax.dot_general(chosen, copies, (((0,), (0,)), ((), ())), preferred_element_type=jnp.float32)
        )
    return jnp.concatenate(rows, 0).astype(jnp.bfloat16)


def block_product(vector, blocks_ref, choices_ref, fold_ref):
    slots, block_rows, width = blocks_ref.shape
    half = block_rows // 2
    lower = lane_iota(vector.shape) < BS
    turned = pltpu.roll(vector, BS, 1)
    table = jnp.concatenate([jnp.where(lower, vector, turned), jnp.where(lower, turned, vector)], 0)
    table = jnp.concatenate(pieces(table), 0)
    picked = lax.dot_general(
        choices_ref[...], table, (((1,), (0,)), ((), ())), preferred_element_type=jnp.float32
    )
    lane = lane_iota((block_rows, LANES))

    def exchanged(value, distance):
        up = (lane // distance) % 2 == 1
        return jnp.where(up, pltpu.roll(value, distance, 1), pltpu.roll(value, LANES - distance, 1))

    def merged(left, right, distance):
        up = (lane // distance) % 2 == 1
        return jnp.where(up, right, left) + exchanged(jnp.where(up, left, right), distance)

    waiting = []
    for c in range(width // LANES):
        total = None
        for k in range(slots):
            term = blocks_ref[k, :, pl.ds(c * LANES, LANES)] * picked[k * block_rows : (k + 1) * block_rows]
            total = term if total is None else total + term
        distance, rest = 2, c
        while rest % 2:
            total = merged(waiting.pop(), total, distance)
            distance, rest = distance * 2, rest // 2
        waiting.append(total)
    result = waiting.pop()
    result = result + exchanged(result, 1)
    result = jnp.where((lane % 2 == 1) != (lane >= BS), pltpu.roll(result, BS, 1), result)
    fold_ref[...] = result
    even = fold_ref[pl.ds(0, half, stride=2), :]
    odd = fold_ref[pl.ds(1, half, stride=2), :]
    return jnp.where(lane_iota((half, LANES)) < BS, even, odd)


def take_trace(rows, places):
    count = rows.shape[0]
    low = jnp.broadcast_to(places % LANES, (count, LANES))
    picked = jnp.take_along_axis(rows, low, axis=1)
    return jnp.sum(jnp.where(row_iota((count, LANES)) == places // LANES, picked, 0.0), axis=0, keepdims=True)


def spread(values, places, count):
    aimed = jnp.where(row_iota((count, LANES)) == places // LANES, values, 0.0)
    high = aimed.astype(jnp.bfloat16).astype(jnp.float32)
    rest = aimed - high
    middle = rest.astype(jnp.bfloat16).astype(jnp.float32)
    stack = jnp.concatenate([high, middle, rest - middle], 0).astype(jnp.bfloat16)
    target = (row_iota((LANES, LANES)) == places % LANES).astype(jnp.float32).astype(jnp.bfloat16)
    landed = lax.dot_general(stack, target, (((1,), (1,)), ((), ())), preferred_element_type=jnp.float32)
    return landed[0:count] + landed[count : 2 * count] + landed[2 * count : 3 * count]


def lines_kernel(start_ref, map_ref, near_ref, coupling_ref, pattern_ref, out_ref, choices_ref):
    places = map_ref[...]
    count = coupling_ref.shape[0]
    first_cell = lax.axis_index("blk") * start_ref.shape[0] * LANES
    lines = [take_trace(start_ref[...], places - first_cell), places.astype(jnp.float32)]
    lines += [coupling_ref[n : n + 1, :] for n in range(count)]
    near = near_ref[...].astype(jnp.float32)
    lines += [jnp.broadcast_to(near[:, n : n + 1], (1, LANES)) for n in range(count)]
    lines += [jnp.zeros((SUBL - len(lines), LANES), jnp.float32)]
    out_ref[...] = jnp.concatenate(lines, 0)
    slots = choices_ref.shape[0] // pattern_ref.shape[1]
    choices_ref[...] = choices(pattern_ref, lax.axis_index("blk") * slots, slots)


def widen_kernel(blocks_ref, out_ref):
    out_ref[...] = blocks_ref[...].astype(jnp.float32)


def first_kernel(start_ref, lines_ref, other_ref, blocks_ref, choices_ref, out_ref, vector_ref, fold_ref):
    own_rows, rows = start_ref.shape[0], vector_ref.shape[0]
    blk, parts = lax.axis_index("blk"), lax.axis_size("blk")
    for step in range(parts):
        place = lax.rem(blk + step, parts)
        place = pl.ds(pl.multiple_of(place * own_rows, SUBL), own_rows)
        vector_ref[place, :] = other_ref[step - 1] if step else start_ref[...]
    partial = block_product(vector_ref[...], blocks_ref, choices_ref, fold_ref)
    for device in range(out_ref.shape[0]):
        out_ref[device, 0:rows, :] = partial
        out_ref[device, rows : rows + SUBL, :] = lines_ref[...]


def line(group_ref, device, i):
    first = group_ref.shape[1] - SUBL + i
    return group_ref[device, first : first + 1, :]


def landed(group_ref, sub_at, part, own_rows, count):
    parts = lax.axis_size("blk")
    traces = [line(group_ref, other * parts + part, 0) for other in range(lax.axis_size("sub"))]
    traces = jnp.concatenate(traces, 0)
    names = row_iota(traces.shape).astype(jnp.float32)
    device = sub_at * parts + part
    inflow = jnp.zeros((1, LANES), jnp.float32)
    for n in range(count):
        chosen = jnp.where(names == line(group_ref, device, 2 + count + n), traces, 0.0)
        inflow = inflow + line(group_ref, device, 2 + n) * jnp.sum(chosen, axis=0, keepdims=True)
    places = line(group_ref, device, 1).astype(jnp.int32) - part * own_rows * LANES
    return spread(inflow, places, own_rows), places


def summed(group_ref, sub_at, first, count):
    parts = lax.axis_size("blk")
    total = group_ref[sub_at * parts, first : first + count, :]
    for b in range(1, parts):
        total = total + group_ref[sub_at * parts + b, first : first + count, :]
    return total


def second_kernel(count, group_ref, blocks_ref, choices_ref, out_ref, image_ref, fold_ref):
    rows = image_ref.shape[0]
    sub, parts = lax.axis_index("sub"), lax.axis_size("blk")
    added = [landed(group_ref, sub, part, rows // parts, count)[0] for part in range(parts)]
    image = summed(group_ref, sub, 0, rows) + jnp.concatenate(added, 0)
    image_ref[...] = image
    out_ref[...] = block_product(image, blocks_ref, choices_ref, fold_ref)


def down(left, right):
    return jnp.sum(left * right, axis=0, keepdims=True)


def inflow_kernel(vector_ref, image_ref, group_ref, near_ref, out_ref, sums_ref):
    rows = image_ref.shape[0]
    count = near_ref.shape[1]
    sub, parts = lax.axis_index("sub"), lax.axis_size("blk")
    own_rows = rows // parts
    for part in range(parts):
        device = sub * parts + part
        inflow = jnp.zeros((1, LANES), jnp.float32)
        for n in range(count):
            source = near_ref[0, n]
            added, places = landed(group_ref, source, part, own_rows, count)
            trace = take_trace(summed(group_ref, source, part * own_rows, own_rows) + added, places)
            inflow = inflow + line(group_ref, device, 2 + n) * trace
        places = line(group_ref, device, 1).astype(jnp.int32) - part * own_rows * LANES
        out_ref[part * own_rows : (part + 1) * own_rows, :] = spread(inflow, places, own_rows)
    vector, image = vector_ref[...], image_ref[...]
    sums = [down(vector, vector), down(vector, image), down(image, image)]
    sums_ref[...] = jnp.concatenate([*sums, jnp.zeros((SUBL - len(sums), LANES), jnp.float32)], 0)


def pair_kernel(vector_ref, image_ref, sums_ref, inflow_ref, mine_ref, other_ref, out_ref, again_ref, part_ref):
    parts = part_ref.shape[0]
    for step in range(parts):
        part_ref[lax.rem(lax.axis_index("blk") + step, parts)] = other_ref[step - 1] if step else mine_ref[...]
    again = inflow_ref[...]
    for part in range(parts):
        again = again + part_ref[part]
    again_ref[...] = again
    sums = [down(vector_ref[...], again), down(image_ref[...], again), down(again, again)]
    sums = jnp.concatenate([sums_ref[0:3, :], *sums, sums_ref[6:SUBL, :]], 0)
    sums = jnp.sum(sums, axis=1, keepdims=True)
    sums = jnp.where(row_iota((SUBL, LANES)) == lane_iota((SUBL, LANES)), sums, 0.0)
    sums = jnp.sum(sums, axis=0, keepdims=True)
    for device in range(out_ref.shape[0]):
        out_ref[device] = sums


def last_kernel(cells, start_ref, image_ref, again_ref, sums_ref, second_ref, third_ref, entries_ref):
    sums = jnp.sum(sums_ref[...], axis=0) / cells

    def whole(i):
        return jnp.broadcast_to(sums[:, i : i + 1], (1, LANES))

    vv, vw, ww, vy, wy, yy = (whole(i) for i in range(6))
    norm_square = vv + epsilon
    inverse = 1.0 / norm_square
    h11 = vw * inverse
    skew = vy - h11 * vw
    first_square = jnp.maximum(ww - 2.0 * h11 * vw + h11 * h11 * vv, 0.0) * inverse + epsilon
    over_first = lax.rsqrt(first_square)
    h21 = first_square * over_first
    scale = lax.rsqrt(norm_square) * over_first
    h12 = skew * inverse * over_first
    h22 = (wy - h11 * (ww + skew)) * scale * scale
    near = h11 + h22
    far = skew * inverse - h11 * h22
    second_square = yy + near * near * ww + far * far * vv + 2.0 * (near * far * vw - near * wy - far * vy)
    second_square = jnp.maximum(second_square, 0.0) * scale * scale + epsilon
    over_second = lax.rsqrt(second_square)
    h32 = second_square * over_second

    own_rows = start_ref.shape[0]
    own = pl.ds(pl.multiple_of(lax.axis_index("blk") * own_rows, SUBL), own_rows)
    vector, image = start_ref[...], image_ref[own, :]
    second_ref[...] = (image - h11 * vector) * scale
    third_ref[...] = (again_ref[own, :] - near * image - far * vector) * (scale * over_second)
    lane = lane_iota((1, LANES))
    entries = h32
    for i, value in enumerate((h11, h21, h12, h22)):
        entries = jnp.where(lane == i, value, entries)
    entries_ref[...] = entries[:, 0:5]


def per_device(start_vector, blocks, pattern, trace_map, neighbours, coupling):
    own_cells = start_vector.shape[2]
    own_rows = own_cells // LANES
    parts, subs, reps = lax.axis_size("blk"), lax.axis_size("sub"), lax.axis_size("rep")
    rows = own_rows * parts
    cells = own_cells * parts * subs * reps
    start = start_vector.reshape(own_rows, LANES)
    local_map = trace_map[0]
    blocks, pattern, neighbours, coupling = blocks[0, 0], pattern[0, 0], neighbours[0], coupling[0, 0]
    vmem = pl.BlockSpec(memory_space=pltpu.VMEM)
    params = pltpu.CompilerParams(vmem_limit_bytes=32 * 1024 * 1024)

    def rowed(*shape):
        return jax.ShapeDtypeStruct((*shape, LANES), jnp.float32)

    smem = pl.BlockSpec(memory_space=pltpu.SMEM)

    def from_others(value):
        got = [
            lax.ppermute(value[None], "blk", [((i + step) % parts, i) for i in range(parts)])
            for step in range(1, parts)
        ]
        return got[0] if parts == 2 else jnp.concatenate(got, 0)

    others = from_others(start)
    slots, block_rows = blocks.shape[:2]
    scratch = [pltpu.VMEM((block_rows, LANES), jnp.float32)]
    lines, chosen = pl.pallas_call(
        lines_kernel,
        out_shape=(rowed(SUBL), jax.ShapeDtypeStruct((slots * block_rows, 3 * block_rows), jnp.bfloat16)),
        in_specs=[vmem] * 5,
        out_specs=(vmem, vmem),
        compiler_params=params,
        cost_estimate=pl.CostEstimate(flops=1 << 32, bytes_accessed=1 << 20, transcendentals=0),
        name="group_lines",
    )(start, local_map, neighbours, coupling, pattern)
    wide = pl.pallas_call(
        widen_kernel,
        out_shape=jax.ShapeDtypeStruct(blocks.shape, jnp.float32),
        in_specs=[vmem],
        out_specs=vmem,
        compiler_params=params,
        cost_estimate=pl.CostEstimate(flops=1 << 32, bytes_accessed=3 << 20, transcendentals=0),
        name="wide_blocks",
    )(blocks)
    partial, vector = pl.pallas_call(
        first_kernel,
        out_shape=(rowed(subs * parts, rows + SUBL), rowed(rows)),
        in_specs=[vmem] * 5,
        out_specs=(vmem, vmem),
        scratch_shapes=scratch,
        compiler_params=params,
        name="first_image",
    )(start, lines, others, wide, chosen)
    group = lax.all_to_all(partial, ("sub", "blk"), 0, 0, tiled=True)
    second, image = pl.pallas_call(
        functools.partial(second_kernel, coupling.shape[0]),
        out_shape=(rowed(rows), rowed(rows)),
        in_specs=[vmem] * 3,
        out_specs=(vmem, vmem),
        scratch_shapes=scratch,
        compiler_params=params,
        name="second_image",
    )(group, wide, chosen)
    others = from_others(second)
    inflow, sums = pl.pallas_call(
        inflow_kernel,
        out_shape=(rowed(rows), rowed(SUBL)),
        in_specs=[vmem, vmem, vmem, smem],
        out_specs=(vmem, vmem),
        compiler_params=params,
        cost_estimate=pl.CostEstimate(flops=1 << 32, bytes_accessed=1 << 20, transcendentals=0),
        name="second_inflow",
    )(vector, image, group, neighbours)
    sums, again = pl.pallas_call(
        pair_kernel,
        out_shape=(rowed(reps * subs, 1), rowed(rows)),
        in_specs=[vmem] * 6,
        out_specs=(vmem, vmem),
        scratch_shapes=[pltpu.VMEM((parts, rows, LANES), jnp.float32)],
        compiler_params=params,
        name="pair_sums",
    )(vector, image, sums, inflow, second, others)
    sums = lax.all_to_all(sums, ("rep", "sub"), 0, 0, tiled=True)
    second, third, entries = pl.pallas_call(
        functools.partial(last_kernel, float(cells)),
        out_shape=(rowed(own_rows), rowed(own_rows), jax.ShapeDtypeStruct((1, 5), jnp.float32)),
        in_specs=[vmem] * 4,
        out_specs=(vmem, vmem, vmem),
        compiler_params=params,
        name="arnoldi_entries",
    )(start, image, again, sums)
    return second.reshape(start_vector.shape), third.reshape(start_vector.shape), entries.reshape(5)


def solution(mesh):
    return jax.shard_map(
        per_device,
        mesh=mesh,
        in_specs=(
            P("rep", "sub", "blk"),
            P("rep", "sub", "blk", None, None),
            P("rep", "sub", None, None),
            P("rep", "sub", "blk"),
            P("rep", "sub", None),
            P("rep", "sub", None, "blk"),
        ),
        out_specs=(P("rep", "sub", "blk"), P("rep", "sub", "blk"), P()),
        check_vma=False,
    )
```

```python
import functools

import jax
import jax.numpy as jnp
from jax import lax
from jax.experimental import pallas as pl
from jax.experimental.pallas import tpu as pltpu
from jax.sharding import PartitionSpec as P

BS = 64
LANES = 128
SUBL = 8
epsilon = 1e-06


def pieces(value):
    high = value.astype(jnp.bfloat16)
    rest = value - high.astype(jnp.float32)
    middle = rest.astype(jnp.bfloat16)
    low = (rest - middle.astype(jnp.float32)).astype(jnp.bfloat16)
    return high, middle, low


def lane_iota(shape):
    return lax.broadcasted_iota(jnp.int32, shape, len(shape) - 1)


def row_iota(shape):
    return lax.broadcasted_iota(jnp.int32, shape, 0)


def choices(pattern_ref, slot):
    block_rows = pattern_ref.shape[1]
    half = block_rows // 2
    place = row_iota((block_rows, block_rows))
    place = jnp.where(place < half, 2 * place, 2 * (place - half) + 1)
    thrice = (block_rows, 3 * block_rows)
    copies = (lane_iota(thrice) % block_rows == row_iota(thrice)).astype(jnp.float32).astype(jnp.bfloat16)
    chosen = (place == pattern_ref[pl.ds(slot, 1), :]).astype(jnp.float32).astype(jnp.bfloat16)
    return lax.dot_general(chosen, copies, (((0,), (0,)), ((), ())), preferred_element_type=jnp.float32)


def block_product(vector, fetch, width, chosen, fold_ref, halves_ref):
    block_rows = fold_ref.shape[0]
    slots = chosen.shape[0] // block_rows
    half = block_rows // 2
    lower = lane_iota(vector.shape) < BS
    turned = pltpu.roll(vector, BS, 1)
    table = jnp.concatenate([jnp.where(lower, vector, turned), jnp.where(lower, turned, vector)], 0)
    table = jnp.concatenate(pieces(table), 0)
    picked = lax.dot_general(chosen, table, (((1,), (0,)), ((), ())), preferred_element_type=jnp.float32)
    ones = (row_iota((2 * LANES, LANES)) % LANES) // BS == lane_iota((2 * LANES, LANES)) % 2
    ones = ones.astype(jnp.float32).astype(jnp.bfloat16)
    pair = (lane_iota((block_rows, LANES)) % BS) // 2
    chunks = width // LANES
    together = chunks // 4
    result = jnp.zeros((block_rows, LANES), jnp.float32)
    for first in range(0, chunks, together):
        for c in range(first, first + together):
            total = None
            for k in range(slots):
                term = fetch(k, pl.ds(c * LANES, LANES)) * picked[k * block_rows : (k + 1) * block_rows]
                total = term if total is None else total + term
            high = total.astype(jnp.bfloat16)
            here = pl.ds(c * block_rows, block_rows)
            halves_ref[here, 0:LANES] = high
            halves_ref[here, LANES : 2 * LANES] = (total - high.astype(jnp.float32)).astype(jnp.bfloat16)
        sums = lax.dot_general(
            halves_ref[pl.ds(first * block_rows, together * block_rows), :],
            ones,
            (((1,), (0,)), ((), ())),
            preferred_element_type=jnp.float32,
        )
        for i in range(together):
            result = jnp.where(pair == first + i, sums[i * block_rows : (i + 1) * block_rows], result)
    fold_ref[...] = result
    even = fold_ref[pl.ds(0, half, stride=2), :]
    odd = fold_ref[pl.ds(1, half, stride=2), :]
    return jnp.where(lane_iota((half, LANES)) < BS, even, odd)


def take_trace(rows, places):
    count = rows.shape[0]
    low = jnp.broadcast_to(places % LANES, (count, LANES))
    picked = jnp.take_along_axis(rows, low, axis=1)
    return jnp.sum(jnp.where(row_iota((count, LANES)) == places // LANES, picked, 0.0), axis=0, keepdims=True)


def spread(values, places, count):
    aimed = jnp.where(row_iota((count, LANES)) == places // LANES, values, 0.0)
    high = aimed.astype(jnp.bfloat16).astype(jnp.float32)
    rest = aimed - high
    middle = rest.astype(jnp.bfloat16).astype(jnp.float32)
    stack = jnp.concatenate([high, middle, rest - middle], 0).astype(jnp.bfloat16)
    target = (row_iota((LANES, LANES)) == places % LANES).astype(jnp.float32).astype(jnp.bfloat16)
    landed = lax.dot_general(stack, target, (((1,), (1,)), ((), ())), preferred_element_type=jnp.float32)
    return landed[0:count] + landed[count : 2 * count] + landed[2 * count : 3 * count]


def lines_kernel(
    start_ref, map_ref, near_ref, coupling_ref, pattern_ref, out_ref, first_ref, second_ref, rows_ref
):
    places = map_ref[...]
    count = coupling_ref.shape[0]
    blk, parts = lax.axis_index("blk"), lax.axis_size("blk")
    lines = [take_trace(start_ref[...], places - blk * start_ref.shape[0] * LANES), places.astype(jnp.float32)]
    lines += [coupling_ref[n : n + 1, :] for n in range(count)]
    near = near_ref[...].astype(jnp.float32)
    lines += [jnp.broadcast_to(near[:, n : n + 1], (1, LANES)) for n in range(count)]
    lines += [jnp.zeros((SUBL - len(lines), LANES), jnp.float32)]
    out_ref[...] = jnp.concatenate(lines, 0)
    all_slots, block_rows = pattern_ref.shape
    slots = all_slots // parts
    own_rows = block_rows // parts
    for step in range(parts):
        for k in range(slots):
            at = step * slots + k
            chosen = choices(pattern_ref, lax.rem(blk + step, parts) * slots + k)
            if step == 0:
                first_ref[k * block_rows : (k + 1) * block_rows, :] = chosen.astype(jnp.bfloat16)
            rows_ref[...] = chosen
            own = rows_ref[pl.ds(pl.multiple_of(blk * own_rows, SUBL), own_rows), :]
            second_ref[at * own_rows : (at + 1) * own_rows, :] = own.astype(jnp.bfloat16)


def widen_kernel(blocks_ref, out_ref, send_ref):
    out_ref[...] = blocks_ref[...].astype(jnp.float32)
    others, _, own_rows, _ = send_ref.shape
    blk, parts = lax.axis_index("blk"), lax.axis_size("blk")
    for step in range(1, others + 1):
        part = lax.rem(blk + parts - step, parts)
        send_ref[step - 1] = blocks_ref[:, pl.ds(pl.multiple_of(part * own_rows, 16), own_rows), :]


def first_kernel(
    start_ref, lines_ref, other_ref, blocks_ref, choices_ref, out_ref, vector_ref, fold_ref, halves_ref
):
    own_rows, rows = start_ref.shape[0], vector_ref.shape[0]
    blk, parts = lax.axis_index("blk"), lax.axis_size("blk")
    for step in range(parts):
        place = lax.rem(blk + step, parts)
        place = pl.ds(pl.multiple_of(place * own_rows, SUBL), own_rows)
        vector_ref[place, :] = other_ref[step - 1] if step else start_ref[...]

    def fetch(k, lanes):
        return blocks_ref[k, :, lanes]

    partial = block_product(
        vector_ref[...], fetch, blocks_ref.shape[2], choices_ref[...], fold_ref, halves_ref
    )
    for device in range(out_ref.shape[0]):
        out_ref[device, 0:rows, :] = partial
        out_ref[device, rows : rows + SUBL, :] = lines_ref[...]


def line(group_ref, device, i):
    first = group_ref.shape[1] - SUBL + i
    return group_ref[device, first : first + 1, :]


def landed(group_ref, sub_at, part, own_rows, count):
    parts = lax.axis_size("blk")
    traces = [line(group_ref, other * parts + part, 0) for other in range(lax.axis_size("sub"))]
    traces = jnp.concatenate(traces, 0)
    names = row_iota(traces.shape).astype(jnp.float32)
    device = sub_at * parts + part
    inflow = jnp.zeros((1, LANES), jnp.float32)
    for n in range(count):
        chosen = jnp.where(names == line(group_ref, device, 2 + count + n), traces, 0.0)
        inflow = inflow + line(group_ref, device, 2 + n) * jnp.sum(chosen, axis=0, keepdims=True)
    places = line(group_ref, device, 1).astype(jnp.int32) - part * own_rows * LANES
    return spread(inflow, places, own_rows), places


def summed(group_ref, sub_at, where):
    parts = lax.axis_size("blk")
    total = group_ref[sub_at * parts, where, :]
    for b in range(1, parts):
        total = total + group_ref[sub_at * parts + b, where, :]
    return total


def down(left, right):
    return jnp.sum(left * right, axis=0, keepdims=True)


def second_kernel(
    start_ref,
    group_ref,
    blocks_ref,
    other_ref,
    choices_ref,
    near_ref,
    out_ref,
    image_ref,
    again_ref,
    whole_ref,
    fold_ref,
    halves_ref,
):
    own_rows = start_ref.shape[0]
    slots, block_rows, width = blocks_ref.shape
    count = near_ref.shape[1]
    sub, blk, parts = lax.axis_index("sub"), lax.axis_index("blk"), lax.axis_size("blk")
    own_blocks = block_rows // parts
    here = pl.ds(pl.multiple_of(blk * own_blocks, 16), own_blocks)
    own = pl.ds(pl.multiple_of(blk * own_rows, SUBL), own_rows)
    added = [landed(group_ref, sub, part, own_rows, count)[0] for part in range(parts)]
    image = summed(group_ref, sub, pl.ds(0, own_rows * parts)) + jnp.concatenate(added, 0)
    whole_ref[...] = image

    def fetch(k, lanes):
        if k < slots:
            return blocks_ref[k, here, lanes]
        return other_ref[k // slots - 1, k % slots, :, lanes].astype(jnp.float32)

    again = block_product(image, fetch, width, choices_ref[...], fold_ref, halves_ref)
    inflow = jnp.zeros((1, LANES), jnp.float32)
    for n in range(count):
        source = near_ref[0, n]
        added, places = landed(group_ref, source, blk, own_rows, count)
        trace = take_trace(summed(group_ref, source, own) + added, places)
        inflow = inflow + line(group_ref, sub * parts + blk, 2 + n) * trace
    places = line(group_ref, sub * parts + blk, 1).astype(jnp.int32) - blk * own_rows * LANES
    again = again + spread(inflow, places, own_rows)
    again_ref[...] = again
    vector, image = start_ref[...], whole_ref[own, :]
    image_ref[...] = image
    sums = [down(vector, vector), down(vector, image), down(image, image)]
    sums += [down(vector, again), down(image, again), down(again, again)]
    sums = jnp.concatenate([*sums, jnp.zeros((SUBL - 6, LANES), jnp.float32)], 0)
    sums = jnp.sum(sums, axis=1, keepdims=True)
    sums = jnp.where(row_iota((SUBL, LANES)) == lane_iota((SUBL, LANES)), sums, 0.0)
    sums = jnp.sum(sums, axis=0, keepdims=True)
    for device in range(out_ref.shape[0]):
        out_ref[device] = sums


def last_kernel(cells, start_ref, image_ref, again_ref, sums_ref, second_ref, third_ref, entries_ref):
    sums = jnp.sum(sums_ref[...], axis=0) / cells

    def whole(i):
        return jnp.broadcast_to(sums[:, i : i + 1], (1, LANES))

    vv, vw, ww, vy, wy, yy = (whole(i) for i in range(6))
    norm_square = vv + epsilon
    inverse = 1.0 / norm_square
    h11 = vw * inverse
    skew = vy - h11 * vw
    first_square = jnp.maximum(ww - 2.0 * h11 * vw + h11 * h11 * vv, 0.0) * inverse + epsilon
    over_first = lax.rsqrt(first_square)
    h21 = first_square * over_first
    scale = lax.rsqrt(norm_square) * over_first
    h12 = skew * inverse * over_first
    h22 = (wy - h11 * (ww + skew)) * scale * scale
    near = h11 + h22
    far = skew * inverse - h11 * h22
    second_square = yy + near * near * ww + far * far * vv + 2.0 * (near * far * vw - near * wy - far * vy)
    second_square = jnp.maximum(second_square, 0.0) * scale * scale + epsilon
    over_second = lax.rsqrt(second_square)
    h32 = second_square * over_second

    vector, image = start_ref[...], image_ref[...]
    second_ref[...] = (image - h11 * vector) * scale
    third_ref[...] = (again_ref[...] - near * image - far * vector) * (scale * over_second)
    lane = lane_iota((1, LANES))
    entries = h32
    for i, value in enumerate((h11, h21, h12, h22)):
        entries = jnp.where(lane == i, value, entries)
    entries_ref[...] = entries[:, 0:5]


def per_device(start_vector, blocks, pattern, trace_map, neighbours, coupling):
    own_cells = start_vector.shape[2]
    own_rows = own_cells // LANES
    parts, subs, reps = lax.axis_size("blk"), lax.axis_size("sub"), lax.axis_size("rep")
    rows = own_rows * parts
    cells = own_cells * parts * subs * reps
    start = start_vector.reshape(own_rows, LANES)
    local_map = trace_map[0]
    blocks, pattern, neighbours, coupling = blocks[0, 0], pattern[0, 0], neighbours[0], coupling[0, 0]
    vmem = pl.BlockSpec(memory_space=pltpu.VMEM)
    params = pltpu.CompilerParams(vmem_limit_bytes=32 * 1024 * 1024)

    def rowed(*shape):
        return jax.ShapeDtypeStruct((*shape, LANES), jnp.float32)

    smem = pl.BlockSpec(memory_space=pltpu.SMEM)

    def from_others(pick):
        got = [
            lax.ppermute(pick(step), "blk", [((i + step) % parts, i) for i in range(parts)])
            for step in range(1, parts)
        ]
        return got[0] if parts == 2 else jnp.concatenate(got, 0)

    slots, block_rows, width = blocks.shape
    own_blocks = block_rows // parts

    def scratch(count):
        return [
            pltpu.VMEM((count, LANES), jnp.float32),
            pltpu.VMEM((count * width // LANES, 2 * LANES), jnp.bfloat16),
        ]

    def shaped(dtype, *shape):
        return jax.ShapeDtypeStruct(shape, dtype)

    long = pl.CostEstimate(flops=1 << 32, bytes_accessed=1 << 20, transcendentals=0)
    others = from_others(lambda step: start[None])
    wide, send = pl.pallas_call(
        widen_kernel,
        out_shape=(
            shaped(jnp.float32, *blocks.shape),
            shaped(jnp.bfloat16, parts - 1, slots, own_blocks, width),
        ),
        in_specs=[vmem],
        out_specs=(vmem, vmem),
        compiler_params=params,
        cost_estimate=long,
        name="wide_blocks",
    )(blocks)
    other_blocks = from_others(lambda step: send if parts == 2 else send[step - 1 : step])
    lines, chosen, chosen_own = pl.pallas_call(
        lines_kernel,
        out_shape=(
            rowed(SUBL),
            shaped(jnp.bfloat16, slots * block_rows, 3 * block_rows),
            shaped(jnp.bfloat16, slots * block_rows, 3 * block_rows),
        ),
        in_specs=[vmem] * 5,
        out_specs=(vmem, vmem, vmem),
        scratch_shapes=[pltpu.VMEM((block_rows, 3 * block_rows), jnp.float32)],
        compiler_params=params,
        cost_estimate=long,
        name="group_lines",
    )(start, local_map, neighbours, coupling, pattern)
    partial, vector = pl.pallas_call(
        first_kernel,
        out_shape=(rowed(subs * parts, rows + SUBL), rowed(rows)),
        in_specs=[vmem] * 5,
        out_specs=(vmem, vmem),
        scratch_shapes=scratch(block_rows),
        compiler_params=params,
        name="first_image",
    )(start, lines, others, wide, chosen)
    group = lax.all_to_all(partial, ("sub", "blk"), 0, 0, tiled=True)
    sums, image, again = pl.pallas_call(
        second_kernel,
        out_shape=(rowed(reps * subs * parts, 1), rowed(own_rows), rowed(own_rows)),
        in_specs=[vmem] * 5 + [smem],
        out_specs=(vmem, vmem, vmem),
        scratch_shapes=[pltpu.VMEM((rows, LANES), jnp.float32), *scratch(own_blocks)],
        compiler_params=params,
        name="second_image",
    )(start, group, wide, other_blocks, chosen_own, neighbours)
    sums = lax.all_to_all(sums, ("rep", "sub", "blk"), 0, 0, tiled=True)
    second, third, entries = pl.pallas_call(
        functools.partial(last_kernel, float(cells)),
        out_shape=(rowed(own_rows), rowed(own_rows), jax.ShapeDtypeStruct((1, 5), jnp.float32)),
        in_specs=[vmem] * 4,
        out_specs=(vmem, vmem, vmem),
        compiler_params=params,
        name="arnoldi_entries",
    )(start, image, again, sums)
    return second.reshape(start_vector.shape), third.reshape(start_vector.shape), entries.reshape(5)


def solution(mesh):
    return jax.shard_map(
        per_device,
        mesh=mesh,
        in_specs=(
            P("rep", "sub", "blk"),
            P("rep", "sub", "blk", None, None),
            P("rep", "sub", None, None),
            P("rep", "sub", "blk"),
            P("rep", "sub", None),
            P("rep", "sub", None, "blk"),
        ),
        out_specs=(P("rep", "sub", "blk"), P("rep", "sub", "blk"), P()),
        check_vma=False,
    )
```

```python
import functools

import jax
import jax.numpy as jnp
from jax import lax
from jax.experimental import pallas as pl
from jax.experimental.pallas import tpu as pltpu
from jax.sharding import PartitionSpec as P

BS = 64
LANES = 128
SUBL = 8
epsilon = 1e-06


def pieces(value):
    high = value.astype(jnp.bfloat16)
    rest = value - high.astype(jnp.float32)
    middle = rest.astype(jnp.bfloat16)
    low = (rest - middle.astype(jnp.float32)).astype(jnp.bfloat16)
    return high, middle, low


def lane_iota(shape):
    return lax.broadcasted_iota(jnp.int32, shape, len(shape) - 1)


def row_iota(shape):
    return lax.broadcasted_iota(jnp.int32, shape, 0)


def choices(pattern_ref, slot):
    block_rows = pattern_ref.shape[1]
    half = block_rows // 2
    place = row_iota((block_rows, block_rows))
    place = jnp.where(place < half, 2 * place, 2 * (place - half) + 1)
    thrice = (block_rows, 3 * block_rows)
    copies = (lane_iota(thrice) % block_rows == row_iota(thrice)).astype(jnp.float32).astype(jnp.bfloat16)
    chosen = (place == pattern_ref[pl.ds(slot, 1), :]).astype(jnp.float32).astype(jnp.bfloat16)
    return lax.dot_general(chosen, copies, (((0,), (0,)), ((), ())), preferred_element_type=jnp.float32)


def block_product(vector, fetch, width, chosen, fold_ref, halves_ref):
    block_rows = fold_ref.shape[0]
    slots = chosen.shape[0] // block_rows
    half = block_rows // 2
    lower = lane_iota(vector.shape) < BS
    turned = pltpu.roll(vector, BS, 1)
    table = jnp.concatenate([jnp.where(lower, vector, turned), jnp.where(lower, turned, vector)], 0)
    table = jnp.concatenate(pieces(table), 0)
    picked = lax.dot_general(chosen, table, (((1,), (0,)), ((), ())), preferred_element_type=jnp.float32)
    ones = (row_iota((2 * LANES, LANES)) % LANES) // BS == lane_iota((2 * LANES, LANES)) % 2
    ones = ones.astype(jnp.float32).astype(jnp.bfloat16)
    pair = (lane_iota((block_rows, LANES)) % BS) // 2
    chunks = width // LANES
    together = chunks // 4
    result = jnp.zeros((block_rows, LANES), jnp.float32)
    for first in range(0, chunks, together):
        for c in range(first, first + together):
            total = None
            for k in range(slots):
                term = fetch(k, pl.ds(c * LANES, LANES)) * picked[k * block_rows : (k + 1) * block_rows]
                total = term if total is None else total + term
            high = total.astype(jnp.bfloat16)
            here = pl.ds(c * block_rows, block_rows)
            halves_ref[here, 0:LANES] = high
            halves_ref[here, LANES : 2 * LANES] = (total - high.astype(jnp.float32)).astype(jnp.bfloat16)
        sums = lax.dot_general(
            halves_ref[pl.ds(first * block_rows, together * block_rows), :],
            ones,
            (((1,), (0,)), ((), ())),
            preferred_element_type=jnp.float32,
        )
        for i in range(together):
            result = jnp.where(pair == first + i, sums[i * block_rows : (i + 1) * block_rows], result)
    fold_ref[...] = result
    even = fold_ref[pl.ds(0, half, stride=2), :]
    odd = fold_ref[pl.ds(1, half, stride=2), :]
    return jnp.where(lane_iota((half, LANES)) < BS, even, odd)


def take_trace(rows, places):
    count = rows.shape[0]
    low = jnp.broadcast_to(places % LANES, (count, LANES))
    picked = jnp.take_along_axis(rows, low, axis=1)
    return jnp.sum(jnp.where(row_iota((count, LANES)) == places // LANES, picked, 0.0), axis=0, keepdims=True)


def spread(values, places, count):
    aimed = jnp.where(row_iota((count, LANES)) == places // LANES, values, 0.0)
    high = aimed.astype(jnp.bfloat16).astype(jnp.float32)
    rest = aimed - high
    middle = rest.astype(jnp.bfloat16).astype(jnp.float32)
    stack = jnp.concatenate([high, middle, rest - middle], 0).astype(jnp.bfloat16)
    target = (row_iota((LANES, LANES)) == places % LANES).astype(jnp.float32).astype(jnp.bfloat16)
    landed = lax.dot_general(stack, target, (((1,), (1,)), ((), ())), preferred_element_type=jnp.float32)
    return landed[0:count] + landed[count : 2 * count] + landed[2 * count : 3 * count]


def lines_kernel(
    start_ref, map_ref, near_ref, coupling_ref, pattern_ref, out_ref, first_ref, second_ref, rows_ref
):
    places = map_ref[...]
    count = coupling_ref.shape[0]
    blk, parts = lax.axis_index("blk"), lax.axis_size("blk")
    lines = [take_trace(start_ref[...], places - blk * start_ref.shape[0] * LANES), places.astype(jnp.float32)]
    lines += [coupling_ref[n : n + 1, :] for n in range(count)]
    near = near_ref[...].astype(jnp.float32)
    lines += [jnp.broadcast_to(near[:, n : n + 1], (1, LANES)) for n in range(count)]
    lines += [jnp.zeros((SUBL - len(lines), LANES), jnp.float32)]
    out_ref[...] = jnp.concatenate(lines, 0)
    all_slots, block_rows = pattern_ref.shape
    slots = all_slots // parts
    own_rows = block_rows // parts
    for step in range(parts):
        for k in range(slots):
            at = step * slots + k
            chosen = choices(pattern_ref, lax.rem(blk + step, parts) * slots + k)
            if step == 0:
                first_ref[k * block_rows : (k + 1) * block_rows, :] = chosen.astype(jnp.bfloat16)
            rows_ref[...] = chosen
            own = rows_ref[pl.ds(pl.multiple_of(blk * own_rows, SUBL), own_rows), :]
            second_ref[at * own_rows : (at + 1) * own_rows, :] = own.astype(jnp.bfloat16)


def widen_kernel(blocks_ref, out_ref):
    out_ref[...] = blocks_ref[...].astype(jnp.float32)


def first_kernel(
    start_ref, lines_ref, other_ref, blocks_ref, choices_ref, out_ref, vector_ref, fold_ref, halves_ref
):
    own_rows, rows = start_ref.shape[0], vector_ref.shape[0]
    blk, parts = lax.axis_index("blk"), lax.axis_size("blk")
    for step in range(parts):
        place = lax.rem(blk + step, parts)
        place = pl.ds(pl.multiple_of(place * own_rows, SUBL), own_rows)
        vector_ref[place, :] = other_ref[step - 1] if step else start_ref[...]

    def fetch(k, lanes):
        return blocks_ref[k, :, lanes]

    partial = block_product(
        vector_ref[...], fetch, blocks_ref.shape[2], choices_ref[...], fold_ref, halves_ref
    )
    for device in range(out_ref.shape[0]):
        out_ref[device, 0:rows, :] = partial
        out_ref[device, rows : rows + SUBL, :] = lines_ref[...]


def line(group_ref, device, i):
    first = group_ref.shape[1] - SUBL + i
    return group_ref[device, first : first + 1, :]


def landed(group_ref, sub_at, part, own_rows, count):
    parts = lax.axis_size("blk")
    traces = [line(group_ref, other * parts + part, 0) for other in range(lax.axis_size("sub"))]
    traces = jnp.concatenate(traces, 0)
    names = row_iota(traces.shape).astype(jnp.float32)
    device = sub_at * parts + part
    inflow = jnp.zeros((1, LANES), jnp.float32)
    for n in range(count):
        chosen = jnp.where(names == line(group_ref, device, 2 + count + n), traces, 0.0)
        inflow = inflow + line(group_ref, device, 2 + n) * jnp.sum(chosen, axis=0, keepdims=True)
    places = line(group_ref, device, 1).astype(jnp.int32) - part * own_rows * LANES
    return spread(inflow, places, own_rows), places


def summed(group_ref, sub_at, where):
    parts = lax.axis_size("blk")
    total = group_ref[sub_at * parts, where, :]
    for b in range(1, parts):
        total = total + group_ref[sub_at * parts + b, where, :]
    return total


def down(left, right):
    return jnp.sum(left * right, axis=0, keepdims=True)


def second_kernel(
    start_ref,
    group_ref,
    blocks_ref,
    other_ref,
    choices_ref,
    near_ref,
    out_ref,
    image_ref,
    again_ref,
    whole_ref,
    fold_ref,
    halves_ref,
):
    own_rows = start_ref.shape[0]
    slots, block_rows, width = blocks_ref.shape
    count = near_ref.shape[1]
    sub, blk, parts = lax.axis_index("sub"), lax.axis_index("blk"), lax.axis_size("blk")
    own_blocks = block_rows // parts
    here = pl.ds(pl.multiple_of(blk * own_blocks, 16), own_blocks)
    own = pl.ds(pl.multiple_of(blk * own_rows, SUBL), own_rows)
    added = [landed(group_ref, sub, part, own_rows, count)[0] for part in range(parts)]
    image = summed(group_ref, sub, pl.ds(0, own_rows * parts)) + jnp.concatenate(added, 0)
    whole_ref[...] = image

    def fetch(k, lanes):
        if k < slots:
            return blocks_ref[k, here, lanes]
        return other_ref[k // slots - 1, k % slots, :, lanes].astype(jnp.float32)

    again = block_product(image, fetch, width, choices_ref[...], fold_ref, halves_ref)
    inflow = jnp.zeros((1, LANES), jnp.float32)
    for n in range(count):
        source = near_ref[0, n]
        added, places = landed(group_ref, source, blk, own_rows, count)
        trace = take_trace(summed(group_ref, source, own) + added, places)
        inflow = inflow + line(group_ref, sub * parts + blk, 2 + n) * trace
    places = line(group_ref, sub * parts + blk, 1).astype(jnp.int32) - blk * own_rows * LANES
    again = again + spread(inflow, places, own_rows)
    again_ref[...] = again
    vector, image = start_ref[...], whole_ref[own, :]
    image_ref[...] = image
    sums = [down(vector, vector), down(vector, image), down(image, image)]
    sums += [down(vector, again), down(image, again), down(again, again)]
    sums = jnp.concatenate([*sums, jnp.zeros((SUBL - 6, LANES), jnp.float32)], 0)
    sums = jnp.sum(sums, axis=1, keepdims=True)
    sums = jnp.where(row_iota((SUBL, LANES)) == lane_iota((SUBL, LANES)), sums, 0.0)
    sums = jnp.sum(sums, axis=0, keepdims=True)
    for device in range(out_ref.shape[0]):
        out_ref[device] = sums


def last_kernel(cells, start_ref, image_ref, again_ref, sums_ref, second_ref, third_ref, entries_ref):
    sums = jnp.sum(sums_ref[...], axis=0) / cells

    def whole(i):
        return jnp.broadcast_to(sums[:, i : i + 1], (1, LANES))

    vv, vw, ww, vy, wy, yy = (whole(i) for i in range(6))
    norm_square = vv + epsilon
    inverse = 1.0 / norm_square
    h11 = vw * inverse
    skew = vy - h11 * vw
    first_square = jnp.maximum(ww - 2.0 * h11 * vw + h11 * h11 * vv, 0.0) * inverse + epsilon
    over_first = lax.rsqrt(first_square)
    h21 = first_square * over_first
    scale = lax.rsqrt(norm_square) * over_first
    h12 = skew * inverse * over_first
    h22 = (wy - h11 * (ww + skew)) * scale * scale
    near = h11 + h22
    far = skew * inverse - h11 * h22
    second_square = yy + near * near * ww + far * far * vv + 2.0 * (near * far * vw - near * wy - far * vy)
    second_square = jnp.maximum(second_square, 0.0) * scale * scale + epsilon
    over_second = lax.rsqrt(second_square)
    h32 = second_square * over_second

    vector, image = start_ref[...], image_ref[...]
    second_ref[...] = (image - h11 * vector) * scale
    third_ref[...] = (again_ref[...] - near * image - far * vector) * (scale * over_second)
    lane = lane_iota((1, LANES))
    entries = h32
    for i, value in enumerate((h11, h21, h12, h22)):
        entries = jnp.where(lane == i, value, entries)
    entries_ref[...] = entries[:, 0:5]


def per_device(start_vector, blocks, pattern, trace_map, neighbours, coupling):
    own_cells = start_vector.shape[2]
    own_rows = own_cells // LANES
    parts, subs, reps = lax.axis_size("blk"), lax.axis_size("sub"), lax.axis_size("rep")
    rows = own_rows * parts
    cells = own_cells * parts * subs * reps
    start = start_vector.reshape(own_rows, LANES)
    local_map = trace_map[0]
    blocks, pattern, neighbours, coupling = blocks[0, 0], pattern[0, 0], neighbours[0], coupling[0, 0]
    vmem = pl.BlockSpec(memory_space=pltpu.VMEM)
    params = pltpu.CompilerParams(vmem_limit_bytes=32 * 1024 * 1024)

    def rowed(*shape):
        return jax.ShapeDtypeStruct((*shape, LANES), jnp.float32)

    smem = pl.BlockSpec(memory_space=pltpu.SMEM)

    def from_others(pick):
        got = [
            lax.ppermute(pick(step), "blk", [((i + step) % parts, i) for i in range(parts)])
            for step in range(1, parts)
        ]
        return got[0] if parts == 2 else jnp.concatenate(got, 0)

    slots, block_rows, width = blocks.shape
    own_blocks = block_rows // parts

    def scratch(count):
        return [
            pltpu.VMEM((count, LANES), jnp.float32),
            pltpu.VMEM((count * width // LANES, 2 * LANES), jnp.bfloat16),
        ]

    def shaped(dtype, *shape):
        return jax.ShapeDtypeStruct(shape, dtype)

    long = pl.CostEstimate(flops=1 << 32, bytes_accessed=1 << 20, transcendentals=0)
    others = from_others(lambda step: start[None])

    def rows_of_other(step):
        part = lax.rem(lax.axis_index("blk") + parts - step, parts)
        return lax.dynamic_slice_in_dim(blocks, part * own_blocks, own_blocks, 1)[None]

    other_blocks = from_others(rows_of_other)
    wide = pl.pallas_call(
        widen_kernel,
        out_shape=shaped(jnp.float32, *blocks.shape),
        in_specs=[vmem],
        out_specs=vmem,
        compiler_params=params,
        cost_estimate=long,
        name="wide_blocks",
    )(blocks)
    lines, chosen, chosen_own = pl.pallas_call(
        lines_kernel,
        out_shape=(
            rowed(SUBL),
            shaped(jnp.bfloat16, slots * block_rows, 3 * block_rows),
            shaped(jnp.bfloat16, slots * block_rows, 3 * block_rows),
        ),
        in_specs=[vmem] * 5,
        out_specs=(vmem, vmem, vmem),
        scratch_shapes=[pltpu.VMEM((block_rows, 3 * block_rows), jnp.float32)],
        compiler_params=params,
        cost_estimate=long,
        name="group_lines",
    )(start, local_map, neighbours, coupling, pattern)
    partial, vector = pl.pallas_call(
        first_kernel,
        out_shape=(rowed(subs * parts, rows + SUBL), rowed(rows)),
        in_specs=[vmem] * 5,
        out_specs=(vmem, vmem),
        scratch_shapes=scratch(block_rows),
        compiler_params=params,
        name="first_image",
    )(start, lines, others, wide, chosen)
    group = lax.all_to_all(partial, ("sub", "blk"), 0, 0, tiled=True)
    sums, image, again = pl.pallas_call(
        second_kernel,
        out_shape=(rowed(reps * subs * parts, 1), rowed(own_rows), rowed(own_rows)),
        in_specs=[vmem] * 5 + [smem],
        out_specs=(vmem, vmem, vmem),
        scratch_shapes=[pltpu.VMEM((rows, LANES), jnp.float32), *scratch(own_blocks)],
        compiler_params=params,
        name="second_image",
    )(start, group, wide, other_blocks, chosen_own, neighbours)
    sums = lax.all_to_all(sums, ("rep", "sub", "blk"), 0, 0, tiled=True)
    second, third, entries = pl.pallas_call(
        functools.partial(last_kernel, float(cells)),
        out_shape=(rowed(own_rows), rowed(own_rows), jax.ShapeDtypeStruct((1, 5), jnp.float32)),
        in_specs=[vmem] * 4,
        out_specs=(vmem, vmem, vmem),
        compiler_params=params,
        name="arnoldi_entries",
    )(start, image, again, sums)
    return second.reshape(start_vector.shape), third.reshape(start_vector.shape), entries.reshape(5)


def solution(mesh):
    return jax.shard_map(
        per_device,
        mesh=mesh,
        in_specs=(
            P("rep", "sub", "blk"),
            P("rep", "sub", "blk", None, None),
            P("rep", "sub", None, None),
            P("rep", "sub", "blk"),
            P("rep", "sub", None),
            P("rep", "sub", None, "blk"),
        ),
        out_specs=(P("rep", "sub", "blk"), P("rep", "sub", "blk"), P()),
        check_vma=False,
    )
```

```python
import functools

import jax
import jax.numpy as jnp
from jax import lax
from jax.experimental import pallas as pl
from jax.experimental.pallas import tpu as pltpu
from jax.sharding import PartitionSpec as P

BS = 64
LANES = 128
SUBL = 8
epsilon = 1e-06


def pieces(value):
    high = value.astype(jnp.bfloat16)
    rest = value - high.astype(jnp.float32)
    middle = rest.astype(jnp.bfloat16)
    low = (rest - middle.astype(jnp.float32)).astype(jnp.bfloat16)
    return high, middle, low


def lane_iota(shape):
    return lax.broadcasted_iota(jnp.int32, shape, len(shape) - 1)


def row_iota(shape):
    return lax.broadcasted_iota(jnp.int32, shape, 0)


def choices(pattern_ref, slot):
    block_rows = pattern_ref.shape[1]
    half = block_rows // 2
    place = row_iota((block_rows, block_rows))
    place = jnp.where(place < half, 2 * place, 2 * (place - half) + 1)
    thrice = (block_rows, 3 * block_rows)
    copies = (lane_iota(thrice) % block_rows == row_iota(thrice)).astype(jnp.float32).astype(jnp.bfloat16)
    chosen = (place == pattern_ref[pl.ds(slot, 1), :]).astype(jnp.float32).astype(jnp.bfloat16)
    return lax.dot_general(chosen, copies, (((0,), (0,)), ((), ())), preferred_element_type=jnp.float32)


def block_product(vector, fetch, width, chosen, fold_ref, halves_ref):
    block_rows = fold_ref.shape[0]
    slots = chosen.shape[0] // block_rows
    half = block_rows // 2
    lower = lane_iota(vector.shape) < BS
    turned = pltpu.roll(vector, BS, 1)
    table = jnp.concatenate([jnp.where(lower, vector, turned), jnp.where(lower, turned, vector)], 0)
    table = jnp.concatenate(pieces(table), 0)
    picked = lax.dot_general(chosen, table, (((1,), (0,)), ((), ())), preferred_element_type=jnp.float32)
    ones = (row_iota((2 * LANES, LANES)) % LANES) // BS == lane_iota((2 * LANES, LANES)) % 2
    ones = ones.astype(jnp.float32).astype(jnp.bfloat16)
    pair = (lane_iota((block_rows, LANES)) % BS) // 2
    chunks = width // LANES
    together = chunks // 4
    result = jnp.zeros((block_rows, LANES), jnp.float32)
    for first in range(0, chunks, together):
        for c in range(first, first + together):
            total = None
            for k in range(slots):
                term = fetch(k, pl.ds(c * LANES, LANES)) * picked[k * block_rows : (k + 1) * block_rows]
                total = term if total is None else total + term
            high = total.astype(jnp.bfloat16)
            here = pl.ds(c * block_rows, block_rows)
            halves_ref[here, 0:LANES] = high
            halves_ref[here, LANES : 2 * LANES] = (total - high.astype(jnp.float32)).astype(jnp.bfloat16)
        sums = lax.dot_general(
            halves_ref[pl.ds(first * block_rows, together * block_rows), :],
            ones,
            (((1,), (0,)), ((), ())),
            preferred_element_type=jnp.float32,
        )
        for i in range(together):
            result = jnp.where(pair == first + i, sums[i * block_rows : (i + 1) * block_rows], result)
    fold_ref[...] = result
    even = fold_ref[pl.ds(0, half, stride=2), :]
    odd = fold_ref[pl.ds(1, half, stride=2), :]
    return jnp.where(lane_iota((half, LANES)) < BS, even, odd)


def take_trace(rows, places):
    count = rows.shape[0]
    low = jnp.broadcast_to(places % LANES, (count, LANES))
    picked = jnp.take_along_axis(rows, low, axis=1)
    return jnp.sum(jnp.where(row_iota((count, LANES)) == places // LANES, picked, 0.0), axis=0, keepdims=True)


def spread(values, places, count):
    aimed = jnp.where(row_iota((count, LANES)) == places // LANES, values, 0.0)
    high = aimed.astype(jnp.bfloat16).astype(jnp.float32)
    rest = aimed - high
    middle = rest.astype(jnp.bfloat16).astype(jnp.float32)
    stack = jnp.concatenate([high, middle, rest - middle], 0).astype(jnp.bfloat16)
    target = (row_iota((LANES, LANES)) == places % LANES).astype(jnp.float32).astype(jnp.bfloat16)
    landed = lax.dot_general(stack, target, (((1,), (1,)), ((), ())), preferred_element_type=jnp.float32)
    return landed[0:count] + landed[count : 2 * count] + landed[2 * count : 3 * count]


def lines_kernel(
    start_ref, map_ref, near_ref, coupling_ref, pattern_ref, out_ref, first_ref, second_ref, rows_ref
):
    places = map_ref[...]
    count = coupling_ref.shape[0]
    blk, parts = lax.axis_index("blk"), lax.axis_size("blk")
    lines = [take_trace(start_ref[...], places - blk * start_ref.shape[0] * LANES), places.astype(jnp.float32)]
    lines += [coupling_ref[n : n + 1, :] for n in range(count)]
    near = near_ref[...].astype(jnp.float32)
    lines += [jnp.broadcast_to(near[:, n : n + 1], (1, LANES)) for n in range(count)]
    lines += [jnp.zeros((SUBL - len(lines), LANES), jnp.float32)]
    out_ref[...] = jnp.concatenate(lines, 0)
    all_slots, block_rows = pattern_ref.shape
    slots = all_slots // parts
    own_rows = block_rows // parts
    for step in range(parts):
        for k in range(slots):
            at = step * slots + k
            chosen = choices(pattern_ref, lax.rem(blk + step, parts) * slots + k)
            if step == 0:
                first_ref[k * block_rows : (k + 1) * block_rows, :] = chosen.astype(jnp.bfloat16)
            rows_ref[...] = chosen
            own = rows_ref[pl.ds(pl.multiple_of(blk * own_rows, SUBL), own_rows), :]
            second_ref[at * own_rows : (at + 1) * own_rows, :] = own.astype(jnp.bfloat16)


def send_kernel(blocks_ref, out_ref):
    others, _, own_rows, _ = out_ref.shape
    blk, parts = lax.axis_index("blk"), lax.axis_size("blk")
    for step in range(1, others + 1):
        part = lax.rem(blk + parts - step, parts)
        out_ref[step - 1] = blocks_ref[:, pl.ds(pl.multiple_of(part * own_rows, 16), own_rows), :]


def widen_kernel(blocks_ref, out_ref):
    out_ref[...] = blocks_ref[...].astype(jnp.float32)


def first_kernel(
    start_ref, lines_ref, other_ref, blocks_ref, choices_ref, out_ref, vector_ref, fold_ref, halves_ref
):
    own_rows, rows = start_ref.shape[0], vector_ref.shape[0]
    blk, parts = lax.axis_index("blk"), lax.axis_size("blk")
    for step in range(parts):
        place = lax.rem(blk + step, parts)
        place = pl.ds(pl.multiple_of(place * own_rows, SUBL), own_rows)
        vector_ref[place, :] = other_ref[step - 1] if step else start_ref[...]

    def fetch(k, lanes):
        return blocks_ref[k, :, lanes]

    partial = block_product(
        vector_ref[...], fetch, blocks_ref.shape[2], choices_ref[...], fold_ref, halves_ref
    )
    for device in range(out_ref.shape[0]):
        out_ref[device, 0:rows, :] = partial
        out_ref[device, rows : rows + SUBL, :] = lines_ref[...]


def line(group_ref, device, i):
    first = group_ref.shape[1] - SUBL + i
    return group_ref[device, first : first + 1, :]


def landed(group_ref, sub_at, part, own_rows, count):
    parts = lax.axis_size("blk")
    traces = [line(group_ref, other * parts + part, 0) for other in range(lax.axis_size("sub"))]
    traces = jnp.concatenate(traces, 0)
    names = row_iota(traces.shape).astype(jnp.float32)
    device = sub_at * parts + part
    inflow = jnp.zeros((1, LANES), jnp.float32)
    for n in range(count):
        chosen = jnp.where(names == line(group_ref, device, 2 + count + n), traces, 0.0)
        inflow = inflow + line(group_ref, device, 2 + n) * jnp.sum(chosen, axis=0, keepdims=True)
    places = line(group_ref, device, 1).astype(jnp.int32) - part * own_rows * LANES
    return spread(inflow, places, own_rows), places


def summed(group_ref, sub_at, where):
    parts = lax.axis_size("blk")
    total = group_ref[sub_at * parts, where, :]
    for b in range(1, parts):
        total = total + group_ref[sub_at * parts + b, where, :]
    return total


def down(left, right):
    return jnp.sum(left * right, axis=0, keepdims=True)


def second_kernel(
    start_ref,
    group_ref,
    blocks_ref,
    other_ref,
    choices_ref,
    near_ref,
    out_ref,
    image_ref,
    again_ref,
    whole_ref,
    fold_ref,
    halves_ref,
):
    own_rows = start_ref.shape[0]
    slots, block_rows, width = blocks_ref.shape
    count = near_ref.shape[1]
    sub, blk, parts = lax.axis_index("sub"), lax.axis_index("blk"), lax.axis_size("blk")
    own_blocks = block_rows // parts
    here = pl.ds(pl.multiple_of(blk * own_blocks, 16), own_blocks)
    own = pl.ds(pl.multiple_of(blk * own_rows, SUBL), own_rows)
    inflow = jnp.zeros((1, LANES), jnp.float32)
    for n in range(count):
        source = near_ref[0, n]
        added, places = landed(group_ref, source, blk, own_rows, count)
        trace = take_trace(summed(group_ref, source, own) + added, places)
        inflow = inflow + line(group_ref, sub * parts + blk, 2 + n) * trace
    places = line(group_ref, sub * parts + blk, 1).astype(jnp.int32) - blk * own_rows * LANES
    inflow = spread(inflow, places, own_rows)
    added = [landed(group_ref, sub, part, own_rows, count)[0] for part in range(parts)]
    image = summed(group_ref, sub, pl.ds(0, own_rows * parts)) + jnp.concatenate(added, 0)
    whole_ref[...] = image

    def fetch(k, lanes):
        if k < slots:
            return blocks_ref[k, here, lanes]
        return other_ref[k // slots - 1, k % slots, :, lanes].astype(jnp.float32)

    again = block_product(image, fetch, width, choices_ref[...], fold_ref, halves_ref) + inflow
    again_ref[...] = again
    vector, image = start_ref[...], whole_ref[own, :]
    image_ref[...] = image
    sums = [down(vector, vector), down(vector, image), down(image, image)]
    sums += [down(vector, again), down(image, again), down(again, again)]
    sums = jnp.concatenate([*sums, jnp.zeros((SUBL - 6, LANES), jnp.float32)], 0)
    sums = jnp.sum(sums, axis=1, keepdims=True)
    sums = jnp.where(row_iota((SUBL, LANES)) == lane_iota((SUBL, LANES)), sums, 0.0)
    sums = jnp.sum(sums, axis=0, keepdims=True)
    for device in range(out_ref.shape[0]):
        out_ref[device] = sums


def last_kernel(cells, start_ref, image_ref, again_ref, sums_ref, second_ref, third_ref, entries_ref):
    sums = jnp.sum(sums_ref[...], axis=0) / cells

    def whole(i):
        return jnp.broadcast_to(sums[:, i : i + 1], (1, LANES))

    vv, vw, ww, vy, wy, yy = (whole(i) for i in range(6))
    norm_square = vv + epsilon
    inverse = 1.0 / norm_square
    h11 = vw * inverse
    skew = vy - h11 * vw
    first_square = jnp.maximum(ww - 2.0 * h11 * vw + h11 * h11 * vv, 0.0) * inverse + epsilon
    over_first = lax.rsqrt(first_square)
    h21 = first_square * over_first
    scale = lax.rsqrt(norm_square) * over_first
    h12 = skew * inverse * over_first
    h22 = (wy - h11 * (ww + skew)) * scale * scale
    near = h11 + h22
    far = skew * inverse - h11 * h22
    second_square = yy + near * near * ww + far * far * vv + 2.0 * (near * far * vw - near * wy - far * vy)
    second_square = jnp.maximum(second_square, 0.0) * scale * scale + epsilon
    over_second = lax.rsqrt(second_square)
    h32 = second_square * over_second

    vector, image = start_ref[...], image_ref[...]
    second_ref[...] = (image - h11 * vector) * scale
    third_ref[...] = (again_ref[...] - near * image - far * vector) * (scale * over_second)
    lane = lane_iota((1, LANES))
    entries = h32
    for i, value in enumerate((h11, h21, h12, h22)):
        entries = jnp.where(lane == i, value, entries)
    entries_ref[...] = entries[:, 0:5]


def per_device(start_vector, blocks, pattern, trace_map, neighbours, coupling):
    own_cells = start_vector.shape[2]
    own_rows = own_cells // LANES
    parts, subs, reps = lax.axis_size("blk"), lax.axis_size("sub"), lax.axis_size("rep")
    rows = own_rows * parts
    cells = own_cells * parts * subs * reps
    start = start_vector.reshape(own_rows, LANES)
    local_map = trace_map[0]
    blocks, pattern, neighbours, coupling = blocks[0, 0], pattern[0, 0], neighbours[0], coupling[0, 0]
    vmem = pl.BlockSpec(memory_space=pltpu.VMEM)
    params = pltpu.CompilerParams(vmem_limit_bytes=32 * 1024 * 1024)

    def rowed(*shape):
        return jax.ShapeDtypeStruct((*shape, LANES), jnp.float32)

    smem = pl.BlockSpec(memory_space=pltpu.SMEM)

    def from_others(pick):
        got = [
            lax.ppermute(pick(step), "blk", [((i + step) % parts, i) for i in range(parts)])
            for step in range(1, parts)
        ]
        return got[0] if parts == 2 else jnp.concatenate(got, 0)

    slots, block_rows, width = blocks.shape
    own_blocks = block_rows // parts

    def scratch(count):
        return [
            pltpu.VMEM((count, LANES), jnp.float32),
            pltpu.VMEM((count * width // LANES, 2 * LANES), jnp.bfloat16),
        ]

    def shaped(dtype, *shape):
        return jax.ShapeDtypeStruct(shape, dtype)

    long = pl.CostEstimate(flops=1 << 32, bytes_accessed=1 << 20, transcendentals=0)
    others = from_others(lambda step: start[None])

    send = pl.pallas_call(
        send_kernel,
        out_shape=shaped(jnp.bfloat16, parts - 1, slots, own_blocks, width),
        in_specs=[vmem],
        out_specs=vmem,
        compiler_params=params,
        name="send_blocks",
    )(blocks)
    other_blocks = from_others(lambda step: send if parts == 2 else send[step - 1 : step])
    wide = pl.pallas_call(
        widen_kernel,
        out_shape=shaped(jnp.float32, *blocks.shape),
        in_specs=[vmem],
        out_specs=vmem,
        compiler_params=params,
        cost_estimate=long,
        name="wide_blocks",
    )(blocks)
    lines, chosen, chosen_own = pl.pallas_call(
        lines_kernel,
        out_shape=(
            rowed(SUBL),
            shaped(jnp.bfloat16, slots * block_rows, 3 * block_rows),
            shaped(jnp.bfloat16, slots * block_rows, 3 * block_rows),
        ),
        in_specs=[vmem] * 5,
        out_specs=(vmem, vmem, vmem),
        scratch_shapes=[pltpu.VMEM((block_rows, 3 * block_rows), jnp.float32)],
        compiler_params=params,
        cost_estimate=long,
        name="group_lines",
    )(start, local_map, neighbours, coupling, pattern)
    partial, vector = pl.pallas_call(
        first_kernel,
        out_shape=(rowed(subs * parts, rows + SUBL), rowed(rows)),
        in_specs=[vmem] * 5,
        out_specs=(vmem, vmem),
        scratch_shapes=scratch(block_rows),
        compiler_params=params,
        name="first_image",
    )(start, lines, others, wide, chosen)
    group = lax.all_to_all(partial, ("sub", "blk"), 0, 0, tiled=True)
    sums, image, again = pl.pallas_call(
        second_kernel,
        out_shape=(rowed(reps * subs * parts, 1), rowed(own_rows), rowed(own_rows)),
        in_specs=[vmem] * 5 + [smem],
        out_specs=(vmem, vmem, vmem),
        scratch_shapes=[pltpu.VMEM((rows, LANES), jnp.float32), *scratch(own_blocks)],
        compiler_params=params,
        name="second_image",
    )(start, group, wide, other_blocks, chosen_own, neighbours)
    sums = lax.all_to_all(sums, ("rep", "sub", "blk"), 0, 0, tiled=True)
    second, third, entries = pl.pallas_call(
        functools.partial(last_kernel, float(cells)),
        out_shape=(rowed(own_rows), rowed(own_rows), jax.ShapeDtypeStruct((1, 5), jnp.float32)),
        in_specs=[vmem] * 4,
        out_specs=(vmem, vmem, vmem),
        compiler_params=params,
        name="arnoldi_entries",
    )(start, image, again, sums)
    return second.reshape(start_vector.shape), third.reshape(start_vector.shape), entries.reshape(5)


def solution(mesh):
    return jax.shard_map(
        per_device,
        mesh=mesh,
        in_specs=(
            P("rep", "sub", "blk"),
            P("rep", "sub", "blk", None, None),
            P("rep", "sub", None, None),
            P("rep", "sub", "blk"),
            P("rep", "sub", None),
            P("rep", "sub", None, "blk"),
        ),
        out_specs=(P("rep", "sub", "blk"), P("rep", "sub", "blk"), P()),
        check_vma=False,
    )
```

```python
import functools

import jax
import jax.numpy as jnp
from jax import lax
from jax.experimental import pallas as pl
from jax.experimental.pallas import tpu as pltpu
from jax.sharding import PartitionSpec as P

BS = 64
LANES = 128
SUBL = 8
epsilon = 1e-06


def pieces(value):
    high = value.astype(jnp.bfloat16)
    rest = value - high.astype(jnp.float32)
    middle = rest.astype(jnp.bfloat16)
    low = (rest - middle.astype(jnp.float32)).astype(jnp.bfloat16)
    return high, middle, low


def lane_iota(shape):
    return lax.broadcasted_iota(jnp.int32, shape, len(shape) - 1)


def row_iota(shape):
    return lax.broadcasted_iota(jnp.int32, shape, 0)


def choices(pattern_ref, slot):
    block_rows = pattern_ref.shape[1]
    half = block_rows // 2
    place = row_iota((block_rows, block_rows))
    place = jnp.where(place < half, 2 * place, 2 * (place - half) + 1)
    thrice = (block_rows, 3 * block_rows)
    copies = (lane_iota(thrice) % block_rows == row_iota(thrice)).astype(jnp.float32).astype(jnp.bfloat16)
    chosen = (place == pattern_ref[pl.ds(slot, 1), :]).astype(jnp.float32).astype(jnp.bfloat16)
    return lax.dot_general(chosen, copies, (((0,), (0,)), ((), ())), preferred_element_type=jnp.float32)


def block_product(vector, fetch, width, chosen, fold_ref, halves_ref):
    block_rows = fold_ref.shape[0]
    slots = chosen.shape[0] // block_rows
    half = block_rows // 2
    lower = lane_iota(vector.shape) < BS
    turned = pltpu.roll(vector, BS, 1)
    table = jnp.concatenate([jnp.where(lower, vector, turned), jnp.where(lower, turned, vector)], 0)
    table = jnp.concatenate(pieces(table), 0)
    picked = lax.dot_general(chosen, table, (((1,), (0,)), ((), ())), preferred_element_type=jnp.float32)
    ones = (row_iota((2 * LANES, LANES)) % LANES) // BS == lane_iota((2 * LANES, LANES)) % 2
    ones = ones.astype(jnp.float32).astype(jnp.bfloat16)
    pair = (lane_iota((block_rows, LANES)) % BS) // 2
    chunks = width // LANES
    together = chunks // 4
    result = jnp.zeros((block_rows, LANES), jnp.float32)
    for first in range(0, chunks, together):
        for c in range(first, first + together):
            total = None
            for k in range(slots):
                term = fetch(k, pl.ds(c * LANES, LANES)) * picked[k * block_rows : (k + 1) * block_rows]
                total = term if total is None else total + term
            high = total.astype(jnp.bfloat16)
            here = pl.ds(c * block_rows, block_rows)
            halves_ref[here, 0:LANES] = high
            halves_ref[here, LANES : 2 * LANES] = (total - high.astype(jnp.float32)).astype(jnp.bfloat16)
        sums = lax.dot_general(
            halves_ref[pl.ds(first * block_rows, together * block_rows), :],
            ones,
            (((1,), (0,)), ((), ())),
            preferred_element_type=jnp.float32,
        )
        for i in range(together):
            result = jnp.where(pair == first + i, sums[i * block_rows : (i + 1) * block_rows], result)
    fold_ref[...] = result
    even = fold_ref[pl.ds(0, half, stride=2), :]
    odd = fold_ref[pl.ds(1, half, stride=2), :]
    return jnp.where(lane_iota((half, LANES)) < BS, even, odd)


def take_trace(rows, places):
    count = rows.shape[0]
    low = jnp.broadcast_to(places % LANES, (count, LANES))
    picked = jnp.take_along_axis(rows, low, axis=1)
    return jnp.sum(jnp.where(row_iota((count, LANES)) == places // LANES, picked, 0.0), axis=0, keepdims=True)


def spread(values, places, count):
    aimed = jnp.where(row_iota((count, LANES)) == places // LANES, values, 0.0)
    high = aimed.astype(jnp.bfloat16).astype(jnp.float32)
    rest = aimed - high
    middle = rest.astype(jnp.bfloat16).astype(jnp.float32)
    stack = jnp.concatenate([high, middle, rest - middle], 0).astype(jnp.bfloat16)
    target = (row_iota((LANES, LANES)) == places % LANES).astype(jnp.float32).astype(jnp.bfloat16)
    landed = lax.dot_general(stack, target, (((1,), (1,)), ((), ())), preferred_element_type=jnp.float32)
    return landed[0:count] + landed[count : 2 * count] + landed[2 * count : 3 * count]


def lines_kernel(
    start_ref, map_ref, near_ref, coupling_ref, pattern_ref, out_ref, first_ref, second_ref, rows_ref
):
    places = map_ref[...]
    count = coupling_ref.shape[0]
    blk, parts = lax.axis_index("blk"), lax.axis_size("blk")
    lines = [take_trace(start_ref[...], places - blk * start_ref.shape[0] * LANES), places.astype(jnp.float32)]
    lines += [coupling_ref[n : n + 1, :] for n in range(count)]
    near = near_ref[...].astype(jnp.float32)
    lines += [jnp.broadcast_to(near[:, n : n + 1], (1, LANES)) for n in range(count)]
    lines += [jnp.zeros((SUBL - len(lines), LANES), jnp.float32)]
    out_ref[...] = jnp.concatenate(lines, 0)
    all_slots, block_rows = pattern_ref.shape
    slots = all_slots // parts
    own_rows = block_rows // parts
    for step in range(parts):
        for k in range(slots):
            at = step * slots + k
            chosen = choices(pattern_ref, lax.rem(blk + step, parts) * slots + k)
            if step == 0:
                first_ref[k * block_rows : (k + 1) * block_rows, :] = chosen.astype(jnp.bfloat16)
            rows_ref[...] = chosen
            own = rows_ref[pl.ds(pl.multiple_of(blk * own_rows, SUBL), own_rows), :]
            second_ref[at * own_rows : (at + 1) * own_rows, :] = own.astype(jnp.bfloat16)


def send_kernel(blocks_ref, out_ref):
    others, _, own_rows, _ = out_ref.shape
    blk, parts = lax.axis_index("blk"), lax.axis_size("blk")
    for step in range(1, others + 1):
        part = lax.rem(blk + parts - step, parts)
        out_ref[step - 1] = blocks_ref[:, pl.ds(pl.multiple_of(part * own_rows, 16), own_rows), :]


def widen_kernel(blocks_ref, out_ref):
    out_ref[...] = blocks_ref[...].astype(jnp.float32)


def first_kernel(
    start_ref, lines_ref, other_ref, blocks_ref, choices_ref, out_ref, vector_ref, fold_ref, halves_ref
):
    own_rows, rows = start_ref.shape[0], vector_ref.shape[0]
    blk, parts = lax.axis_index("blk"), lax.axis_size("blk")
    for step in range(parts):
        place = lax.rem(blk + step, parts)
        place = pl.ds(pl.multiple_of(place * own_rows, SUBL), own_rows)
        vector_ref[place, :] = other_ref[step - 1] if step else start_ref[...]

    def fetch(k, lanes):
        return blocks_ref[k, :, lanes]

    partial = block_product(
        vector_ref[...], fetch, blocks_ref.shape[2], choices_ref[...], fold_ref, halves_ref
    )
    for device in range(out_ref.shape[0]):
        out_ref[device, 0:rows, :] = partial
        out_ref[device, rows : rows + SUBL, :] = lines_ref[...]


def line(group_ref, device, i):
    first = group_ref.shape[1] - SUBL + i
    return group_ref[device, first : first + 1, :]


def landed(group_ref, sub_at, part, own_rows, count):
    parts = lax.axis_size("blk")
    traces = [line(group_ref, other * parts + part, 0) for other in range(lax.axis_size("sub"))]
    traces = jnp.concatenate(traces, 0)
    names = row_iota(traces.shape).astype(jnp.float32)
    device = sub_at * parts + part
    inflow = jnp.zeros((1, LANES), jnp.float32)
    for n in range(count):
        chosen = jnp.where(names == line(group_ref, device, 2 + count + n), traces, 0.0)
        inflow = inflow + line(group_ref, device, 2 + n) * jnp.sum(chosen, axis=0, keepdims=True)
    places = line(group_ref, device, 1).astype(jnp.int32) - part * own_rows * LANES
    return spread(inflow, places, own_rows), places


def summed(group_ref, sub_at, where):
    parts = lax.axis_size("blk")
    total = group_ref[sub_at * parts, where, :]
    for b in range(1, parts):
        total = total + group_ref[sub_at * parts + b, where, :]
    return total


def down(left, right):
    return jnp.sum(left * right, axis=0, keepdims=True)


def second_kernel(
    start_ref,
    group_ref,
    blocks_ref,
    other_ref,
    first_ref,
    second_ref,
    near_ref,
    base_ref,
    give_ref,
    image_ref,
    whole_ref,
    fold_ref,
    halves_ref,
    own_fold_ref,
    own_halves_ref,
):
    own_rows = start_ref.shape[0]
    slots, block_rows, width = blocks_ref.shape
    count = near_ref.shape[1]
    sub, blk, parts = lax.axis_index("sub"), lax.axis_index("blk"), lax.axis_size("blk")
    odd = lax.rem(lax.axis_index("rep"), 2)
    own_blocks = block_rows // parts
    here = pl.ds(pl.multiple_of(blk * own_blocks, 16), own_blocks)
    own = pl.ds(pl.multiple_of(blk * own_rows, SUBL), own_rows)
    inflow = jnp.zeros((1, LANES), jnp.float32)
    for n in range(count):
        source = near_ref[0, n]
        added, places = landed(group_ref, source, blk, own_rows, count)
        trace = take_trace(summed(group_ref, source, own) + added, places)
        inflow = inflow + line(group_ref, sub * parts + blk, 2 + n) * trace
    places = line(group_ref, sub * parts + blk, 1).astype(jnp.int32) - blk * own_rows * LANES
    base_ref[...] = spread(inflow, places, own_rows)
    added = [landed(group_ref, sub, part, own_rows, count)[0] for part in range(parts)]
    whole_ref[...] = summed(group_ref, sub, pl.ds(0, own_rows * parts)) + jnp.concatenate(added, 0)
    image_ref[...] = whole_ref[own, :]

    def fetch_own(k, lanes):
        if k < slots:
            return blocks_ref[k, here, lanes]
        return other_ref[k // slots - 1, k % slots, :, lanes].astype(jnp.float32)

    def fetch(k, lanes):
        return blocks_ref[k, :, lanes]

    @pl.when(odd == 0)
    def _():
        product = block_product(whole_ref[...], fetch_own, width, second_ref[...], own_fold_ref, own_halves_ref)
        base_ref[...] = base_ref[...] + product
        give_ref[...] = jnp.zeros(give_ref.shape, jnp.float32)

    @pl.when(odd == 1)
    def _():
        product = block_product(whole_ref[...], fetch, width, first_ref[...], fold_ref, halves_ref)
        whole_ref[...] = product
        base_ref[...] = base_ref[...] + whole_ref[own, :]
        for step in range(1, parts):
            part = lax.rem(blk + parts - step, parts)
            give_ref[step - 1] = whole_ref[pl.ds(pl.multiple_of(part * own_rows, SUBL), own_rows), :]


def sums_kernel(start_ref, image_ref, base_ref, other_ref, out_ref, again_ref):
    again = base_ref[...]
    for step in range(other_ref.shape[0]):
        again = again + other_ref[step]
    again_ref[...] = again
    vector, image = start_ref[...], image_ref[...]
    sums = [down(vector, vector), down(vector, image), down(image, image)]
    sums += [down(vector, again), down(image, again), down(again, again)]
    sums = jnp.concatenate([*sums, jnp.zeros((SUBL - 6, LANES), jnp.float32)], 0)
    sums = jnp.sum(sums, axis=1, keepdims=True)
    sums = jnp.where(row_iota((SUBL, LANES)) == lane_iota((SUBL, LANES)), sums, 0.0)
    sums = jnp.sum(sums, axis=0, keepdims=True)
    for device in range(out_ref.shape[0]):
        out_ref[device] = sums


def last_kernel(cells, start_ref, image_ref, again_ref, sums_ref, second_ref, third_ref, entries_ref):
    sums = jnp.sum(sums_ref[...], axis=0) / cells

    def whole(i):
        return jnp.broadcast_to(sums[:, i : i + 1], (1, LANES))

    vv, vw, ww, vy, wy, yy = (whole(i) for i in range(6))
    norm_square = vv + epsilon
    inverse = 1.0 / norm_square
    h11 = vw * inverse
    skew = vy - h11 * vw
    first_square = jnp.maximum(ww - 2.0 * h11 * vw + h11 * h11 * vv, 0.0) * inverse + epsilon
    over_first = lax.rsqrt(first_square)
    h21 = first_square * over_first
    scale = lax.rsqrt(norm_square) * over_first
    h12 = skew * inverse * over_first
    h22 = (wy - h11 * (ww + skew)) * scale * scale
    near = h11 + h22
    far = skew * inverse - h11 * h22
    second_square = yy + near * near * ww + far * far * vv + 2.0 * (near * far * vw - near * wy - far * vy)
    second_square = jnp.maximum(second_square, 0.0) * scale * scale + epsilon
    over_second = lax.rsqrt(second_square)
    h32 = second_square * over_second

    vector, image = start_ref[...], image_ref[...]
    second_ref[...] = (image - h11 * vector) * scale
    third_ref[...] = (again_ref[...] - near * image - far * vector) * (scale * over_second)
    lane = lane_iota((1, LANES))
    entries = h32
    for i, value in enumerate((h11, h21, h12, h22)):
        entries = jnp.where(lane == i, value, entries)
    entries_ref[...] = entries[:, 0:5]


def per_device(start_vector, blocks, pattern, trace_map, neighbours, coupling):
    own_cells = start_vector.shape[2]
    own_rows = own_cells // LANES
    parts, subs, reps = lax.axis_size("blk"), lax.axis_size("sub"), lax.axis_size("rep")
    rows = own_rows * parts
    cells = own_cells * parts * subs * reps
    start = start_vector.reshape(own_rows, LANES)
    local_map = trace_map[0]
    blocks, pattern, neighbours, coupling = blocks[0, 0], pattern[0, 0], neighbours[0], coupling[0, 0]
    vmem = pl.BlockSpec(memory_space=pltpu.VMEM)
    params = pltpu.CompilerParams(vmem_limit_bytes=32 * 1024 * 1024)

    def rowed(*shape):
        return jax.ShapeDtypeStruct((*shape, LANES), jnp.float32)

    smem = pl.BlockSpec(memory_space=pltpu.SMEM)

    def from_others(pick, members=range(reps)):
        got = []
        for step in range(1, parts):
            route = [((i + step) % parts * reps + r, i * reps + r) for r in members for i in range(parts)]
            got.append(lax.ppermute(pick(step), ("blk", "rep"), route))
        return got[0] if parts == 2 else jnp.concatenate(got, 0)

    slots, block_rows, width = blocks.shape
    own_blocks = block_rows // parts

    def scratch(count):
        return [
            pltpu.VMEM((count, LANES), jnp.float32),
            pltpu.VMEM((count * width // LANES, 2 * LANES), jnp.bfloat16),
        ]

    def shaped(dtype, *shape):
        return jax.ShapeDtypeStruct(shape, dtype)

    long = pl.CostEstimate(flops=1 << 32, bytes_accessed=1 << 20, transcendentals=0)
    others = from_others(lambda step: start[None])

    send = pl.pallas_call(
        send_kernel,
        out_shape=shaped(jnp.bfloat16, parts - 1, slots, own_blocks, width),
        in_specs=[vmem],
        out_specs=vmem,
        compiler_params=params,
        name="send_blocks",
    )(blocks)
    other_blocks = from_others(lambda step: send if parts == 2 else send[step - 1 : step], range(0, reps, 2))
    wide = pl.pallas_call(
        widen_kernel,
        out_shape=shaped(jnp.float32, *blocks.shape),
        in_specs=[vmem],
        out_specs=vmem,
        compiler_params=params,
        cost_estimate=long,
        name="wide_blocks",
    )(blocks)
    lines, chosen, chosen_own = pl.pallas_call(
        lines_kernel,
        out_shape=(
            rowed(SUBL),
            shaped(jnp.bfloat16, slots * block_rows, 3 * block_rows),
            shaped(jnp.bfloat16, slots * block_rows, 3 * block_rows),
        ),
        in_specs=[vmem] * 5,
        out_specs=(vmem, vmem, vmem),
        scratch_shapes=[pltpu.VMEM((block_rows, 3 * block_rows), jnp.float32)],
        compiler_params=params,
        cost_estimate=long,
        name="group_lines",
    )(start, local_map, neighbours, coupling, pattern)
    partial, vector = pl.pallas_call(
        first_kernel,
        out_shape=(rowed(subs * parts, rows + SUBL), rowed(rows)),
        in_specs=[vmem] * 5,
        out_specs=(vmem, vmem),
        scratch_shapes=scratch(block_rows),
        compiler_params=params,
        name="first_image",
    )(start, lines, others, wide, chosen)
    group = lax.all_to_all(partial, ("sub", "blk"), 0, 0, tiled=True)
    base, give, image = pl.pallas_call(
        second_kernel,
        out_shape=(rowed(own_rows), rowed(parts - 1, own_rows), rowed(own_rows)),
        in_specs=[vmem] * 6 + [smem],
        out_specs=(vmem, vmem, vmem),
        scratch_shapes=[pltpu.VMEM((rows, LANES), jnp.float32), *scratch(block_rows), *scratch(own_blocks)],
        compiler_params=params,
        name="second_image",
    )(start, group, wide, other_blocks, chosen, chosen_own, neighbours)
    given = from_others(lambda step: give if parts == 2 else give[step - 1 : step], range(1, reps, 2))
    sums, again = pl.pallas_call(
        sums_kernel,
        out_shape=(rowed(reps * subs * parts, 1), rowed(own_rows)),
        in_specs=[vmem] * 4,
        out_specs=(vmem, vmem),
        compiler_params=params,
        name="own_sums",
    )(start, image, base, given)
    sums = lax.all_to_all(sums, ("rep", "sub", "blk"), 0, 0, tiled=True)
    second, third, entries = pl.pallas_call(
        functools.partial(last_kernel, float(cells)),
        out_shape=(rowed(own_rows), rowed(own_rows), jax.ShapeDtypeStruct((1, 5), jnp.float32)),
        in_specs=[vmem] * 4,
        out_specs=(vmem, vmem, vmem),
        compiler_params=params,
        name="arnoldi_entries",
    )(start, image, again, sums)
    return second.reshape(start_vector.shape), third.reshape(start_vector.shape), entries.reshape(5)


def solution(mesh):
    return jax.shard_map(
        per_device,
        mesh=mesh,
        in_specs=(
            P("rep", "sub", "blk"),
            P("rep", "sub", "blk", None, None),
            P("rep", "sub", None, None),
            P("rep", "sub", "blk"),
            P("rep", "sub", None),
            P("rep", "sub", None, "blk"),
        ),
        out_specs=(P("rep", "sub", "blk"), P("rep", "sub", "blk"), P()),
        check_vma=False,
    )
```

```python
import functools

import jax
import jax.numpy as jnp
from jax import lax
from jax.experimental import pallas as pl
from jax.experimental.pallas import tpu as pltpu
from jax.sharding import PartitionSpec as P

BS = 64
LANES = 128
SUBL = 8
epsilon = 1e-06


def pieces(value):
    high = value.astype(jnp.bfloat16)
    rest = value - high.astype(jnp.float32)
    middle = rest.astype(jnp.bfloat16)
    low = (rest - middle.astype(jnp.float32)).astype(jnp.bfloat16)
    return high, middle, low


def lane_iota(shape):
    return lax.broadcasted_iota(jnp.int32, shape, len(shape) - 1)


def row_iota(shape):
    return lax.broadcasted_iota(jnp.int32, shape, 0)


def choices(pattern_ref, slot):
    block_rows = pattern_ref.shape[1]
    half = block_rows // 2
    place = row_iota((block_rows, block_rows))
    place = jnp.where(place < half, 2 * place, 2 * (place - half) + 1)
    thrice = (block_rows, 3 * block_rows)
    copies = (lane_iota(thrice) % block_rows == row_iota(thrice)).astype(jnp.float32).astype(jnp.bfloat16)
    chosen = (place == pattern_ref[pl.ds(slot, 1), :]).astype(jnp.float32).astype(jnp.bfloat16)
    return lax.dot_general(chosen, copies, (((0,), (0,)), ((), ())), preferred_element_type=jnp.float32)


def block_product(vector, fetch, width, chosen, fold_ref, halves_ref):
    block_rows = fold_ref.shape[0]
    slots = chosen.shape[0] // block_rows
    half = block_rows // 2
    lower = lane_iota(vector.shape) < BS
    turned = pltpu.roll(vector, BS, 1)
    table = jnp.concatenate([jnp.where(lower, vector, turned), jnp.where(lower, turned, vector)], 0)
    table = jnp.concatenate(pieces(table), 0)
    picked = lax.dot_general(chosen, table, (((1,), (0,)), ((), ())), preferred_element_type=jnp.float32)
    ones = (row_iota((2 * LANES, LANES)) % LANES) // BS == lane_iota((2 * LANES, LANES)) % 2
    ones = ones.astype(jnp.float32).astype(jnp.bfloat16)
    pair = (lane_iota((block_rows, LANES)) % BS) // 2
    chunks = width // LANES
    together = chunks // 4
    result = jnp.zeros((block_rows, LANES), jnp.float32)
    for first in range(0, chunks, together):
        for c in range(first, first + together):
            total = None
            for k in range(slots):
                term = fetch(k, pl.ds(c * LANES, LANES)) * picked[k * block_rows : (k + 1) * block_rows]
                total = term if total is None else total + term
            high = total.astype(jnp.bfloat16)
            here = pl.ds(c * block_rows, block_rows)
            halves_ref[here, 0:LANES] = high
            halves_ref[here, LANES : 2 * LANES] = (total - high.astype(jnp.float32)).astype(jnp.bfloat16)
        sums = lax.dot_general(
            halves_ref[pl.ds(first * block_rows, together * block_rows), :],
            ones,
            (((1,), (0,)), ((), ())),
            preferred_element_type=jnp.float32,
        )
        for i in range(together):
            result = jnp.where(pair == first + i, sums[i * block_rows : (i + 1) * block_rows], result)
    fold_ref[...] = result
    even = fold_ref[pl.ds(0, half, stride=2), :]
    odd = fold_ref[pl.ds(1, half, stride=2), :]
    return jnp.where(lane_iota((half, LANES)) < BS, even, odd)


def take_trace(rows, places):
    count = rows.shape[0]
    low = jnp.broadcast_to(places % LANES, (count, LANES))
    picked = jnp.take_along_axis(rows, low, axis=1)
    return jnp.sum(jnp.where(row_iota((count, LANES)) == places // LANES, picked, 0.0), axis=0, keepdims=True)


def spread(values, places, count):
    aimed = jnp.where(row_iota((count, LANES)) == places // LANES, values, 0.0)
    high = aimed.astype(jnp.bfloat16).astype(jnp.float32)
    rest = aimed - high
    middle = rest.astype(jnp.bfloat16).astype(jnp.float32)
    stack = jnp.concatenate([high, middle, rest - middle], 0).astype(jnp.bfloat16)
    target = (row_iota((LANES, LANES)) == places % LANES).astype(jnp.float32).astype(jnp.bfloat16)
    landed = lax.dot_general(stack, target, (((1,), (1,)), ((), ())), preferred_element_type=jnp.float32)
    return landed[0:count] + landed[count : 2 * count] + landed[2 * count : 3 * count]


def lines_kernel(
    start_ref, map_ref, near_ref, coupling_ref, pattern_ref, out_ref, first_ref, second_ref, rows_ref
):
    places = map_ref[...]
    count = coupling_ref.shape[0]
    blk, parts = lax.axis_index("blk"), lax.axis_size("blk")
    lines = [take_trace(start_ref[...], places - blk * start_ref.shape[0] * LANES), places.astype(jnp.float32)]
    lines += [coupling_ref[n : n + 1, :] for n in range(count)]
    near = near_ref[...].astype(jnp.float32)
    lines += [jnp.broadcast_to(near[:, n : n + 1], (1, LANES)) for n in range(count)]
    lines += [jnp.zeros((SUBL - len(lines), LANES), jnp.float32)]
    out_ref[...] = jnp.concatenate(lines, 0)
    all_slots, block_rows = pattern_ref.shape
    slots = all_slots // parts
    own_rows = block_rows // parts
    for step in range(parts):
        for k in range(slots):
            at = step * slots + k
            chosen = choices(pattern_ref, lax.rem(blk + step, parts) * slots + k)
            if step == 0:
                first_ref[k * block_rows : (k + 1) * block_rows, :] = chosen.astype(jnp.bfloat16)
            rows_ref[...] = chosen
            own = rows_ref[pl.ds(pl.multiple_of(blk * own_rows, SUBL), own_rows), :]
            second_ref[at * own_rows : (at + 1) * own_rows, :] = own.astype(jnp.bfloat16)


def send_kernel(blocks_ref, out_ref):
    others, _, own_rows, _ = out_ref.shape
    blk, parts = lax.axis_index("blk"), lax.axis_size("blk")
    for step in range(1, others + 1):
        part = lax.rem(blk + parts - step, parts)
        out_ref[step - 1] = blocks_ref[:, pl.ds(pl.multiple_of(part * own_rows, 16), own_rows), :]


def widen_kernel(blocks_ref, out_ref):
    out_ref[...] = blocks_ref[...].astype(jnp.float32)


def first_kernel(
    start_ref, lines_ref, other_ref, blocks_ref, choices_ref, out_ref, vector_ref, fold_ref, halves_ref
):
    own_rows, rows = start_ref.shape[0], vector_ref.shape[0]
    blk, parts = lax.axis_index("blk"), lax.axis_size("blk")
    for step in range(parts):
        place = lax.rem(blk + step, parts)
        place = pl.ds(pl.multiple_of(place * own_rows, SUBL), own_rows)
        vector_ref[place, :] = other_ref[step - 1] if step else start_ref[...]

    def fetch(k, lanes):
        return blocks_ref[k, :, lanes]

    partial = block_product(
        vector_ref[...], fetch, blocks_ref.shape[2], choices_ref[...], fold_ref, halves_ref
    )
    for device in range(out_ref.shape[0]):
        out_ref[device, 0:rows, :] = partial
        out_ref[device, rows : rows + SUBL, :] = lines_ref[...]


def line(group_ref, device, i):
    first = group_ref.shape[1] - SUBL + i
    return group_ref[device, first : first + 1, :]


def landed(group_ref, sub_at, part, own_rows, count):
    parts = lax.axis_size("blk")
    traces = [line(group_ref, other * parts + part, 0) for other in range(lax.axis_size("sub"))]
    traces = jnp.concatenate(traces, 0)
    names = row_iota(traces.shape).astype(jnp.float32)
    device = sub_at * parts + part
    inflow = jnp.zeros((1, LANES), jnp.float32)
    for n in range(count):
        chosen = jnp.where(names == line(group_ref, device, 2 + count + n), traces, 0.0)
        inflow = inflow + line(group_ref, device, 2 + n) * jnp.sum(chosen, axis=0, keepdims=True)
    places = line(group_ref, device, 1).astype(jnp.int32) - part * own_rows * LANES
    return spread(inflow, places, own_rows), places


def summed(group_ref, sub_at, where):
    parts = lax.axis_size("blk")
    total = group_ref[sub_at * parts, where, :]
    for b in range(1, parts):
        total = total + group_ref[sub_at * parts + b, where, :]
    return total


def down(left, right):
    return jnp.sum(left * right, axis=0, keepdims=True)


def second_kernel(
    start_ref,
    group_ref,
    blocks_ref,
    other_ref,
    first_ref,
    second_ref,
    near_ref,
    base_ref,
    give_ref,
    image_ref,
    whole_ref,
    fold_ref,
    halves_ref,
    own_fold_ref,
    own_halves_ref,
):
    own_rows = start_ref.shape[0]
    slots, block_rows, width = blocks_ref.shape
    count = near_ref.shape[1]
    sub, blk, parts = lax.axis_index("sub"), lax.axis_index("blk"), lax.axis_size("blk")
    odd = lax.rem(lax.axis_index("rep"), 2)
    own_blocks = block_rows // parts
    here = pl.ds(pl.multiple_of(blk * own_blocks, 16), own_blocks)
    own = pl.ds(pl.multiple_of(blk * own_rows, SUBL), own_rows)
    inflow = jnp.zeros((1, LANES), jnp.float32)
    for n in range(count):
        source = near_ref[0, n]
        added, places = landed(group_ref, source, blk, own_rows, count)
        trace = take_trace(summed(group_ref, source, own) + added, places)
        inflow = inflow + line(group_ref, sub * parts + blk, 2 + n) * trace
    places = line(group_ref, sub * parts + blk, 1).astype(jnp.int32) - blk * own_rows * LANES
    base_ref[...] = spread(inflow, places, own_rows)
    added = [landed(group_ref, sub, part, own_rows, count)[0] for part in range(parts)]
    whole_ref[...] = summed(group_ref, sub, pl.ds(0, own_rows * parts)) + jnp.concatenate(added, 0)
    image_ref[...] = whole_ref[own, :]

    def fetch_own(k, lanes):
        if k < slots:
            return blocks_ref[k, here, lanes]
        return other_ref[k // slots - 1, k % slots, :, lanes].astype(jnp.float32)

    def fetch(k, lanes):
        return blocks_ref[k, :, lanes]

    @pl.when(odd == 0)
    def _():
        product = block_product(whole_ref[...], fetch_own, width, second_ref[...], own_fold_ref, own_halves_ref)
        base_ref[...] = base_ref[...] + product
        give_ref[...] = jnp.zeros(give_ref.shape, jnp.float32)

    @pl.when(odd == 1)
    def _():
        product = block_product(whole_ref[...], fetch, width, first_ref[...], fold_ref, halves_ref)
        whole_ref[...] = product
        base_ref[...] = base_ref[...] + whole_ref[own, :]
        for step in range(1, parts):
            part = lax.rem(blk + parts - step, parts)
            give_ref[step - 1] = whole_ref[pl.ds(pl.multiple_of(part * own_rows, SUBL), own_rows), :]


def sums_kernel(start_ref, image_ref, base_ref, other_ref, out_ref, again_ref):
    again = base_ref[...]
    for step in range(other_ref.shape[0]):
        again = again + other_ref[step]
    again_ref[...] = again
    vector, image = start_ref[...], image_ref[...]
    sums = [down(vector, vector), down(vector, image), down(image, image)]
    sums += [down(vector, again), down(image, again), down(again, again)]
    sums = jnp.concatenate([*sums, jnp.zeros((SUBL - 6, LANES), jnp.float32)], 0)
    sums = jnp.sum(sums, axis=1, keepdims=True)
    sums = jnp.where(row_iota((SUBL, LANES)) == lane_iota((SUBL, LANES)), sums, 0.0)
    sums = jnp.sum(sums, axis=0, keepdims=True)
    for device in range(out_ref.shape[0]):
        out_ref[device] = sums


def last_kernel(cells, start_ref, image_ref, again_ref, sums_ref, second_ref, third_ref, entries_ref):
    sums = jnp.sum(sums_ref[...], axis=0) / cells

    def whole(i):
        return jnp.broadcast_to(sums[:, i : i + 1], (1, LANES))

    vv, vw, ww, vy, wy, yy = (whole(i) for i in range(6))
    norm_square = vv + epsilon
    inverse = 1.0 / norm_square
    h11 = vw * inverse
    skew = vy - h11 * vw
    first_square = jnp.maximum(ww - 2.0 * h11 * vw + h11 * h11 * vv, 0.0) * inverse + epsilon
    over_first = lax.rsqrt(first_square)
    h21 = first_square * over_first
    scale = lax.rsqrt(norm_square) * over_first
    h12 = skew * inverse * over_first
    h22 = (wy - h11 * (ww + skew)) * scale * scale
    near = h11 + h22
    far = skew * inverse - h11 * h22
    second_square = yy + near * near * ww + far * far * vv + 2.0 * (near * far * vw - near * wy - far * vy)
    second_square = jnp.maximum(second_square, 0.0) * scale * scale + epsilon
    over_second = lax.rsqrt(second_square)
    h32 = second_square * over_second

    vector, image = start_ref[...], image_ref[...]
    second_ref[...] = (image - h11 * vector) * scale
    third_ref[...] = (again_ref[...] - near * image - far * vector) * (scale * over_second)
    lane = lane_iota((1, LANES))
    entries = h32
    for i, value in enumerate((h11, h21, h12, h22)):
        entries = jnp.where(lane == i, value, entries)
    entries_ref[...] = entries[:, 0:5]


def per_device(start_vector, blocks, pattern, trace_map, neighbours, coupling):
    own_cells = start_vector.shape[2]
    own_rows = own_cells // LANES
    parts, subs, reps = lax.axis_size("blk"), lax.axis_size("sub"), lax.axis_size("rep")
    rows = own_rows * parts
    cells = own_cells * parts * subs * reps
    start = start_vector.reshape(own_rows, LANES)
    local_map = trace_map[0]
    blocks, pattern, neighbours, coupling = blocks[0, 0], pattern[0, 0], neighbours[0], coupling[0, 0]
    vmem = pl.BlockSpec(memory_space=pltpu.VMEM)
    params = pltpu.CompilerParams(vmem_limit_bytes=32 * 1024 * 1024)

    def rowed(*shape):
        return jax.ShapeDtypeStruct((*shape, LANES), jnp.float32)

    smem = pl.BlockSpec(memory_space=pltpu.SMEM)

    def from_others(pick, members=range(reps)):
        got = []
        for step in range(1, parts):
            route = [
                ((i + step * (r in members)) % parts * reps + r, i * reps + r) for r in range(reps) for i in range(parts)
            ]
            got.append(lax.ppermute(pick(step), ("blk", "rep"), route))
        return got[0] if parts == 2 else jnp.concatenate(got, 0)

    slots, block_rows, width = blocks.shape
    own_blocks = block_rows // parts

    def scratch(count):
        return [
            pltpu.VMEM((count, LANES), jnp.float32),
            pltpu.VMEM((count * width // LANES, 2 * LANES), jnp.bfloat16),
        ]

    def shaped(dtype, *shape):
        return jax.ShapeDtypeStruct(shape, dtype)

    long = pl.CostEstimate(flops=1 << 32, bytes_accessed=1 << 20, transcendentals=0)
    others = from_others(lambda step: start[None])

    send = pl.pallas_call(
        send_kernel,
        out_shape=shaped(jnp.bfloat16, parts - 1, slots, own_blocks, width),
        in_specs=[vmem],
        out_specs=vmem,
        compiler_params=params,
        name="send_blocks",
    )(blocks)
    other_blocks = from_others(lambda step: send if parts == 2 else send[step - 1 : step], range(0, reps, 2))
    wide = pl.pallas_call(
        widen_kernel,
        out_shape=shaped(jnp.float32, *blocks.shape),
        in_specs=[vmem],
        out_specs=vmem,
        compiler_params=params,
        cost_estimate=long,
        name="wide_blocks",
    )(blocks)
    lines, chosen, chosen_own = pl.pallas_call(
        lines_kernel,
        out_shape=(
            rowed(SUBL),
            shaped(jnp.bfloat16, slots * block_rows, 3 * block_rows),
            shaped(jnp.bfloat16, slots * block_rows, 3 * block_rows),
        ),
        in_specs=[vmem] * 5,
        out_specs=(vmem, vmem, vmem),
        scratch_shapes=[pltpu.VMEM((block_rows, 3 * block_rows), jnp.float32)],
        compiler_params=params,
        cost_estimate=long,
        name="group_lines",
    )(start, local_map, neighbours, coupling, pattern)
    partial, vector = pl.pallas_call(
        first_kernel,
        out_shape=(rowed(subs * parts, rows + SUBL), rowed(rows)),
        in_specs=[vmem] * 5,
        out_specs=(vmem, vmem),
        scratch_shapes=scratch(block_rows),
        compiler_params=params,
        name="first_image",
    )(start, lines, others, wide, chosen)
    group = lax.all_to_all(partial, ("sub", "blk"), 0, 0, tiled=True)
    base, give, image = pl.pallas_call(
        second_kernel,
        out_shape=(rowed(own_rows), rowed(parts - 1, own_rows), rowed(own_rows)),
        in_specs=[vmem] * 6 + [smem],
        out_specs=(vmem, vmem, vmem),
        scratch_shapes=[pltpu.VMEM((rows, LANES), jnp.float32), *scratch(block_rows), *scratch(own_blocks)],
        compiler_params=params,
        name="second_image",
    )(start, group, wide, other_blocks, chosen, chosen_own, neighbours)
    given = from_others(lambda step: give if parts == 2 else give[step - 1 : step], range(1, reps, 2))
    sums, again = pl.pallas_call(
        sums_kernel,
        out_shape=(rowed(reps * subs * parts, 1), rowed(own_rows)),
        in_specs=[vmem] * 4,
        out_specs=(vmem, vmem),
        compiler_params=params,
        name="own_sums",
    )(start, image, base, given)
    sums = lax.all_to_all(sums, ("rep", "sub", "blk"), 0, 0, tiled=True)
    second, third, entries = pl.pallas_call(
        functools.partial(last_kernel, float(cells)),
        out_shape=(rowed(own_rows), rowed(own_rows), jax.ShapeDtypeStruct((1, 5), jnp.float32)),
        in_specs=[vmem] * 4,
        out_specs=(vmem, vmem, vmem),
        compiler_params=params,
        name="arnoldi_entries",
    )(start, image, again, sums)
    return second.reshape(start_vector.shape), third.reshape(start_vector.shape), entries.reshape(5)


def solution(mesh):
    return jax.shard_map(
        per_device,
        mesh=mesh,
        in_specs=(
            P("rep", "sub", "blk"),
            P("rep", "sub", "blk", None, None),
            P("rep", "sub", None, None),
            P("rep", "sub", "blk"),
            P("rep", "sub", None),
            P("rep", "sub", None, "blk"),
        ),
        out_specs=(P("rep", "sub", "blk"), P("rep", "sub", "blk"), P()),
        check_vma=False,
    )
```

```python
import functools

import jax
import jax.numpy as jnp
from jax import lax
from jax.experimental import pallas as pl
from jax.experimental.pallas import tpu as pltpu
from jax.sharding import PartitionSpec as P

BS = 64
LANES = 128
SUBL = 8
epsilon = 1e-06


def pieces(value):
    high = value.astype(jnp.bfloat16)
    rest = value - high.astype(jnp.float32)
    middle = rest.astype(jnp.bfloat16)
    low = (rest - middle.astype(jnp.float32)).astype(jnp.bfloat16)
    return high, middle, low


def lane_iota(shape):
    return lax.broadcasted_iota(jnp.int32, shape, len(shape) - 1)


def row_iota(shape):
    return lax.broadcasted_iota(jnp.int32, shape, 0)


def choices(pattern_ref, slot):
    block_rows = pattern_ref.shape[1]
    half = block_rows // 2
    place = row_iota((block_rows, block_rows))
    place = jnp.where(place < half, 2 * place, 2 * (place - half) + 1)
    thrice = (block_rows, 3 * block_rows)
    copies = (lane_iota(thrice) % block_rows == row_iota(thrice)).astype(jnp.float32).astype(jnp.bfloat16)
    chosen = (place == pattern_ref[pl.ds(slot, 1), :]).astype(jnp.float32).astype(jnp.bfloat16)
    return lax.dot_general(chosen, copies, (((0,), (0,)), ((), ())), preferred_element_type=jnp.float32)


def block_product(vector, fetch, width, chosen, fold_ref, halves_ref):
    block_rows = fold_ref.shape[0]
    slots = chosen.shape[0] // block_rows
    half = block_rows // 2
    lower = lane_iota(vector.shape) < BS
    turned = pltpu.roll(vector, BS, 1)
    table = jnp.concatenate([jnp.where(lower, vector, turned), jnp.where(lower, turned, vector)], 0)
    table = jnp.concatenate(pieces(table), 0)
    picked = lax.dot_general(chosen, table, (((1,), (0,)), ((), ())), preferred_element_type=jnp.float32)
    ones = (row_iota((2 * LANES, LANES)) % LANES) // BS == lane_iota((2 * LANES, LANES)) % 2
    ones = ones.astype(jnp.float32).astype(jnp.bfloat16)
    pair = (lane_iota((block_rows, LANES)) % BS) // 2
    chunks = width // LANES
    together = chunks // 4
    result = jnp.zeros((block_rows, LANES), jnp.float32)
    for first in range(0, chunks, together):
        for c in range(first, first + together):
            total = None
            for k in range(slots):
                term = fetch(k, pl.ds(c * LANES, LANES)) * picked[k * block_rows : (k + 1) * block_rows]
                total = term if total is None else total + term
            high = total.astype(jnp.bfloat16)
            here = pl.ds(c * block_rows, block_rows)
            halves_ref[here, 0:LANES] = high
            halves_ref[here, LANES : 2 * LANES] = (total - high.astype(jnp.float32)).astype(jnp.bfloat16)
        sums = lax.dot_general(
            halves_ref[pl.ds(first * block_rows, together * block_rows), :],
            ones,
            (((1,), (0,)), ((), ())),
            preferred_element_type=jnp.float32,
        )
        for i in range(together):
            result = jnp.where(pair == first + i, sums[i * block_rows : (i + 1) * block_rows], result)
    fold_ref[...] = result
    even = fold_ref[pl.ds(0, half, stride=2), :]
    odd = fold_ref[pl.ds(1, half, stride=2), :]
    return jnp.where(lane_iota((half, LANES)) < BS, even, odd)


def take_trace(rows, places):
    count = rows.shape[0]
    low = jnp.broadcast_to(places % LANES, (count, LANES))
    picked = jnp.take_along_axis(rows, low, axis=1)
    return jnp.sum(jnp.where(row_iota((count, LANES)) == places // LANES, picked, 0.0), axis=0, keepdims=True)


def spread(values, places, count):
    aimed = jnp.where(row_iota((count, LANES)) == places // LANES, values, 0.0)
    high = aimed.astype(jnp.bfloat16).astype(jnp.float32)
    rest = aimed - high
    middle = rest.astype(jnp.bfloat16).astype(jnp.float32)
    stack = jnp.concatenate([high, middle, rest - middle], 0).astype(jnp.bfloat16)
    target = (row_iota((LANES, LANES)) == places % LANES).astype(jnp.float32).astype(jnp.bfloat16)
    landed = lax.dot_general(stack, target, (((1,), (1,)), ((), ())), preferred_element_type=jnp.float32)
    return landed[0:count] + landed[count : 2 * count] + landed[2 * count : 3 * count]


def lines_kernel(
    start_ref, map_ref, near_ref, coupling_ref, pattern_ref, out_ref, first_ref, second_ref, rows_ref
):
    places = map_ref[...]
    count = coupling_ref.shape[0]
    blk, parts = lax.axis_index("blk"), lax.axis_size("blk")
    lines = [take_trace(start_ref[...], places - blk * start_ref.shape[0] * LANES), places.astype(jnp.float32)]
    lines += [coupling_ref[n : n + 1, :] for n in range(count)]
    near = near_ref[...].astype(jnp.float32)
    lines += [jnp.broadcast_to(near[:, n : n + 1], (1, LANES)) for n in range(count)]
    lines += [jnp.zeros((SUBL - len(lines), LANES), jnp.float32)]
    out_ref[...] = jnp.concatenate(lines, 0)
    all_slots, block_rows = pattern_ref.shape
    slots = all_slots // parts
    own_rows = block_rows // parts
    for step in range(parts):
        for k in range(slots):
            at = step * slots + k
            chosen = choices(pattern_ref, lax.rem(blk + step, parts) * slots + k)
            if step == 0:
                first_ref[k * block_rows : (k + 1) * block_rows, :] = chosen.astype(jnp.bfloat16)
            rows_ref[...] = chosen
            own = rows_ref[pl.ds(pl.multiple_of(blk * own_rows, SUBL), own_rows), :]
            second_ref[at * own_rows : (at + 1) * own_rows, :] = own.astype(jnp.bfloat16)


def send_kernel(blocks_ref, out_ref):
    others, _, own_rows, _ = out_ref.shape
    blk, parts = lax.axis_index("blk"), lax.axis_size("blk")
    for step in range(1, others + 1):
        part = lax.rem(blk + parts - step, parts)
        out_ref[step - 1] = blocks_ref[:, pl.ds(pl.multiple_of(part * own_rows, 16), own_rows), :]


def widen_kernel(blocks_ref, out_ref):
    out_ref[...] = blocks_ref[...].astype(jnp.float32)


def first_kernel(
    start_ref, lines_ref, other_ref, blocks_ref, choices_ref, out_ref, vector_ref, fold_ref, halves_ref
):
    own_rows, rows = start_ref.shape[0], vector_ref.shape[0]
    blk, parts = lax.axis_index("blk"), lax.axis_size("blk")
    for step in range(parts):
        place = lax.rem(blk + step, parts)
        place = pl.ds(pl.multiple_of(place * own_rows, SUBL), own_rows)
        vector_ref[place, :] = other_ref[step - 1] if step else start_ref[...]

    def fetch(k, lanes):
        return blocks_ref[k, :, lanes]

    partial = block_product(
        vector_ref[...], fetch, blocks_ref.shape[2], choices_ref[...], fold_ref, halves_ref
    )
    for device in range(out_ref.shape[0]):
        out_ref[device, 0:rows, :] = partial
        out_ref[device, rows : rows + SUBL, :] = lines_ref[...]


def line(group_ref, device, i):
    first = group_ref.shape[1] - SUBL + i
    return group_ref[device, first : first + 1, :]


def landed(group_ref, sub_at, part, own_rows, count):
    parts = lax.axis_size("blk")
    traces = [line(group_ref, other * parts + part, 0) for other in range(lax.axis_size("sub"))]
    traces = jnp.concatenate(traces, 0)
    names = row_iota(traces.shape).astype(jnp.float32)
    device = sub_at * parts + part
    inflow = jnp.zeros((1, LANES), jnp.float32)
    for n in range(count):
        chosen = jnp.where(names == line(group_ref, device, 2 + count + n), traces, 0.0)
        inflow = inflow + line(group_ref, device, 2 + n) * jnp.sum(chosen, axis=0, keepdims=True)
    places = line(group_ref, device, 1).astype(jnp.int32) - part * own_rows * LANES
    return spread(inflow, places, own_rows), places


def summed(group_ref, sub_at, where):
    parts = lax.axis_size("blk")
    total = group_ref[sub_at * parts, where, :]
    for b in range(1, parts):
        total = total + group_ref[sub_at * parts + b, where, :]
    return total


def down(left, right):
    return jnp.sum(left * right, axis=0, keepdims=True)


def second_kernel(
    start_ref,
    group_ref,
    blocks_ref,
    other_ref,
    first_ref,
    second_ref,
    near_ref,
    base_ref,
    give_ref,
    image_ref,
    whole_ref,
    fold_ref,
    halves_ref,
    own_fold_ref,
    own_halves_ref,
):
    own_rows = start_ref.shape[0]
    slots, block_rows, width = blocks_ref.shape
    count = near_ref.shape[1]
    sub, blk, parts = lax.axis_index("sub"), lax.axis_index("blk"), lax.axis_size("blk")
    odd = lax.rem(lax.axis_index("rep"), 2)
    own_blocks = block_rows // parts
    here = pl.ds(pl.multiple_of(blk * own_blocks, 16), own_blocks)
    own = pl.ds(pl.multiple_of(blk * own_rows, SUBL), own_rows)
    inflow = jnp.zeros((1, LANES), jnp.float32)
    for n in range(count):
        source = near_ref[0, n]
        added, places = landed(group_ref, source, blk, own_rows, count)
        trace = take_trace(summed(group_ref, source, own) + added, places)
        inflow = inflow + line(group_ref, sub * parts + blk, 2 + n) * trace
    places = line(group_ref, sub * parts + blk, 1).astype(jnp.int32) - blk * own_rows * LANES
    base_ref[...] = spread(inflow, places, own_rows)
    added = [landed(group_ref, sub, part, own_rows, count)[0] for part in range(parts)]
    whole_ref[...] = summed(group_ref, sub, pl.ds(0, own_rows * parts)) + jnp.concatenate(added, 0)
    image_ref[...] = whole_ref[own, :]

    def fetch_own(k, lanes):
        if k < slots:
            return blocks_ref[k, here, lanes]
        return other_ref[k // slots - 1, k % slots, :, lanes].astype(jnp.float32)

    def fetch(k, lanes):
        return blocks_ref[k, :, lanes]

    @pl.when(odd == 0)
    def _():
        product = block_product(whole_ref[...], fetch_own, width, second_ref[...], own_fold_ref, own_halves_ref)
        base_ref[...] = base_ref[...] + product
        give_ref[...] = jnp.zeros(give_ref.shape, jnp.float32)

    @pl.when(odd == 1)
    def _():
        product = block_product(whole_ref[...], fetch, width, first_ref[...], fold_ref, halves_ref)
        whole_ref[...] = product
        base_ref[...] = base_ref[...] + whole_ref[own, :]
        for step in range(1, parts):
            part = lax.rem(blk + parts - step, parts)
            give_ref[step - 1] = whole_ref[pl.ds(pl.multiple_of(part * own_rows, SUBL), own_rows), :]


def sums_kernel(start_ref, image_ref, base_ref, other_ref, out_ref, again_ref):
    again = base_ref[...]
    for step in range(other_ref.shape[0]):
        again = again + other_ref[step]
    again_ref[...] = again
    vector, image = start_ref[...], image_ref[...]
    sums = [down(vector, vector), down(vector, image), down(image, image)]
    sums += [down(vector, again), down(image, again), down(again, again)]
    sums = jnp.concatenate([*sums, jnp.zeros((SUBL - 6, LANES), jnp.float32)], 0)
    sums = jnp.sum(sums, axis=1, keepdims=True)
    sums = jnp.where(row_iota((SUBL, LANES)) == lane_iota((SUBL, LANES)), sums, 0.0)
    sums = jnp.sum(sums, axis=0, keepdims=True)
    for device in range(out_ref.shape[0]):
        out_ref[device] = sums


def last_kernel(cells, start_ref, image_ref, again_ref, sums_ref, second_ref, third_ref, entries_ref):
    sums = jnp.sum(sums_ref[...], axis=0) / cells

    def whole(i):
        return jnp.broadcast_to(sums[:, i : i + 1], (1, LANES))

    vv, vw, ww, vy, wy, yy = (whole(i) for i in range(6))
    norm_square = vv + epsilon
    inverse = 1.0 / norm_square
    h11 = vw * inverse
    skew = vy - h11 * vw
    first_square = jnp.maximum(ww - 2.0 * h11 * vw + h11 * h11 * vv, 0.0) * inverse + epsilon
    over_first = lax.rsqrt(first_square)
    h21 = first_square * over_first
    scale = lax.rsqrt(norm_square) * over_first
    h12 = skew * inverse * over_first
    h22 = (wy - h11 * (ww + skew)) * scale * scale
    near = h11 + h22
    far = skew * inverse - h11 * h22
    second_square = yy + near * near * ww + far * far * vv + 2.0 * (near * far * vw - near * wy - far * vy)
    second_square = jnp.maximum(second_square, 0.0) * scale * scale + epsilon
    over_second = lax.rsqrt(second_square)
    h32 = second_square * over_second

    vector, image = start_ref[...], image_ref[...]
    second_ref[...] = (image - h11 * vector) * scale
    third_ref[...] = (again_ref[...] - near * image - far * vector) * (scale * over_second)
    lane = lane_iota((1, LANES))
    entries = h32
    for i, value in enumerate((h11, h21, h12, h22)):
        entries = jnp.where(lane == i, value, entries)
    entries_ref[...] = entries[:, 0:5]


def per_device(start_vector, blocks, pattern, trace_map, neighbours, coupling):
    own_cells = start_vector.shape[2]
    own_rows = own_cells // LANES
    parts, subs, reps = lax.axis_size("blk"), lax.axis_size("sub"), lax.axis_size("rep")
    rows = own_rows * parts
    cells = own_cells * parts * subs * reps
    start = start_vector.reshape(own_rows, LANES)
    local_map = trace_map[0]
    blocks, pattern, neighbours, coupling = blocks[0, 0], pattern[0, 0], neighbours[0], coupling[0, 0]
    vmem = pl.BlockSpec(memory_space=pltpu.VMEM)
    params = pltpu.CompilerParams(vmem_limit_bytes=32 * 1024 * 1024)

    def rowed(*shape):
        return jax.ShapeDtypeStruct((*shape, LANES), jnp.float32)

    smem = pl.BlockSpec(memory_space=pltpu.SMEM)

    def from_others(pick, members=range(reps), idle=()):
        got = []
        for step in range(1, parts):
            route = [((i + step) % parts * reps + r, i * reps + r) for r in members for i in range(parts)]
            if idle:
                route += [(i * reps + idle[n - 1], i * reps + r) for n, r in enumerate(idle) for i in range(parts)]
            got.append(lax.ppermute(pick(step), ("blk", "rep"), route))
        return got[0] if parts == 2 else jnp.concatenate(got, 0)

    slots, block_rows, width = blocks.shape
    own_blocks = block_rows // parts

    def scratch(count):
        return [
            pltpu.VMEM((count, LANES), jnp.float32),
            pltpu.VMEM((count * width // LANES, 2 * LANES), jnp.bfloat16),
        ]

    def shaped(dtype, *shape):
        return jax.ShapeDtypeStruct(shape, dtype)

    long = pl.CostEstimate(flops=1 << 32, bytes_accessed=1 << 20, transcendentals=0)
    others = from_others(lambda step: start[None])

    send = pl.pallas_call(
        send_kernel,
        out_shape=shaped(jnp.bfloat16, parts - 1, slots, own_blocks, width),
        in_specs=[vmem],
        out_specs=vmem,
        compiler_params=params,
        name="send_blocks",
    )(blocks)
    other_blocks = from_others(lambda step: send if parts == 2 else send[step - 1 : step], range(0, reps, 2), range(1, reps, 2))
    wide = pl.pallas_call(
        widen_kernel,
        out_shape=shaped(jnp.float32, *blocks.shape),
        in_specs=[vmem],
        out_specs=vmem,
        compiler_params=params,
        cost_estimate=long,
        name="wide_blocks",
    )(blocks)
    lines, chosen, chosen_own = pl.pallas_call(
        lines_kernel,
        out_shape=(
            rowed(SUBL),
            shaped(jnp.bfloat16, slots * block_rows, 3 * block_rows),
            shaped(jnp.bfloat16, slots * block_rows, 3 * block_rows),
        ),
        in_specs=[vmem] * 5,
        out_specs=(vmem, vmem, vmem),
        scratch_shapes=[pltpu.VMEM((block_rows, 3 * block_rows), jnp.float32)],
        compiler_params=params,
        cost_estimate=long,
        name="group_lines",
    )(start, local_map, neighbours, coupling, pattern)
    partial, vector = pl.pallas_call(
        first_kernel,
        out_shape=(rowed(subs * parts, rows + SUBL), rowed(rows)),
        in_specs=[vmem] * 5,
        out_specs=(vmem, vmem),
        scratch_shapes=scratch(block_rows),
        compiler_params=params,
        name="first_image",
    )(start, lines, others, wide, chosen)
    group = lax.all_to_all(partial, ("sub", "blk"), 0, 0, tiled=True)
    base, give, image = pl.pallas_call(
        second_kernel,
        out_shape=(rowed(own_rows), rowed(parts - 1, own_rows), rowed(own_rows)),
        in_specs=[vmem] * 6 + [smem],
        out_specs=(vmem, vmem, vmem),
        scratch_shapes=[pltpu.VMEM((rows, LANES), jnp.float32), *scratch(block_rows), *scratch(own_blocks)],
        compiler_params=params,
        name="second_image",
    )(start, group, wide, other_blocks, chosen, chosen_own, neighbours)
    given = from_others(lambda step: give if parts == 2 else give[step - 1 : step], range(1, reps, 2))
    sums, again = pl.pallas_call(
        sums_kernel,
        out_shape=(rowed(reps * subs * parts, 1), rowed(own_rows)),
        in_specs=[vmem] * 4,
        out_specs=(vmem, vmem),
        compiler_params=params,
        name="own_sums",
    )(start, image, base, given)
    sums = lax.all_to_all(sums, ("rep", "sub", "blk"), 0, 0, tiled=True)
    second, third, entries = pl.pallas_call(
        functools.partial(last_kernel, float(cells)),
        out_shape=(rowed(own_rows), rowed(own_rows), jax.ShapeDtypeStruct((1, 5), jnp.float32)),
        in_specs=[vmem] * 4,
        out_specs=(vmem, vmem, vmem),
        compiler_params=params,
        name="arnoldi_entries",
    )(start, image, again, sums)
    return second.reshape(start_vector.shape), third.reshape(start_vector.shape), entries.reshape(5)


def solution(mesh):
    return jax.shard_map(
        per_device,
        mesh=mesh,
        in_specs=(
            P("rep", "sub", "blk"),
            P("rep", "sub", "blk", None, None),
            P("rep", "sub", None, None),
            P("rep", "sub", "blk"),
            P("rep", "sub", None),
            P("rep", "sub", None, "blk"),
        ),
        out_specs=(P("rep", "sub", "blk"), P("rep", "sub", "blk"), P()),
        check_vma=False,
    )
```

```python
import functools

import jax
import jax.numpy as jnp
from jax import lax
from jax.experimental import pallas as pl
from jax.experimental.pallas import tpu as pltpu
from jax.sharding import PartitionSpec as P

BS = 64
LANES = 128
SUBL = 8
epsilon = 1e-06


def pieces(value):
    high = value.astype(jnp.bfloat16)
    rest = value - high.astype(jnp.float32)
    middle = rest.astype(jnp.bfloat16)
    low = (rest - middle.astype(jnp.float32)).astype(jnp.bfloat16)
    return high, middle, low


def lane_iota(shape):
    return lax.broadcasted_iota(jnp.int32, shape, len(shape) - 1)


def row_iota(shape):
    return lax.broadcasted_iota(jnp.int32, shape, 0)


def choices(pattern_ref, slot):
    block_rows = pattern_ref.shape[1]
    half = block_rows // 2
    place = row_iota((block_rows, block_rows))
    place = jnp.where(place < half, 2 * place, 2 * (place - half) + 1)
    thrice = (block_rows, 3 * block_rows)
    copies = (lane_iota(thrice) % block_rows == row_iota(thrice)).astype(jnp.float32).astype(jnp.bfloat16)
    chosen = (place == pattern_ref[pl.ds(slot, 1), :]).astype(jnp.float32).astype(jnp.bfloat16)
    return lax.dot_general(chosen, copies, (((0,), (0,)), ((), ())), preferred_element_type=jnp.float32)


def block_product(vector, fetch, width, chosen, fold_ref, halves_ref):
    block_rows = fold_ref.shape[0]
    slots = chosen.shape[0] // block_rows
    half = block_rows // 2
    lower = lane_iota(vector.shape) < BS
    turned = pltpu.roll(vector, BS, 1)
    table = jnp.concatenate([jnp.where(lower, vector, turned), jnp.where(lower, turned, vector)], 0)
    table = jnp.concatenate(pieces(table), 0)
    picked = lax.dot_general(chosen, table, (((1,), (0,)), ((), ())), preferred_element_type=jnp.float32)
    ones = (row_iota((2 * LANES, LANES)) % LANES) // BS == lane_iota((2 * LANES, LANES)) % 2
    ones = ones.astype(jnp.float32).astype(jnp.bfloat16)
    pair = (lane_iota((block_rows, LANES)) % BS) // 2
    chunks = width // LANES
    together = chunks // 4
    result = jnp.zeros((block_rows, LANES), jnp.float32)
    for first in range(0, chunks, together):
        for c in range(first, first + together):
            total = None
            for k in range(slots):
                term = fetch(k, pl.ds(c * LANES, LANES)) * picked[k * block_rows : (k + 1) * block_rows]
                total = term if total is None else total + term
            high = total.astype(jnp.bfloat16)
            here = pl.ds(c * block_rows, block_rows)
            halves_ref[here, 0:LANES] = high
            halves_ref[here, LANES : 2 * LANES] = (total - high.astype(jnp.float32)).astype(jnp.bfloat16)
        sums = lax.dot_general(
            halves_ref[pl.ds(first * block_rows, together * block_rows), :],
            ones,
            (((1,), (0,)), ((), ())),
            preferred_element_type=jnp.float32,
        )
        for i in range(together):
            result = jnp.where(pair == first + i, sums[i * block_rows : (i + 1) * block_rows], result)
    fold_ref[...] = result
    even = fold_ref[pl.ds(0, half, stride=2), :]
    odd = fold_ref[pl.ds(1, half, stride=2), :]
    return jnp.where(lane_iota((half, LANES)) < BS, even, odd)


def take_trace(rows, places):
    count = rows.shape[0]
    low = jnp.broadcast_to(places % LANES, (count, LANES))
    picked = jnp.take_along_axis(rows, low, axis=1)
    return jnp.sum(jnp.where(row_iota((count, LANES)) == places // LANES, picked, 0.0), axis=0, keepdims=True)


def spread(values, places, count):
    aimed = jnp.where(row_iota((count, LANES)) == places // LANES, values, 0.0)
    high = aimed.astype(jnp.bfloat16).astype(jnp.float32)
    rest = aimed - high
    middle = rest.astype(jnp.bfloat16).astype(jnp.float32)
    stack = jnp.concatenate([high, middle, rest - middle], 0).astype(jnp.bfloat16)
    target = (row_iota((LANES, LANES)) == places % LANES).astype(jnp.float32).astype(jnp.bfloat16)
    landed = lax.dot_general(stack, target, (((1,), (1,)), ((), ())), preferred_element_type=jnp.float32)
    return landed[0:count] + landed[count : 2 * count] + landed[2 * count : 3 * count]


def lines_kernel(
    start_ref, map_ref, near_ref, coupling_ref, pattern_ref, out_ref, first_ref, second_ref, rows_ref
):
    places = map_ref[...]
    count = coupling_ref.shape[0]
    blk, parts = lax.axis_index("blk"), lax.axis_size("blk")
    lines = [take_trace(start_ref[...], places - blk * start_ref.shape[0] * LANES), places.astype(jnp.float32)]
    lines += [coupling_ref[n : n + 1, :] for n in range(count)]
    near = near_ref[...].astype(jnp.float32)
    lines += [jnp.broadcast_to(near[:, n : n + 1], (1, LANES)) for n in range(count)]
    lines += [jnp.zeros((SUBL - len(lines), LANES), jnp.float32)]
    out_ref[...] = jnp.concatenate(lines, 0)
    all_slots, block_rows = pattern_ref.shape
    slots = all_slots // parts
    own_rows = block_rows // parts
    for step in range(parts):
        for k in range(slots):
            at = step * slots + k
            chosen = choices(pattern_ref, lax.rem(blk + step, parts) * slots + k)
            if step == 0:
                first_ref[k * block_rows : (k + 1) * block_rows, :] = chosen.astype(jnp.bfloat16)
            rows_ref[...] = chosen
            own = rows_ref[pl.ds(pl.multiple_of(blk * own_rows, SUBL), own_rows), :]
            second_ref[at * own_rows : (at + 1) * own_rows, :] = own.astype(jnp.bfloat16)


def send_kernel(blocks_ref, out_ref):
    others, _, own_rows, _ = out_ref.shape
    blk, parts = lax.axis_index("blk"), lax.axis_size("blk")
    for step in range(1, others + 1):
        part = lax.rem(blk + parts - step, parts)
        out_ref[step - 1] = blocks_ref[:, pl.ds(pl.multiple_of(part * own_rows, 16), own_rows), :]


def widen_kernel(blocks_ref, out_ref):
    out_ref[...] = blocks_ref[...].astype(jnp.float32)


def first_kernel(
    start_ref, lines_ref, other_ref, blocks_ref, choices_ref, out_ref, vector_ref, fold_ref, halves_ref
):
    own_rows, rows = start_ref.shape[0], vector_ref.shape[0]
    blk, parts = lax.axis_index("blk"), lax.axis_size("blk")
    for step in range(parts):
        place = lax.rem(blk + step, parts)
        place = pl.ds(pl.multiple_of(place * own_rows, SUBL), own_rows)
        vector_ref[place, :] = other_ref[step - 1] if step else start_ref[...]

    def fetch(k, lanes):
        return blocks_ref[k, :, lanes]

    partial = block_product(
        vector_ref[...], fetch, blocks_ref.shape[2], choices_ref[...], fold_ref, halves_ref
    )
    for device in range(out_ref.shape[0]):
        out_ref[device, 0:rows, :] = partial
        out_ref[device, rows : rows + SUBL, :] = lines_ref[...]


def line(group_ref, device, i):
    first = group_ref.shape[1] - SUBL + i
    return group_ref[device, first : first + 1, :]


def landed(group_ref, sub_at, part, own_rows, count):
    parts = lax.axis_size("blk")
    traces = [line(group_ref, other * parts + part, 0) for other in range(lax.axis_size("sub"))]
    traces = jnp.concatenate(traces, 0)
    names = row_iota(traces.shape).astype(jnp.float32)
    device = sub_at * parts + part
    inflow = jnp.zeros((1, LANES), jnp.float32)
    for n in range(count):
        chosen = jnp.where(names == line(group_ref, device, 2 + count + n), traces, 0.0)
        inflow = inflow + line(group_ref, device, 2 + n) * jnp.sum(chosen, axis=0, keepdims=True)
    places = line(group_ref, device, 1).astype(jnp.int32) - part * own_rows * LANES
    return spread(inflow, places, own_rows), places


def summed(group_ref, sub_at, where):
    parts = lax.axis_size("blk")
    total = group_ref[sub_at * parts, where, :]
    for b in range(1, parts):
        total = total + group_ref[sub_at * parts + b, where, :]
    return total


def down(left, right):
    return jnp.sum(left * right, axis=0, keepdims=True)


def second_kernel(
    start_ref,
    group_ref,
    blocks_ref,
    other_ref,
    first_ref,
    second_ref,
    near_ref,
    base_ref,
    give_ref,
    image_ref,
    whole_ref,
    fold_ref,
    halves_ref,
    own_fold_ref,
    own_halves_ref,
):
    own_rows = start_ref.shape[0]
    slots, block_rows, width = blocks_ref.shape
    count = near_ref.shape[1]
    sub, blk, parts = lax.axis_index("sub"), lax.axis_index("blk"), lax.axis_size("blk")
    odd = lax.rem(lax.axis_index("rep"), 2)
    own_blocks = block_rows // parts
    here = pl.ds(pl.multiple_of(blk * own_blocks, 16), own_blocks)
    own = pl.ds(pl.multiple_of(blk * own_rows, SUBL), own_rows)
    base_ref[...] = jnp.zeros(base_ref.shape, jnp.float32)
    added = [landed(group_ref, sub, part, own_rows, count)[0] for part in range(parts)]
    whole_ref[...] = summed(group_ref, sub, pl.ds(0, own_rows * parts)) + jnp.concatenate(added, 0)
    image_ref[...] = whole_ref[own, :]

    def fetch_own(k, lanes):
        if k < slots:
            return blocks_ref[k, here, lanes]
        return other_ref[k // slots - 1, k % slots, :, lanes].astype(jnp.float32)

    def fetch(k, lanes):
        return blocks_ref[k, :, lanes]

    @pl.when(odd == 0)
    def _():
        product = block_product(whole_ref[...], fetch_own, width, second_ref[...], own_fold_ref, own_halves_ref)
        base_ref[...] = base_ref[...] + product
        give_ref[...] = jnp.zeros(give_ref.shape, jnp.float32)

    @pl.when(odd == 1)
    def _():
        product = block_product(whole_ref[...], fetch, width, first_ref[...], fold_ref, halves_ref)
        whole_ref[...] = product
        base_ref[...] = base_ref[...] + whole_ref[own, :]
        for step in range(1, parts):
            part = lax.rem(blk + parts - step, parts)
            give_ref[step - 1] = whole_ref[pl.ds(pl.multiple_of(part * own_rows, SUBL), own_rows), :]


def inflow_kernel(group_ref, near_ref, out_ref):
    own_rows, count = out_ref.shape[0], near_ref.shape[1]
    sub, blk, parts = lax.axis_index("sub"), lax.axis_index("blk"), lax.axis_size("blk")
    own = pl.ds(pl.multiple_of(blk * own_rows, SUBL), own_rows)
    inflow = jnp.zeros((1, LANES), jnp.float32)
    for n in range(count):
        source = near_ref[0, n]
        added, places = landed(group_ref, source, blk, own_rows, count)
        trace = take_trace(summed(group_ref, source, own) + added, places)
        inflow = inflow + line(group_ref, sub * parts + blk, 2 + n) * trace
    places = line(group_ref, sub * parts + blk, 1).astype(jnp.int32) - blk * own_rows * LANES
    out_ref[...] = spread(inflow, places, own_rows)


def sums_kernel(start_ref, image_ref, base_ref, inflow_ref, other_ref, out_ref, again_ref):
    again = base_ref[...] + inflow_ref[...]
    for step in range(other_ref.shape[0]):
        again = again + other_ref[step]
    again_ref[...] = again
    vector, image = start_ref[...], image_ref[...]
    sums = [down(vector, vector), down(vector, image), down(image, image)]
    sums += [down(vector, again), down(image, again), down(again, again)]
    sums = jnp.concatenate([*sums, jnp.zeros((SUBL - 6, LANES), jnp.float32)], 0)
    sums = jnp.sum(sums, axis=1, keepdims=True)
    sums = jnp.where(row_iota((SUBL, LANES)) == lane_iota((SUBL, LANES)), sums, 0.0)
    sums = jnp.sum(sums, axis=0, keepdims=True)
    for device in range(out_ref.shape[0]):
        out_ref[device] = sums


def last_kernel(cells, start_ref, image_ref, again_ref, sums_ref, second_ref, third_ref, entries_ref):
    sums = jnp.sum(sums_ref[...], axis=0) / cells

    def whole(i):
        return jnp.broadcast_to(sums[:, i : i + 1], (1, LANES))

    vv, vw, ww, vy, wy, yy = (whole(i) for i in range(6))
    norm_square = vv + epsilon
    inverse = 1.0 / norm_square
    h11 = vw * inverse
    skew = vy - h11 * vw
    first_square = jnp.maximum(ww - 2.0 * h11 * vw + h11 * h11 * vv, 0.0) * inverse + epsilon
    over_first = lax.rsqrt(first_square)
    h21 = first_square * over_first
    scale = lax.rsqrt(norm_square) * over_first
    h12 = skew * inverse * over_first
    h22 = (wy - h11 * (ww + skew)) * scale * scale
    near = h11 + h22
    far = skew * inverse - h11 * h22
    second_square = yy + near * near * ww + far * far * vv + 2.0 * (near * far * vw - near * wy - far * vy)
    second_square = jnp.maximum(second_square, 0.0) * scale * scale + epsilon
    over_second = lax.rsqrt(second_square)
    h32 = second_square * over_second

    vector, image = start_ref[...], image_ref[...]
    second_ref[...] = (image - h11 * vector) * scale
    third_ref[...] = (again_ref[...] - near * image - far * vector) * (scale * over_second)
    lane = lane_iota((1, LANES))
    entries = h32
    for i, value in enumerate((h11, h21, h12, h22)):
        entries = jnp.where(lane == i, value, entries)
    entries_ref[...] = entries[:, 0:5]


def per_device(start_vector, blocks, pattern, trace_map, neighbours, coupling):
    own_cells = start_vector.shape[2]
    own_rows = own_cells // LANES
    parts, subs, reps = lax.axis_size("blk"), lax.axis_size("sub"), lax.axis_size("rep")
    rows = own_rows * parts
    cells = own_cells * parts * subs * reps
    start = start_vector.reshape(own_rows, LANES)
    local_map = trace_map[0]
    blocks, pattern, neighbours, coupling = blocks[0, 0], pattern[0, 0], neighbours[0], coupling[0, 0]
    vmem = pl.BlockSpec(memory_space=pltpu.VMEM)
    params = pltpu.CompilerParams(vmem_limit_bytes=32 * 1024 * 1024)

    def rowed(*shape):
        return jax.ShapeDtypeStruct((*shape, LANES), jnp.float32)

    smem = pl.BlockSpec(memory_space=pltpu.SMEM)

    def from_others(pick, members=range(reps), idle=()):
        got = []
        for step in range(1, parts):
            route = [((i + step) % parts * reps + r, i * reps + r) for r in members for i in range(parts)]
            if idle:
                route += [(i * reps + idle[n - 1], i * reps + r) for n, r in enumerate(idle) for i in range(parts)]
            got.append(lax.ppermute(pick(step), ("blk", "rep"), route))
        return got[0] if parts == 2 else jnp.concatenate(got, 0)

    slots, block_rows, width = blocks.shape
    own_blocks = block_rows // parts

    def scratch(count):
        return [
            pltpu.VMEM((count, LANES), jnp.float32),
            pltpu.VMEM((count * width // LANES, 2 * LANES), jnp.bfloat16),
        ]

    def shaped(dtype, *shape):
        return jax.ShapeDtypeStruct(shape, dtype)

    long = pl.CostEstimate(flops=1 << 32, bytes_accessed=1 << 20, transcendentals=0)
    others = from_others(lambda step: start[None])

    send = pl.pallas_call(
        send_kernel,
        out_shape=shaped(jnp.bfloat16, parts - 1, slots, own_blocks, width),
        in_specs=[vmem],
        out_specs=vmem,
        compiler_params=params,
        name="send_blocks",
    )(blocks)
    other_blocks = from_others(lambda step: send if parts == 2 else send[step - 1 : step], range(0, reps, 2), range(1, reps, 2))
    wide = pl.pallas_call(
        widen_kernel,
        out_shape=shaped(jnp.float32, *blocks.shape),
        in_specs=[vmem],
        out_specs=vmem,
        compiler_params=params,
        cost_estimate=long,
        name="wide_blocks",
    )(blocks)
    lines, chosen, chosen_own = pl.pallas_call(
        lines_kernel,
        out_shape=(
            rowed(SUBL),
            shaped(jnp.bfloat16, slots * block_rows, 3 * block_rows),
            shaped(jnp.bfloat16, slots * block_rows, 3 * block_rows),
        ),
        in_specs=[vmem] * 5,
        out_specs=(vmem, vmem, vmem),
        scratch_shapes=[pltpu.VMEM((block_rows, 3 * block_rows), jnp.float32)],
        compiler_params=params,
        cost_estimate=long,
        name="group_lines",
    )(start, local_map, neighbours, coupling, pattern)
    partial, vector = pl.pallas_call(
        first_kernel,
        out_shape=(rowed(subs * parts, rows + SUBL), rowed(rows)),
        in_specs=[vmem] * 5,
        out_specs=(vmem, vmem),
        scratch_shapes=scratch(block_rows),
        compiler_params=params,
        name="first_image",
    )(start, lines, others, wide, chosen)
    group = lax.all_to_all(partial, ("sub", "blk"), 0, 0, tiled=True)
    base, give, image = pl.pallas_call(
        second_kernel,
        out_shape=(rowed(own_rows), rowed(parts - 1, own_rows), rowed(own_rows)),
        in_specs=[vmem] * 6 + [smem],
        out_specs=(vmem, vmem, vmem),
        scratch_shapes=[pltpu.VMEM((rows, LANES), jnp.float32), *scratch(block_rows), *scratch(own_blocks)],
        compiler_params=params,
        name="second_image",
    )(start, group, wide, other_blocks, chosen, chosen_own, neighbours)
    given = from_others(lambda step: give if parts == 2 else give[step - 1 : step], range(1, reps, 2))
    inflow = pl.pallas_call(
        inflow_kernel,
        out_shape=rowed(own_rows),
        in_specs=[vmem, smem],
        out_specs=vmem,
        compiler_params=params,
        cost_estimate=long,
        name="second_inflow",
    )(group, neighbours)
    sums, again = pl.pallas_call(
        sums_kernel,
        out_shape=(rowed(reps * subs * parts, 1), rowed(own_rows)),
        in_specs=[vmem] * 5,
        out_specs=(vmem, vmem),
        compiler_params=params,
        name="own_sums",
    )(start, image, base, inflow, given)
    sums = lax.all_to_all(sums, ("rep", "sub", "blk"), 0, 0, tiled=True)
    second, third, entries = pl.pallas_call(
        functools.partial(last_kernel, float(cells)),
        out_shape=(rowed(own_rows), rowed(own_rows), jax.ShapeDtypeStruct((1, 5), jnp.float32)),
        in_specs=[vmem] * 4,
        out_specs=(vmem, vmem, vmem),
        compiler_params=params,
        name="arnoldi_entries",
    )(start, image, again, sums)
    return second.reshape(start_vector.shape), third.reshape(start_vector.shape), entries.reshape(5)


def solution(mesh):
    return jax.shard_map(
        per_device,
        mesh=mesh,
        in_specs=(
            P("rep", "sub", "blk"),
            P("rep", "sub", "blk", None, None),
            P("rep", "sub", None, None),
            P("rep", "sub", "blk"),
            P("rep", "sub", None),
            P("rep", "sub", None, "blk"),
        ),
        out_specs=(P("rep", "sub", "blk"), P("rep", "sub", "blk"), P()),
        check_vma=False,
    )
```
